32 devices in a mesh: head: 2 (over core), wide: 4 (over y, x), dp: 4 (over z).
Axes of the slice: x: 2, y: 2, z: 4, core: 2. Of those that a mesh axis runs over, the one named last changes fastest.
Arguments:
- layer_input: bfloat16 [8192, 1024], P(('wide', 'dp')), may hold values from -6 to 6
- mem_keys: bfloat16 [8192, 4, 112], P(('wide', 'dp'), 'head'), may hold values from -6 to 6
- mem_values: bfloat16 [8192, 4, 112], P(('wide', 'dp'), 'head'), may hold values from -6 to 6
- route_value: int32 [4, 8192, 2], P('head', ('wide', 'dp')), may hold values from 0 to 4, all different within a row; in each aligned block of 512 rows (0 to 511, 512 to 1023, ..., all dimensions but the last counted through in order) at most 256 rows name the same one
- route_output: int32 [4, 8192, 2], P('head', ('wide', 'dp')), may hold values from 0 to 4, all different within a row; in each aligned block of 512 rows (0 to 511, 512 to 1023, ..., all dimensions but the last counted through in order) at most 256 rows name the same one
- ln1_gain: float32 [1024], replicated, may hold values from 0.5 to 1.5
- ln1_bias: float32 [1024], replicated, may hold values from -3 to 3
- w_query: bfloat16 [1024, 4, 112], P(None, 'head'), may hold values from -0.1875 to 0.1875
- w_key: bfloat16 [1024, 4, 112], P(None, 'head'), may hold values from -0.1875 to 0.1875
- w_rel: bfloat16 [1024, 4, 112], P(None, 'head'), may hold values from -0.1875 to 0.1875
- content_bias: float32 [4, 112], P('head'), may hold values from -3 to 3
- position_bias: float32 [4, 112], P('head'), may hold values from -3 to 3
- w_value: bfloat16 [4, 5, 1024, 112], P('head'), may hold values from -0.1875 to 0.1875
- w_out: bfloat16 [4, 5, 112, 1024], P('head'), may hold values from -6 to 6
- router_value: bfloat16 [1024, 4, 5], P(None, 'head'), may hold values from -0.125 to 0.125
- router_output: bfloat16 [1024, 4, 5], P(None, 'head'), may hold values from -0.125 to 0.125
- ln2_gain: float32 [1024], replicated, may hold values from 0.5 to 1.5
- ln2_bias: float32 [1024], replicated, may hold values from -3 to 3
- w_up: bfloat16 [1024, 4096], P(None, 'head'), may hold values from -0.1875 to 0.1875
- w_down: bfloat16 [4096, 1024], P('head'), may hold values from -0.09375 to 0.09375
- cotangent: bfloat16 [8192, 1024], P(('wide', 'dp')), may hold values from -6 to 6
Outputs:
- output: bfloat16 [8192, 1024], P(('wide', 'dp'))
- grad_input: float32 [8192, 1024], P(('wide', 'dp'))
- grad_ln1_gain: float32 [1024], P(('wide', 'dp'))
- grad_ln1_bias: float32 [1024], P(('wide', 'dp'))
- grad_w_query: float32 [1024, 4, 112], P(('wide', 'dp'), 'head')
- grad_w_key: float32 [1024, 4, 112], P(('wide', 'dp'), 'head')
- grad_w_rel: float32 [1024, 4, 112], P(('wide', 'dp'), 'head')
- grad_content_bias: float32 [4, 112], P('head')
- grad_position_bias: float32 [4, 112], P('head')
- grad_w_value: float32 [4, 5, 1024, 112], P('head', None, ('wide', 'dp'))
- grad_w_out: float32 [4, 5, 112, 1024], P('head', None, None, ('wide', 'dp'))
- grad_router_value: float32 [1024, 4, 5], P(('wide', 'dp'), 'head')
- grad_router_output: float32 [1024, 4, 5], P(('wide', 'dp'), 'head')
- grad_ln2_gain: float32 [1024], P(('wide', 'dp'))
- grad_ln2_bias: float32 [1024], P(('wide', 'dp'))
- grad_w_up: float32 [1024, 4096], P(('wide', 'dp'), 'head')
- grad_w_down: float32 [4096, 1024], P('head', ('wide', 'dp'))
The draws below stay inside these ranges and needn't reach their ends.
Inputs may be any that keep to these rules, and one draw needn't show every extreme that they name: `route_value`: each row names two different experts. Among the 512 tokens of one head and one half sequence, no expert is named by more than 256 of them. `route_output`: each row names two different experts. Among the 512 tokens of one head and one half sequence, no expert is named by more than 256 of them.
All inputs are finite; a program needn't handle non-finite values.
Results may differ from the reference program's by a relative error of at most 0.018.
Values may be sent and summed in bfloat16 or wider, within the bound.
A program may use at most 192 MiB of HBM per device.

```python
import math
import jax
import jax.numpy as jnp
import numpy as np
from jax import lax

D = 1024
HEADS = 4
DH = 112
EXPERTS = 5
TOP = 2
FF = 4096
SEQ_LEN = 1024
MEM = 1024
HALF = 512
CAP = 256
TOKENS = 8192
SEQS = 8
MEMROWS = 8192


def strengthened(array, own_key, source, target, blocks, factor):
    owner, partner = [(jnp.arange(array.shape[dim]) // (array.shape[dim] // blocks)).reshape([-1 if axis == dim else 1 for axis in range(array.ndim)]) for dim in (source, target)]
    chosen = jax.random.permutation(own_key, blocks)[partner]
    strong = (owner == chosen) | (owner == (partner + blocks // 2) % blocks)
    return jnp.where(strong, factor * array, array)


def steps_of(key, dims, shards, smallest, high):
    level, own = 1.0, jax.random.fold_in(key, 6)
    for position, blocks in shards:
        draws = jnp.exp(jax.random.uniform(jax.random.fold_in(own, position), (blocks,), jnp.float32, smallest / len(shards), high / len(shards)))
        level = level * jnp.repeat(draws, dims[position] // blocks).reshape([-1 if axis == position else 1 for axis in range(len(dims))])
    return level


def assign_block(own_key, own, number, rows, count, top, bound, slope):
    sequence = jax.random.permutation(own_key, count)
    crowded, ordinary = portions_of(count, rows * top, bound, slope, True), portions_of(count, rows * top, bound, slope, False)
    places = jnp.arange(count)

    def named(sizes, offset_by):
        used = int((sizes > 0).sum())
        fixed = max(1, used // 4)
        moved = fixed + (places - fixed + offset_by * (used - fixed)) % max(1, count - fixed)
        return jnp.zeros((count,), jnp.int32).at[sequence[jnp.where(places < fixed, places, moved)]].set(jnp.asarray(sizes, jnp.int32))

    sizes = jnp.where(number % 4 == 0, named(crowded, number // 4), named(ordinary, number - number // 4 - 1))
    mixed = jax.random.permutation(jax.random.fold_in(own, 3), count)
    donor, receiver = mixed[0:count // 2 * 2:2], mixed[1:count // 2 * 2:2]
    slack = jnp.minimum(sizes[donor] - 1, bound - sizes[receiver]) // 2
    slack = jnp.where((donor == sequence[0]) | (receiver == sequence[0]) | (sizes[receiver] == 0), 0, jnp.maximum(slack, 0))
    moved = jax.random.randint(jax.random.fold_in(own, 4), (count // 2,), 0, 1 << 20) % (slack + 1)
    sizes = sizes.at[donor].add(-moved).at[receiver].add(moved)
    items = jnp.searchsorted(jnp.cumsum(sizes), jnp.arange(rows * top), side="right").astype(jnp.int32)
    table = items.reshape(top, rows).T
    table = table[jax.random.permutation(jax.random.fold_in(own, 1), rows)]
    offset_by = jax.random.randint(jax.random.fold_in(own, 2), (rows, 1), 0, top)
    return jnp.take_along_axis(table, (jnp.arange(top)[None, :] + offset_by) % top, axis=1)


def portions_of(amount, total, bound, slope, full):
    loads = [(1 << 20) // math.isqrt(grade ** slope) + 1 for grade in range(1, amount + 1)]
    largest = bound if full else min(bound, max(-(-total // amount), total * loads[0] // sum(loads)))
    least = 1 if total - largest >= amount - 1 else 0
    counts, rest = [largest] + [least] * (amount - 1), total - largest - least * (amount - 1)
    while rest > 0:
        movable = [i for i in range(1, amount) if counts[i] < largest] or [i for i in range(1, amount) if counts[i] < bound]
        pool, left = sum([loads[i] for i in movable]), rest
        for i in movable:
            addition = min(bound - counts[i], max(1, left * loads[i] // pool), rest)
            counts[i] = counts[i] + addition
            rest = rest - addition
    return np.array(counts)


def bell_draw(key, dims, width, limit, cuts=(), kind=jnp.bfloat16):
    factor_of = steps_of(key, dims, cuts, -0.22, 0.18) if cuts else 1.0
    drawn = jax.random.normal(key, dims, jnp.float32) * width * factor_of
    return jnp.minimum(jnp.maximum(drawn, -limit), limit).astype(kind)


def heavy_noise(stream_key, extent, width, reach, shards, heavy, kind=jnp.bfloat16):
    entries = width * jax.random.normal(stream_key, extent, jnp.float32)
    if shards:
        entries = entries * steps_of(stream_key, extent, shards, -0.22, 0.18)
    return jnp.clip(strengthened(entries, jax.random.fold_in(stream_key, 3), *heavy), -reach, reach).astype(kind)


def setup_inputs(seed: int = 0) -> dict:
    streams_of = jax.random.split(jax.random.key(seed), 22)
    layer_input = bell_draw(streams_of[0], (TOKENS, D), 1.0, 6.0, ((0, 16),))
    mem_keys = bell_draw(streams_of[1], (MEMROWS, HEADS, DH), 1.0, 6.0, ((0, 16), (1, 2)))
    mem_values = bell_draw(streams_of[2], (MEMROWS, HEADS, DH), 0.7, 6.0, ((0, 16), (1, 2)))
    route_value_keys = jax.random.split(jax.random.fold_in(streams_of[3], 1), HEADS * TOKENS // HALF)
    route_value_turns = jax.random.permutation(jax.random.fold_in(streams_of[3], 3), HEADS * TOKENS // HALF)
    route_value = jax.vmap(lambda own, number: assign_block(jax.random.fold_in(streams_of[3], 2), own, number, HALF, EXPERTS, TOP, CAP, 2))(route_value_keys, route_value_turns).reshape((HEADS, TOKENS, TOP))
    route_output_keys = jax.random.split(jax.random.fold_in(streams_of[4], 1), HEADS * TOKENS // HALF)
    route_output_turns = jax.random.permutation(jax.random.fold_in(streams_of[4], 3), HEADS * TOKENS // HALF)
    route_output = jax.vmap(lambda own, number: assign_block(jax.random.fold_in(streams_of[4], 2), own, number, HALF, EXPERTS, TOP, CAP, 2))(route_output_keys, route_output_turns).reshape((HEADS, TOKENS, TOP))
    ln1_gain = jnp.clip(1.0 + 0.1 * jax.random.normal(streams_of[5], (D,), jnp.float32), 0.5, 1.5)
    ln1_bias = bell_draw(streams_of[6], (D,), 0.2, 3.0, (), jnp.float32)
    w_query = bell_draw(streams_of[7], (D, HEADS, DH), D ** -0.5, 0.1875, ((1, 2),))
    w_key = bell_draw(streams_of[8], (D, HEADS, DH), D ** -0.5, 0.1875, ((1, 2),))
    w_rel = bell_draw(streams_of[9], (D, HEADS, DH), D ** -0.5, 0.1875, ((1, 2),))
    content_bias = bell_draw(streams_of[10], (HEADS, DH), 0.5, 3.0, ((0, 2),), jnp.float32)
    position_bias = bell_draw(streams_of[11], (HEADS, DH), 0.5, 3.0, ((0, 2),), jnp.float32)
    w_value = bell_draw(streams_of[12], (HEADS, EXPERTS, D, DH), D ** -0.5, 0.1875, ((0, 2),))
    w_out = bell_draw(streams_of[13], (HEADS, EXPERTS, DH, D), 1 ** -0.5, 6.0, ((0, 2),))
    router_value = bell_draw(streams_of[14], (D, HEADS, EXPERTS), (D * 16 // 9) ** -0.5, 0.125, ((1, 2),))
    router_output = bell_draw(streams_of[15], (D, HEADS, EXPERTS), (D * 16 // 9) ** -0.5, 0.125, ((1, 2),))
    ln2_gain = jnp.clip(1.0 + 0.1 * jax.random.normal(streams_of[16], (D,), jnp.float32), 0.5, 1.5)
    ln2_bias = bell_draw(streams_of[17], (D,), 0.2, 3.0, (), jnp.float32)
    w_up = bell_draw(streams_of[18], (D, FF), D ** -0.5, 0.1875, ((1, 2),))
    w_down = bell_draw(streams_of[19], (FF, D), FF ** -0.5, 0.09375, ((0, 2),))
    cotangent = heavy_noise(streams_of[20], (TOKENS, D), 1.0, 6.0, ((0, 16),), (0, 1, 16, 2.0))
    return dict(layer_input=layer_input, mem_keys=mem_keys, mem_values=mem_values, route_value=route_value, route_output=route_output, ln1_gain=ln1_gain, ln1_bias=ln1_bias, w_query=w_query, w_key=w_key, w_rel=w_rel, content_bias=content_bias, position_bias=position_bias, w_value=w_value, w_out=w_out, router_value=router_value, router_output=router_output, ln2_gain=ln2_gain, ln2_bias=ln2_bias, w_up=w_up, w_down=w_down, cotangent=cotangent)


@jax.custom_vjp
def low(v):
    return lax.optimization_barrier(v.astype(jnp.bfloat16)).astype(jnp.float32)

@jax.custom_vjp
def low_back(v):
    return v

def low_keep(v):
    return (low(v), None)

def low_pass(kept, grad):
    return (grad,)

def back_keep(v):
    return (v, None)

def back_low(kept, grad):
    return (low(grad),)
low.defvjp(low_keep, low_pass)
low_back.defvjp(back_keep, back_low)
PRECISE = lax.Precision.HIGHEST
EPSILON = 1e-05
NEG_LARGE = -1e+30

def normalize(values):
    row_mean = lax.optimization_barrier(jnp.mean(values, axis=-1, keepdims=True))
    centered = values - row_mean
    variance = lax.optimization_barrier(jnp.mean(centered * centered, axis=-1, keepdims=True))
    return centered * lax.rsqrt(variance + EPSILON)

def sinusoid(distance, model_width):
    half_width = model_width // 2
    frequencies = jnp.exp(jnp.arange(half_width, dtype=jnp.float32) * (-2.0 * math.log(10000.0) / model_width))
    angles = distance.astype(jnp.float32)[:, None] * frequencies[None, :]
    return jnp.concatenate([jnp.sin(angles), jnp.cos(angles)], axis=1)

def attend_block(query_block, keys, values, content_bias, position_bias, w_rel, query_start):
    row_count = query_block.shape[0]
    key_count = keys.shape[0]
    query_u = low(query_block + content_bias)
    query_v = low(query_block + position_bias)
    distance = query_start + row_count - 1 - jnp.arange(key_count + row_count - 1, dtype=jnp.int32)
    position_table = low(sinusoid(distance, D))
    rel_rows = low(low_back(jnp.einsum('cd,dhk->chk', position_table, w_rel, precision=PRECISE)))
    content = low_back(jnp.einsum('bhk,jhk->hbj', query_u, keys, precision=PRECISE))
    positional = low_back(jnp.einsum('bhk,chk->hbc', query_v, rel_rows, precision=PRECISE))
    column = row_count - 1 - jnp.arange(row_count, dtype=jnp.int32)[:, None] + jnp.arange(key_count, dtype=jnp.int32)[None, :]
    column = jnp.broadcast_to(column[None], (positional.shape[0], row_count, key_count))
    shifted = jnp.take_along_axis(positional, column, axis=2)
    query_pos = query_start + jnp.arange(row_count, dtype=jnp.int32)
    visible = jnp.arange(key_count, dtype=jnp.int32)[None, :] <= query_pos[:, None]
    scores = jnp.where(visible[None], (content + shifted) * (1.0 / math.sqrt(DH)), NEG_LARGE)
    row_peak = lax.optimization_barrier(jnp.max(scores, axis=2, keepdims=True))
    weights = jnp.exp(scores - row_peak)
    probabilities = low(weights / lax.optimization_barrier(jnp.sum(weights, axis=2, keepdims=True)))
    return jnp.einsum('hbj,jhk->bhk', probabilities, values, precision=PRECISE)

def sequence_layer(parameters, tokens, memory_keys, memory_values, value_routes, output_routes):
    ln1_gain, ln1_bias, w_query, w_key, w_rel, content_bias, position_bias, w_value, w_out, router_value, router_output, ln2_gain, ln2_bias, w_up, w_down = parameters
    hidden = low(normalize(tokens) * ln1_gain + ln1_bias)
    queries = low_back(jnp.einsum('td,dhk->thk', hidden, w_query, precision=PRECISE))
    key_own = low(low_back(jnp.einsum('td,dhk->thk', hidden, w_key, precision=PRECISE)))
    logit_value = low_back(jnp.einsum('td,dhe->the', hidden, router_value, precision=PRECISE))
    logit_out = low_back(jnp.einsum('td,dhe->the', hidden, router_output, precision=PRECISE))
    expert_range = jnp.arange(EXPERTS, dtype=jnp.int32)
    mask_value = lax.optimization_barrier(jnp.sum((jnp.transpose(value_routes, (1, 0, 2))[..., None] == expert_range).astype(jnp.float32), axis=2))
    mask_out = lax.optimization_barrier(jnp.sum((jnp.transpose(output_routes, (1, 0, 2))[..., None] == expert_range).astype(jnp.float32), axis=2))
    gate_value = jax.nn.sigmoid(logit_value) * mask_value
    gate_out = jax.nn.sigmoid(logit_out) * mask_out
    value_each = low_back(jnp.einsum('td,hedk->thek', hidden, w_value, precision=PRECISE))
    values_own = low(lax.optimization_barrier(jnp.sum(gate_value[..., None] * value_each, axis=2)))
    keys = jnp.concatenate([memory_keys, key_own], axis=0)
    values = jnp.concatenate([memory_values, values_own], axis=0)
    blocks = [attend_block(queries[index * HALF:(index + 1) * HALF], keys, values, content_bias, position_bias, w_rel, MEM + index * HALF) for index in range(2)]
    att_low = low(low_back(jnp.concatenate(blocks, axis=0)))
    out_each = low(low_back(jnp.einsum('thk,hekd->thed', att_low, w_out, precision=PRECISE)))
    mixed = tokens + lax.optimization_barrier(jnp.sum(gate_out[..., None] * out_each, axis=(1, 2)))
    hidden_two = low(normalize(mixed) * ln2_gain + ln2_bias)
    pre_act = low_back(jnp.dot(hidden_two, w_up, precision=PRECISE))
    act_low = low(jax.nn.gelu(pre_act))
    return mixed + jnp.dot(act_low, w_down, precision=PRECISE)

def reference(layer_input, mem_keys, mem_values, route_value, route_output, ln1_gain, ln1_bias, w_query, w_key, w_rel, content_bias, position_bias, w_value, w_out, router_value, router_output, ln2_gain, ln2_bias, w_up, w_down, cotangent):
    parameters = tuple((weight.astype(jnp.float32) for weight in (ln1_gain, ln1_bias, w_query, w_key, w_rel, content_bias, position_bias, w_value, w_out, router_value, router_output, ln2_gain, ln2_bias, w_up, w_down)))
    memory_keys = mem_keys.astype(jnp.float32).reshape(SEQS, MEM, HEADS, DH)
    memory_values = mem_values.astype(jnp.float32).reshape(SEQS, MEM, HEADS, DH)
    value_routes = jnp.transpose(route_value.reshape(HEADS, SEQS, SEQ_LEN, TOP), (1, 0, 2, 3))
    output_routes = jnp.transpose(route_output.reshape(HEADS, SEQS, SEQ_LEN, TOP), (1, 0, 2, 3))

    def forward(tokens, weights):

        def one_sequence(pieces):
            return sequence_layer(weights, *pieces)
        stacked = lax.map(jax.checkpoint(one_sequence), (tokens.reshape(SEQS, SEQ_LEN, D), memory_keys, memory_values, value_routes, output_routes))
        return stacked.reshape(TOKENS, D)
    result, pullback = jax.vjp(forward, layer_input.astype(jnp.float32), parameters)
    grad_input, gradients = pullback(cotangent.astype(jnp.float32))
    return (result.astype(jnp.bfloat16), grad_input, gradients[0], gradients[1], gradients[2], gradients[3], gradients[4], gradients[5], gradients[6], gradients[7], gradients[8], gradients[9], gradients[10], gradients[11], gradients[12], gradients[13], gradients[14])
```

```python
import functools
import math
import types

import jax
import jax.numpy as jnp
import numpy as np
from jax import lax
from jax.experimental import pallas as pl
from jax.experimental.pallas import tpu as pltpu
from jax.sharding import PartitionSpec as P

EPSILON = 1e-05
NEG_LARGE = -1e30
F32 = jnp.float32
BF16 = jnp.bfloat16
WIDE, DEEP = "wide", "dp"

NN = (((1,), (0,)), ((), ()))
NT = (((1,), (1,)), ((), ()))
TN = (((0,), (0,)), ((), ()))


def mm(a, b, dims=NN):
    return lax.dot_general(a, b, dims, preferred_element_type=F32)


def swapped(block, axis, bit):
    count = lax.axis_size(axis)
    return lax.ppermute(block, axis, [(i, i ^ bit) for i in range(count)])


def normalize(values):
    row_mean = jnp.mean(values, axis=-1, keepdims=True)
    centered = values - row_mean
    variance = jnp.mean(centered * centered, axis=-1, keepdims=True)
    inverse = lax.rsqrt(variance + EPSILON)
    return (centered * inverse, inverse)


def norm_back(grad_normed, normed, inverse):
    first_mean = jnp.mean(grad_normed, axis=-1, keepdims=True)
    second_mean = jnp.mean(grad_normed * normed, axis=-1, keepdims=True)
    return inverse * (grad_normed - first_mean - normed * second_mean)


def position_table(extent, model_width):
    half_width = model_width // 2
    frequencies = np.exp(
        np.arange(half_width, dtype=np.float32) * np.float32(-2.0 * math.log(10000.0) / model_width)
    ).astype(np.float32)
    distance = np.arange(extent - 1, -1, -1).astype(np.float32)
    angles = (frequencies[:, None] * distance[None, :]).astype(np.float64)
    return np.concatenate([np.sin(angles), np.cos(angles)], axis=0).astype(np.float32).astype(BF16)


def whole(array):
    return pl.BlockSpec(array.shape, lambda *_: (0,) * len(array.shape))


def pre_kernel(x_ref, gain_ref, bias_ref, wq_ref, wk_ref, wv_ref, rt_ref, cb_ref, pb_ref, rv_ref, ro_ref,
               hid_ref, qu_ref, qv_ref, k_ref, v_ref, each_ref, sig_ref, gate_ref, *, heads, experts, dh):
    normed, _ = normalize(x_ref[...].astype(F32))
    hid = (normed * gain_ref[...] + bias_ref[...]).astype(BF16)
    hid_ref[...] = hid
    logits = mm(rt_ref[...], hid, NT)
    sig = 1.0 / (1.0 + jnp.exp(-logits))
    masks = []
    for routes in (rv_ref, ro_ref):
        for h in range(heads):
            for e in range(experts):
                hit = (routes[h, 0:1, :] == e) | (routes[h, 1:2, :] == e)
                masks.append(jnp.where(hit, 1.0, 0.0))
    gate = sig * jnp.concatenate(masks, axis=0)
    sig_ref[...] = sig
    gate_ref[...] = gate
    k_ref[...] = mm(wk_ref[...], hid, NT).astype(BF16)
    for h in range(heads):
        total = None
        for e in range(experts):
            rows = pl.ds((h * experts + e) * dh, dh)
            each = mm(wv_ref[rows, :], hid, NT)
            each_ref[rows, :] = each.astype(BF16)
            term = gate[h * experts + e:h * experts + e + 1, :] * each
            total = term if total is None else total + term
        v_ref[pl.ds(h * dh, dh), :] = total.astype(BF16)
    queries = mm(wq_ref[...], hid, NT)
    qu_ref[...] = (queries + cb_ref[...]).astype(BF16)
    qv_ref[...] = (queries + pb_ref[...]).astype(BF16)


def attend_kernel(odd_ref, qu_ref, qv_ref, rel_ref, ko_ref, kp_ref, km_ref, kn_ref, vo_ref, vp_ref, vm_ref, vn_ref,
                  probs_ref, att_ref, *, scale, rows, block):
    odd = odd_ref[0] == 1
    k_one = jnp.where(odd, kp_ref[0], kn_ref[0])
    v_one = jnp.where(odd, vp_ref[0], vn_ref[0])
    keys = (kn_ref[0], km_ref[0], k_one, ko_ref[0])
    values = (vn_ref[0], vm_ref[0], v_one, vo_ref[0])
    total_keys = 4 * rows
    first = jnp.where(odd, 0, rows)
    for base in range(0, rows, block):
        here = slice(base, base + block)
        positional = mm(qv_ref[0, :, here], rel_ref[0], TN)
        positional = pltpu.roll(positional, total_keys - rows + 1 + base, 1, stride=1, stride_axis=0)
        content = jnp.concatenate([mm(qu_ref[0, :, here], k, TN) for k in keys], axis=1)
        row = lax.broadcasted_iota(jnp.int32, (block, total_keys), 0) + base
        col = lax.broadcasted_iota(jnp.int32, (block, total_keys), 1)
        visible = (col <= row + (total_keys - rows)) & (col >= first)
        scores = jnp.where(visible, (content + positional) * scale, NEG_LARGE)
        peak = jnp.max(scores, axis=1, keepdims=True)
        exponents = jnp.exp(scores - peak)
        total = jnp.sum(exponents, axis=1, keepdims=True)
        probs = (exponents * (1.0 / total)).astype(BF16)
        probs_ref[0, here, :] = probs
        att = None
        for i, v in enumerate(values):
            part = mm(v, probs[:, i * rows:(i + 1) * rows], NT)
            att = part if att is None else att + part
        att_ref[0, :, here] = att.astype(BF16)


def gelu_both(x):
    c = math.sqrt(2.0 / math.pi)
    square = x * x
    t = jnp.tanh(c * x * (1.0 + 0.044715 * square))
    half = 0.5 * (1.0 + t)
    return x * half, half + 0.5 * x * (1.0 - t * t) * (c * (1.0 + 3.0 * 0.044715 * square))


def meet(*devices):
    barrier = pltpu.get_barrier_semaphore()
    for device in devices:
        pl.semaphore_signal(barrier, inc=1, device_id=device, device_id_type=pl.DeviceIdType.MESH)
    pl.semaphore_wait(barrier, len(devices))


def other_core():
    return (1 - lax.axis_index("head"), lax.axis_index("wide"), lax.axis_index("dp"))


class Swap:
    def __init__(self, src, dst, sems, slot, device):
        self.parts = (src, dst, sems, slot, device)
        self.copy().start()

    def copy(self):
        src, dst, sems, slot, device = self.parts
        return pltpu.make_async_remote_copy(
            src_ref=src, dst_ref=dst, send_sem=sems[0].at[slot], recv_sem=sems[1].at[slot],
            device_id=device() if callable(device) else device, device_id_type=pl.DeviceIdType.MESH,
        )

    def wait(self):
        self.copy().wait()


remote = Swap


def feed_kernel(att_ref, gate_ref, x_ref, cot_ref, cot_in_ref, wo_ref, gain_ref, bias_ref, up_ref, down_ref,
                mixed_ref, gated_ref, act_ref, pre_ref, two_t_ref, cot_t_ref, first_ref, second_ref, two_out_ref, ffn_ref,
                part_ref, got_ref, two_ref, send_sem, recv_sem, *, heads, experts, dh, wide_bits, share, block):
    there = other_core()
    rows = x_ref.shape[0]
    for h in range(heads):
        for e in range(experts):
            at = h * experts + e
            gated_ref[at * dh:(at + 1) * dh, :] = (gate_ref[at:at + 1, :] * att_ref[h].astype(F32)).astype(BF16)
    part_ref[...] = mm(gated_ref[...], wo_ref[...], TN).astype(BF16)
    meet(there)
    swap = remote(part_ref, got_ref, (send_sem, recv_sem), 0, there)
    cot_t_ref[:, 0:rows] = cot_ref[...].T
    cot_t_ref[:, rows:] = cot_in_ref[...].T
    swap.wait()
    mixed = x_ref[...].astype(F32) + (part_ref[...].astype(F32) + got_ref[...].astype(F32))
    mixed_ref[...] = mixed
    normed, _ = normalize(mixed)
    two = (normed * gain_ref[...] + bias_ref[...]).astype(BF16)
    two_ref[...] = two
    two_t_ref[...] = two.T
    chunk = act_ref.shape[2] // 2
    for part in range(4):
        here = slice(part * chunk, (part + 1) * chunk)
        value, slope = gelu_both(mm(two_ref[...], up_ref[:, here]))
        inner = slice(part % 2 * chunk, part % 2 * chunk + chunk)
        act_ref[part // 2, :, inner] = value.astype(BF16)
        pre_ref[part // 2, :, inner] = (mm(cot_ref[...], down_ref[here, :], NT) * slope).astype(BF16)
    total = None
    for k in range(2):
        half = slice(k * 2 * chunk, (k + 1) * 2 * chunk)
        term = mm(pre_ref[k], up_ref[:, half], NT)
        total = term if total is None else total + term
    two_out_ref[...] = total.astype(BF16)
    wide = lax.axis_index(WIDE)
    for k, (axis, out) in enumerate((("y", first_ref), ("x", second_ref))):
        bit = bit_order(axis, wide_bits, [])[0]
        other = 1 - (wide // (1 << bit[1])) % 2
        for number, run in enumerate(picks(natural(wide_bits), {bit: other})):
            piece = mm(two_t_ref[pl.ds(pl.multiple_of(run * share, share), share), :], pre_ref[k]).astype(BF16)
            for j in range(share // block):
                out[number * (share // block) + j] = piece[j * block:(j + 1) * block]
    total = None
    for k in range(2):
        term = mm(act_ref[k], down_ref[k * 2 * chunk:(k + 1) * 2 * chunk, :])
        total = term if total is None else total + term
    ffn_ref[...] = total.astype(BF16)


def bit_names(wide_count, depth):
    wide_bits = [(WIDE, b) for b in range(int(math.log2(wide_count)))]
    deep_bits = [(DEEP, b) for b in range(int(math.log2(depth)))]
    return wide_bits, deep_bits


def bit_order(axes, wide_bits, deep_bits):
    half = len(wide_bits) // 2
    groups = dict(x=wide_bits[:half], y=wide_bits[half:], n=deep_bits[:1], f=deep_bits[1:])
    return [bit for axis in axes for bit in groups[axis]]


def natural(bits):
    return [b for b in sorted(bits, key=lambda b: (b[0] == WIDE, b[1]), reverse=True)]


def picks(left, fixed):
    free = [b for b in left if b not in fixed]
    found = []
    for number in range(1 << len(free)):
        index = 0
        for place, b in enumerate(left):
            if b in fixed:
                digit = fixed[b]
            else:
                digit = (number >> (len(free) - 1 - free.index(b))) & 1
            index = index + digit * (1 << (len(left) - 1 - place))
        found.append(index)
    return found


class Tree:
    def __init__(self, order, left, acc, send, got, slots, me):
        self.order, self.left, self.acc, self.send, self.got, self.slots, self.me = order, left, acc, send, got, slots, me
        self.level = 0
        self.copies = {}

    def fixed(self, own):
        bit = self.order[self.level]
        return {bit: self.me[bit] if own else 1 - self.me[bit]}

    def launch(self, sems, partner, src=None):
        got = self.got[self.level]
        src = self.send.at[pl.ds(0, got.shape[0])] if src is None else src
        bit = self.order[self.level]
        self.copies[self.level] = remote(src, got, sems, self.slots[self.level], lambda: partner(bit))

    def step(self):
        self.left = [b for b in self.left if b != self.order[self.level]]
        self.level += 1

    def arrive(self):
        self.copies[self.level - 1].wait()
        return self.got[self.level - 1]

    def advance(self, sems, partner):
        got = self.arrive() if self.level else None

        def piece(index):
            mine = self.acc[index].astype(F32)
            return mine if got is None else mine + got[index].astype(F32)

        for place, index in enumerate(picks(self.left, self.fixed(False))):
            self.send[place] = piece(index).astype(BF16)
        self.launch(sems, partner)
        for place, index in enumerate(picks(self.left, self.fixed(True))):
            self.acc[place] = piece(index).astype(self.acc.dtype)
        self.step()

    def finish(self, index=0):
        return self.acc[index].astype(F32) + self.got[self.level - 1][index].astype(F32)


def late_kernel(*refs, names, loaded, sizes, plan):
    r = types.SimpleNamespace(**dict(zip(names, refs)))
    given = types.SimpleNamespace(**dict(zip(loaded, refs)))
    heads, experts, dh, rows, width = sizes.heads, sizes.experts, sizes.dh, sizes.rows, sizes.width
    wide_count, depth, block = sizes.wide, sizes.deep, sizes.block
    hd, he, hed = heads * dh, heads * experts, heads * experts * dh
    blocks = wide_count * depth
    wide_bits, deep_bits = bit_names(wide_count, depth)
    bits = wide_bits + deep_bits
    place = {WIDE: lax.axis_index(WIDE), DEEP: lax.axis_index(DEEP)}
    head = lax.axis_index("head")
    me = {b: (place[b[0]] // (1 << b[1])) % 2 for b in bits}
    x_bit, near = wide_bits[0], deep_bits[0]

    def partner(bit):
        axis, number = bit
        other = place[axis] + (1 - 2 * me[bit]) * (1 << number)
        return (head, other, place[DEEP]) if axis == WIDE else (head, place[WIDE], other)

    across = other_core()
    sems = (r.send_sem, r.recv_sem)
    loads = {}

    def fetch(target, name, slot):
        loads[name] = pltpu.make_async_copy(getattr(given, name), target, r.load_sem.at[slot])
        loads[name].start()

    order = {name: number for number, name in enumerate(loaded)}

    def fetch_all(**targets):
        for name, target in targets.items():
            fetch(target, name, order[name])

    def ready(*wanted):
        for name in wanted:
            if loads.get(name) is not None:
                loads[name].wait()
                loads[name] = None

    def tree_of(axes, left, acc, send, got, slots):
        return Tree(bit_order(axes, wide_bits, deep_bits), natural(left), acc, send, got, slots, me)

    up_a = tree_of("yxnf", bits, None, None, r.got_up_a, plan.up_a)
    up_b = tree_of("xynf", bits, None, None, r.got_up_b, plan.up_b)
    out = tree_of("nxyf", bits, r.acc_out, r.send_out, r.got_out, plan.out)
    share = width // wide_count
    per_share = share // block

    def runs(fixed):
        return picks(natural(wide_bits), {b: v for b, v in fixed.items() if b[0] == WIDE})

    def rows_of(run):
        return pl.ds(pl.multiple_of(run * share, share), share)

    meet(across, *[partner(b) for b in bits])
    two_swap = remote(given.two_out, r.two_in, sems, plan.two, across)
    act_swap = remote(given.act.at[1 - me[x_bit]], r.act_in, sems, plan.act, partner(x_bit))
    up_a.launch(sems, partner, given.up_a)
    gates_swap = remote(given.gates, r.gates_in, sems, plan.gates, partner(near))
    hid_swap = remote(given.hid.at[:, 1 - me[near]], r.hid_in, sems, plan.hid, partner(near))
    fetch_all(two_out=r.two_own, hid=r.hid, two_t=r.two_t, pre=r.pre, cot_t=r.cot_t)
    loads["act"] = pltpu.make_async_copy(given.act.at[me[x_bit]], r.act, r.load_sem.at[len(loaded) + 2])
    loads["act"].start()

    def attention(probs, qu, qv, rel, key_own, part_k, mem_k, part_mem_k, value_own, part_v, mem_v, part_mem_v, flip,
                  acc):
        fetch_all(
            probs=probs, qu=qu, qv=qv, rel=rel, key_own=key_own, part_k=part_k, mem_k=mem_k, part_mem_k=part_mem_k,
            value_own=value_own, part_v=part_v, mem_v=mem_v, part_mem_v=part_mem_v, flip=flip,
        )

        def out_back(mixed_ref, cot, gain, att_ref, gate_ref, sig_ref, wo, gated, low_ref, ffn_own):
            fetch_all(
                mixed=mixed_ref, cot=cot, gain_two=gain, att=att_ref, gate_o=gate_ref, sig_o=sig_ref, wo=wo,
                gated=gated, ffn_out=ffn_own,
            )
            ready("mixed")
            normed, inverse = normalize(mixed_ref[...])
            two_swap.wait()
            ffn_swap = remote(given.ffn_out, r.ffn_in, sems, plan.ffn, across)
            ready("two_out", "cot", "gain_two")
            grad_two = r.two_own[...].astype(F32) + r.two_in[...].astype(F32)
            r.small[2:3, :] = jnp.sum(grad_two * normed, axis=0, keepdims=True)
            r.small[3:4, :] = jnp.sum(grad_two, axis=0, keepdims=True)
            grad_mixed = cot[...].astype(F32) + norm_back(grad_two * gain[...], normed, inverse)
            r.grad_mixed[...] = grad_mixed
            low_ref[...] = grad_mixed.astype(BF16)
            ready("att", "gate_o", "sig_o", "wo")
            for h in range(heads):
                att = att_ref[h].astype(F32)
                total = None
                for e in range(experts):
                    at = h * experts + e
                    back = mm(wo[at * dh:(at + 1) * dh, :], low_ref[...], NT)
                    gate = gate_ref[at:at + 1, :]
                    grad_gate = jnp.sum(att * back, axis=0, keepdims=True)
                    r.logits[he + at:he + at + 1, :] = grad_gate * gate * (1.0 - sig_ref[at:at + 1, :])
                    total = gate * back if total is None else total + gate * back
                r.ga[h] = total.astype(BF16)
            low_t = low_ref[...].T
            ready("gated")
            for run in range(wide_count):
                part = mm(low_t[run * share:(run + 1) * share], gated[...], NT)
                for k in range(0, per_share, 2):
                    pair = [part[i * block:(i + 1) * block] for i in (k, k + 1)]
                    at = (run * per_share + k) // 2
                    out.send[at] = jnp.where(me[near] == 1, pair[0], pair[1]).astype(BF16)
                    out.acc[at] = jnp.where(me[near] == 1, pair[1], pair[0]).astype(BF16)
            out.launch(sems, partner)
            out.step()
            ffn_swap.wait()
            ready("ffn_out")
            ffn_own[...] = (mixed_ref[...] + (ffn_own[...].astype(F32) + r.ffn_in[...].astype(F32))).astype(BF16)
            written = pltpu.make_async_copy(ffn_own, r.output, r.load_sem.at[len(loaded)])
            written.start()
            written.wait()

        pl.run_scoped(
            out_back, pltpu.VMEM((rows, width), F32), pltpu.VMEM((rows, width), BF16), pltpu.VMEM((1, width), F32),
            pltpu.VMEM((heads, dh, rows), BF16), pltpu.VMEM((he, rows), F32), pltpu.VMEM((he, rows), F32),
            pltpu.VMEM((hed, width), BF16), pltpu.VMEM((hed, rows), BF16), pltpu.VMEM((rows, width), BF16),
            pltpu.VMEM((rows, width), BF16),
        )
        up_b.launch(sems, partner, given.up_b)
        ready("probs", "qu", "qv", "rel", "key_own", "part_k", "mem_k", "part_mem_k")
        ready("value_own", "part_v", "mem_v", "part_mem_v", "flip")
        odd = place[DEEP] % 2 == 1
        size = sizes.query_rows
        for h in range(heads):
            k_one = jnp.where(odd, part_k[h], part_mem_k[h])
            v_one = jnp.where(odd, part_v[h], part_mem_v[h])
            keys = (part_mem_k[h], mem_k[h], k_one, key_own[h])
            values = (part_mem_v[h], mem_v[h], v_one, value_own[h])
            bias_u = bias_v = None
            for base in range(0, rows, size):
                here = slice(base, base + size)
                turned = mm(flip[...], probs[h, here, :])
                ga = mm(r.ga[h, :, here], flip[...]).astype(BF16)
                queries_u = mm(qu[h, :, here], flip[...]).astype(BF16)
                queries_v = mm(qv[h, :, here], flip[...]).astype(BF16)
                gp = jnp.concatenate([mm(ga, v, TN) for v in values], axis=1)
                weighted = turned * gp
                delta = jnp.sum(weighted, axis=1, keepdims=True)
                gs = ((weighted - turned * delta) * sizes.scale).astype(BF16)
                gk = mm(queries_u, gs[:, 2 * rows:])
                gv = mm(ga, turned[:, 2 * rows:].astype(BF16))
                gqu = None
                for i, k in enumerate(keys):
                    part = mm(k, gs[:, i * rows:(i + 1) * rows], NT)
                    gqu = part if gqu is None else gqu + part
                gpos = pltpu.roll(gs, rows - size - base, 1, stride=1, stride_axis=0)
                gqv = mm(rel[h], gpos, NT)
                grel = mm(queries_v, gpos)
                r.gq[h * dh:(h + 1) * dh, here] = mm((gqu + gqv).astype(BF16), flip[...]).astype(BF16)
                ones = jnp.ones((8, size), F32)
                sum_u, sum_v = [
                    lax.dot_general(ones, g, NT, precision=lax.Precision.HIGHEST, preferred_element_type=F32)
                    for g in (gqu, gqv)
                ]
                if base == 0:
                    r.gk[h] = gk
                    r.gv[h] = gv
                    acc[...] = grel
                    bias_u, bias_v = sum_u, sum_v
                else:
                    r.gk[h] += gk
                    r.gv[h] += gv
                    acc[...] += grel
                    bias_u, bias_v = bias_u + sum_u, bias_v + sum_v
            r.grel[h * dh:(h + 1) * dh, :] = acc[...].astype(BF16)
            r.small[4 + h:5 + h, 0:dh] = bias_u[0:1]
            r.small[4 + heads + h:5 + heads + h, 0:dh] = bias_v[0:1]
        r.cross_out[0] = r.gk[:, :, :rows].astype(BF16)
        r.cross_out[1] = r.gv[:, :, :rows].astype(BF16)
        crossing.append(remote(r.cross_out, r.cross_in, sems, plan.cross, lambda: partner(near)))

    crossing = []
    hd_up = sizes.hd_up
    r.small[4:8, :] = jnp.zeros((4, width), F32)
    total_keys = 4 * rows
    chunk_shape = pltpu.VMEM((heads, dh, rows), BF16)
    pl.run_scoped(
        attention, pltpu.VMEM((heads, rows, total_keys), BF16), chunk_shape, chunk_shape,
        pltpu.VMEM((heads, dh, total_keys), BF16), *([chunk_shape] * 8),
        pltpu.VMEM((sizes.query_rows, sizes.query_rows), BF16), pltpu.VMEM((dh, total_keys), F32),
    )

    def rest(*held):
        b = types.SimpleNamespace(**dict(zip(sizes.late_names, held)))
        fetch_all(
            table=b.table, each=b.each, sigs=b.sigs, gates=b.gates, wv=b.wv, wq=b.wq, wk=b.wk, rt=b.rt, x=b.x, gain=b.gain
        )
        up_a.acc, up_a.send, up_b.acc, up_b.send = b.acc_up_a, b.send_up_a, b.acc_up_b, b.send_up_b
        query = tree_of("xynf", bits, b.acc_query, b.send_query, r.got_query, plan.query)
        if hd_up > hd:
            for at in range(blocks // 2):
                query.send[at, :, hd:hd_up] = jnp.zeros((block, hd_up - hd), BF16)
                query.acc[at, :, hd:hd_up] = jnp.zeros((block, hd_up - hd), F32)
        down = tree_of("ynf", bits, b.acc_down, b.send_down, r.got_down, plan.down)
        down.order = down.order[:len(wide_bits) // 2] + wide_bits[1:len(wide_bits) // 2] + down.order[len(wide_bits) // 2:]
        value = tree_of("yxf", [v for v in bits if v != near], b.acc_value, b.send_value, r.got_value, plan.value)

        def down_part(own):
            for number, run in enumerate(runs(down.fixed(own))):
                at_rows = rows_of(run)
                part = mm(r.cot_t[at_rows, 0:rows], r.act[...]) + mm(r.cot_t[at_rows, rows:], r.act_in[...])
                for k in range(per_share):
                    at = number * per_share + k
                    piece = part[k * block:(k + 1) * block]
                    if own:
                        down.acc[at] = piece
                    else:
                        down.send[at] = piece.astype(BF16)
            if own:
                down.step()
            else:
                down.launch(sems, partner)

        def up_part(tree, half, own):
            if not own:
                tree.step()
                tree.arrive()
            got = tree.got[0]
            fixed = {tree.order[0]: me[tree.order[0]], **tree.fixed(own)}
            sources = picks(tree.left, tree.fixed(own))
            for number, run in enumerate(runs(fixed)):
                part = mm(r.two_t[rows_of(run), :], r.pre[half])
                for k in range(per_share):
                    at = number * per_share + k
                    piece = part[k * block:(k + 1) * block] + got[sources[at]].astype(F32)
                    if own:
                        tree.acc[at] = piece
                    else:
                        tree.send[at] = piece.astype(BF16)
            if own:
                tree.step()
            else:
                tree.launch(sems, partner)

        ready("act", "cot_t")
        act_swap.wait()
        down_part(False)
        ready("two_t", "pre")
        up_part(up_a, 0, False)

        ready("hid", "table")
        for own in (False, True):
            for number, run in enumerate(runs(query.fixed(own))):
                left = r.hid[pl.ds(pl.multiple_of(run * (per_share // 2), per_share // 2), per_share // 2)]
                part = mm(left.reshape(share, rows), r.gq[...], NT)
                part_rel = mm(b.table[rows_of(run), :], r.grel[...], NT)
                for k in range(per_share):
                    at = number * per_share + k
                    piece, piece_rel = part[k * block:(k + 1) * block], part_rel[k * block:(k + 1) * block]
                    if own:
                        query.acc[at, :, 0:hd] = piece
                        query.acc[at, :, hd_up:] = piece_rel
                    else:
                        query.send[at, :, 0:hd] = piece.astype(BF16)
                        query.send[at, :, hd_up:] = piece_rel.astype(BF16)
            if not own:
                query.launch(sems, partner)
        query.step()

        ready("each", "sigs", "gates")
        crossing[0].wait()
        even = jnp.where(place[DEEP] % 2 == 0, 1.0, 0.0)
        for h in range(heads):
            gk = r.gk[h, :, rows:] + even * r.cross_in[0, h].astype(F32)
            gv = r.gv[h, :, rows:] + even * r.cross_in[1, h].astype(F32)
            b.own_out[h * dh:(h + 1) * dh, :] = gv.astype(BF16)
            b.own_out[hd + h * dh:hd + (h + 1) * dh, :] = gk.astype(BF16)
            for e in range(experts):
                at = h * experts + e
                gate = b.gates[at:at + 1, :]
                grad_gate = jnp.sum(gv * b.each[at * dh:(at + 1) * dh, :].astype(F32), axis=0, keepdims=True)
                r.logits[at:at + 1, :] = grad_gate * gate * (1.0 - b.sigs[at:at + 1, :])
                b.grads[at * dh:(at + 1) * dh, :] = (gate * gv).astype(BF16)
        tail = b.own_out.shape[0] - 2 * hd
        logits = jnp.concatenate([r.logits[0:2 * he, :], jnp.zeros((tail - 2 * he, rows), F32)], axis=0)
        b.own_out[2 * hd:, :] = logits.astype(BF16)
        own_swap = remote(b.own_out, r.own_in, sems, plan.own, partner(near))
        b.grads[hed:, :] = b.own_out[hd:, :]

        ready("wv", "wq", "wk", "rt")
        grad_hidden = mm(b.grads[0:hed, :], b.wv[...], TN)
        grad_hidden += mm(r.gq[...], b.wq[...], TN)
        grad_hidden += mm(b.grads[hed:hed + hd, :], b.wk[...], TN)
        grad_hidden += mm(b.grads[hed + hd:hed + hd + 2 * he, :], b.rt[...], TN)
        r.two_own[...] = grad_hidden.astype(BF16)
        heads_sum = remote(r.two_own, r.head_in, sems, plan.head, across)

        up_part(up_b, 1, False)

        hid_swap.wait()
        gates_swap.wait()
        near_rows = blocks // 2 * block
        mine = mm(r.hid[:, me[near]].reshape(near_rows, rows), b.grads[...], NT)
        for at in range(blocks // 2):
            value.acc[at] = mine[at * block:(at + 1) * block]
        own_swap.wait()
        for at in range(he):
            h = at // experts
            b.grads[at * dh:(at + 1) * dh, :] = (
                r.gates_in[at:at + 1, :] * r.own_in[h * dh:(h + 1) * dh, :].astype(F32)
            ).astype(BF16)
        b.grads[hed:, :] = r.own_in[hd:, :]
        theirs = mm(r.hid_in[...].reshape(near_rows, rows), b.grads[...], NT)
        for at in range(blocks // 2):
            value.acc[at] += theirs[at * block:(at + 1) * block]
        value.advance(sems, partner)

        out.advance(sems, partner)
        down_part(True)
        up_part(up_a, 0, True)

        ready("x", "gain")
        heads_sum.wait()
        grad_hidden = r.two_own[...].astype(F32) + r.head_in[...].astype(F32)
        normed, inverse = normalize(b.x[...].astype(F32))
        small = r.small
        small[0:1, :] = jnp.sum(grad_hidden * normed, axis=0, keepdims=True)
        small[1:2, :] = jnp.sum(grad_hidden, axis=0, keepdims=True)
        state = [remote(small, r.small_in.at[0], sems, plan.small[0], partner(bits[0]))]
        r.grad_mixed[...] += norm_back(grad_hidden * b.gain[...], normed, inverse)
        input_copy = pltpu.make_async_copy(r.grad_mixed, r.grad_input, r.load_sem.at[len(loaded) + 1])
        input_copy.start()

        def small_step():
            at = len(state) - 1
            if at == len(bits):
                return
            state[at].wait()
            small[...] = small[...] + r.small_in[at]
            state.append(
                None if at + 1 == len(bits)
                else remote(small, r.small_in.at[at + 1], sems, plan.small[at + 1], partner(bits[at + 1]))
            )

        up_part(up_b, 1, True)
        queue = [query, down, up_a, up_b, out, value]
        while any(tree.level < len(tree.order) for tree in queue):
            for tree in queue:
                if tree.level < len(tree.order):
                    tree.advance(sems, partner)
                    small_step()
        while len(state) <= len(bits):
            small_step()
        r.small_out[...] = small[...]

        down.arrive()
        keep, leave = me[x_bit], 1 - me[x_bit]
        r.half_out[...] = down.finish(leave).astype(BF16)
        half_swap = remote(r.half_out, r.half_in, sems, plan.half, partner(x_bit))
        half = sizes.hidden_units // 2
        r.g_down[:, pl.ds(pl.multiple_of(keep * half, half), half)] = down.finish(keep)
        for number, tree in enumerate((up_a, up_b)):
            tree.arrive()
            r.g_up[:, number * half:(number + 1) * half] = tree.finish()
        query.arrive()
        total = query.finish()
        for h in range(heads):
            r.g_query[:, h, :] = total[:, h * dh:(h + 1) * dh]
            r.g_rel[:, h, :] = total[:, hd_up + h * dh:hd_up + (h + 1) * dh]
        out.arrive()
        total = out.finish()
        for at in range(he):
            r.g_out[at] = total[:, at * dh:(at + 1) * dh]
        value.arrive()
        total = value.finish()
        for at in range(he):
            r.g_value[at] = total[:, at * dh:(at + 1) * dh]
        for h in range(heads):
            r.g_key[:, h, :] = total[:, hed + h * dh:hed + (h + 1) * dh]
        r.g_router[...] = total[:, hed + hd:hed + hd + 2 * he]
        half_swap.wait()
        r.g_down[:, pl.ds(pl.multiple_of(leave * half, half), half)] = r.half_in[...].astype(F32)
        input_copy.wait()

    pl.run_scoped(rest, *sizes.late_scratch)


def late_call(inputs, sizes):
    wide_bits, deep_bits = bit_names(sizes.wide, sizes.deep)
    bits = len(wide_bits) + len(deep_bits)
    blocks = sizes.wide * sizes.deep
    block, rows, width, heads, dh = sizes.block, sizes.rows, sizes.width, sizes.heads, sizes.dh
    he, hd = heads * sizes.experts, heads * dh
    hed, half = he * dh, sizes.hidden_units // 2
    tail = 32
    sizes.hd_up = -(-hd // 128) * 128
    sizes.value_n = hed + hd + tail
    query_n = sizes.hd_up + hd
    count = 10 + 7 * bits
    slots = iter(range(count))

    def levels():
        return [next(slots) for _ in range(bits)]

    plan = types.SimpleNamespace(
        two=next(slots), ffn=next(slots), act=next(slots), gates=next(slots), hid=next(slots), cross=next(slots),
        own=next(slots), head=next(slots), half=next(slots), small=levels(), up_a=levels(), up_b=levels(),
        out=levels(), query=levels(), down=levels(), value=levels(),
    )

    def got(n, start, stop):
        return [pltpu.VMEM((blocks >> (level + 1), block, n), BF16) for level in range(start, stop)]

    def taken(name):
        return pltpu.VMEM(inputs[name].shape, inputs[name].dtype)

    sem = pltpu.SemaphoreType.DMA
    token_rows = pltpu.VMEM((rows, width), BF16)
    scratch = dict(
        act=pltpu.VMEM((rows, half), BF16), hid=taken("hid"), two_t=taken("two_t"), pre=taken("pre"),
        cot_t=taken("cot_t"), two_own=token_rows, two_in=token_rows, ffn_in=token_rows, head_in=token_rows,
        act_in=pltpu.VMEM((rows, half), BF16), gates_in=pltpu.VMEM((he, rows), F32),
        hid_in=pltpu.VMEM((blocks // 2, block, rows), BF16), grad_mixed=pltpu.VMEM((rows, width), F32),
        small=pltpu.VMEM((8, width), F32), small_in=pltpu.VMEM((bits, 8, width), F32),
        logits=pltpu.VMEM((2 * he, rows), F32), ga=pltpu.VMEM((heads, dh, rows), BF16),
        gq=pltpu.VMEM((hd, rows), BF16), gk=pltpu.VMEM((heads, dh, 2 * rows), F32),
        gv=pltpu.VMEM((heads, dh, 2 * rows), F32), grel=pltpu.VMEM((hd, 4 * rows), BF16),
        cross_out=pltpu.VMEM((2, heads, dh, rows), BF16), cross_in=pltpu.VMEM((2, heads, dh, rows), BF16),
        own_in=pltpu.VMEM((2 * hd + tail, rows), BF16), half_in=pltpu.VMEM((block, half), BF16),
        half_out=pltpu.VMEM((block, half), BF16),
        got_up_a=got(half, 0, bits), got_up_b=got(half, 0, bits), got_out=got(hed, 0, bits),
        got_query=got(query_n, 0, bits), got_down=got(half, 0, bits - 1), got_value=got(sizes.value_n, 1, bits),
        send_out=pltpu.VMEM((blocks >> 1, block, hed), BF16), acc_out=pltpu.VMEM((blocks >> 1, block, hed), BF16),
        load_sem=sem((len(inputs) + 3,)), send_sem=sem((count,)), recv_sem=sem((count,)),
    )
    late = dict(
        table=taken("table"), each=taken("each"), sigs=taken("sigs"), gates=taken("gates"), wv=taken("wv"),
        wq=taken("wq"), wk=taken("wk"), rt=taken("rt"), x=taken("x"), gain=taken("gain"),
        own_out=pltpu.VMEM((2 * hd + tail, rows), BF16), grads=pltpu.VMEM((sizes.value_n, rows), BF16),
        send_up_a=pltpu.VMEM((blocks >> 2, block, half), BF16), send_up_b=pltpu.VMEM((blocks >> 2, block, half), BF16),
        acc_up_a=pltpu.VMEM((blocks >> 2, block, half), F32), acc_up_b=pltpu.VMEM((blocks >> 2, block, half), F32),
        send_query=pltpu.VMEM((blocks >> 1, block, query_n), BF16),
        acc_query=pltpu.VMEM((blocks >> 1, block, query_n), F32),
        send_down=pltpu.VMEM((blocks >> 1, block, half), BF16), acc_down=pltpu.VMEM((blocks >> 1, block, half), F32),
        send_value=pltpu.VMEM((blocks >> 2, block, sizes.value_n), BF16),
        acc_value=pltpu.VMEM((blocks >> 1, block, sizes.value_n), F32),
    )
    sizes.late_names, sizes.late_scratch = list(late), list(late.values())
    outs = dict(
        g_down=((block, 2 * half), F32), g_up=((block, 2 * half), F32), g_out=((he, block, dh), F32),
        g_value=((he, block, dh), F32), g_query=((block, heads, dh), F32), g_key=((block, heads, dh), F32),
        g_rel=((block, heads, dh), F32), g_router=((block, 2 * he), F32), small_out=((8, width), F32),
        grad_input=((rows, width), F32), output=((rows, width), BF16),
    )
    flat, tree = jax.tree.flatten(list(scratch.values()))

    def kernel(*refs):
        held = jax.tree.unflatten(tree, refs[len(inputs) + len(outs):])
        late_kernel(
            *refs[:len(inputs) + len(outs)], *held, names=[None] * 0 + [n + "_" for n in inputs] + list(outs) + list(scratch),
            loaded=list(inputs), sizes=sizes, plan=plan,
        )

    vmem, anywhere = pl.BlockSpec(memory_space=pltpu.VMEM), pl.BlockSpec(memory_space=pl.ANY)
    results = pl.pallas_call(
        kernel,
        in_specs=[anywhere] * len(inputs),
        out_specs=[vmem] * (len(outs) - 2) + [anywhere] * 2,
        out_shape=[jax.ShapeDtypeStruct(shape, dtype) for shape, dtype in outs.values()],
        scratch_shapes=flat,
        compiler_params=pltpu.CompilerParams(collective_id=0, has_side_effects=True, vmem_limit_bytes=60 << 20),
        cost_estimate=pl.CostEstimate(flops=4 * 10**10, bytes_accessed=10**8, transcendentals=0),
    )(*inputs.values())
    return types.SimpleNamespace(**dict(zip(outs, results)))


def body(
    layer_input, mem_keys, mem_values, route_value, route_output, ln1_gain, ln1_bias, w_query, w_key, w_rel,
    content_bias, position_bias, w_value, w_out, router_value, router_output, ln2_gain, ln2_bias, w_up, w_down,
    cotangent,
):
    rows, width = layer_input.shape
    heads, dh = content_bias.shape
    experts = w_value.shape[1]
    odd = (lax.axis_index("dp") % 2).astype(jnp.int32)
    scale = 1.0 / math.sqrt(dh)
    total_keys = 4 * rows
    block = rows // 2
    hd = heads * dh
    hed = heads * experts * dh

    wq = jnp.transpose(w_query, (1, 2, 0)).reshape(hd, width)
    wk = jnp.transpose(w_key, (1, 2, 0)).reshape(hd, width)
    wr = jnp.transpose(w_rel, (1, 2, 0)).reshape(hd, width)
    wv = jnp.transpose(w_value, (0, 1, 3, 2)).reshape(hed, width)
    wo = w_out.reshape(hed, width)
    rt = jnp.concatenate(
        [jnp.transpose(r, (1, 2, 0)).reshape(heads * experts, width) for r in (router_value, router_output)], axis=0
    )
    mem_k = jnp.transpose(mem_keys, (1, 2, 0))
    mem_v = jnp.transpose(mem_values, (1, 2, 0))
    part_mem_k = swapped(mem_k, "dp", 1)
    part_mem_v = swapped(mem_v, "dp", 1)
    rv = jnp.transpose(route_value, (0, 2, 1))
    ro = jnp.transpose(route_output, (0, 2, 1))
    he2 = 2 * heads * experts

    pre_args = (
        layer_input, ln1_gain.reshape(1, width), ln1_bias.reshape(1, width), wq, wk, wv, rt,
        content_bias.reshape(hd, 1), position_bias.reshape(hd, 1), rv, ro,
    )
    pre_shapes = [
        ((rows, width), BF16), ((hd, rows), BF16), ((hd, rows), BF16), ((hd, rows), BF16), ((hd, rows), BF16),
        ((hed, rows), BF16), ((he2, rows), F32), ((he2, rows), F32),
    ]
    hidden, qu, qv, key_own, value_own, value_each, sig, gate = pl.pallas_call(
        functools.partial(pre_kernel, heads=heads, experts=experts, dh=dh),
        out_shape=[jax.ShapeDtypeStruct(s, t) for s, t in pre_shapes],
        compiler_params=pltpu.CompilerParams(vmem_limit_bytes=50 << 20),
        cost_estimate=pl.CostEstimate(flops=4 * 10**9, bytes_accessed=8 * 10**6, transcendentals=10**5),
    )(*pre_args)

    qu = qu.reshape(heads, dh, rows)
    qv = qv.reshape(heads, dh, rows)
    key_own = key_own.reshape(heads, dh, rows)
    value_own = value_own.reshape(heads, dh, rows)
    part_k = swapped(key_own, "dp", 1)
    part_v = swapped(value_own, "dp", 1)
    table = jnp.asarray(position_table(total_keys, width))
    rel = mm(wr, table).astype(BF16).reshape(heads, dh, total_keys)

    odd_arg = odd.reshape(1)
    kv = (key_own, part_k, mem_k, part_mem_k, value_own, part_v, mem_v, part_mem_v)
    smem = pl.BlockSpec(memory_space=pltpu.SMEM)

    def per_head(last):
        return pl.BlockSpec((1, dh, last), lambda h: (h, 0, 0))

    per_block = per_head(rows)
    probs_spec = pl.BlockSpec((1, rows, total_keys), lambda h: (h, 0, 0))
    probs, att = pl.pallas_call(
        functools.partial(attend_kernel, scale=scale, rows=rows, block=block),
        grid=(heads,),
        in_specs=[smem, per_block, per_block, per_head(total_keys)] + [per_head(rows)] * 8,
        out_specs=[probs_spec, per_block],
        out_shape=[
            jax.ShapeDtypeStruct((heads, rows, total_keys), BF16), jax.ShapeDtypeStruct((heads, dh, rows), BF16),
        ],
        compiler_params=pltpu.CompilerParams(vmem_limit_bytes=50 << 20),
        cost_estimate=pl.CostEstimate(flops=10**10, bytes_accessed=10**7, transcendentals=2 * 10**6),
    )(odd_arg, qu, qv, rel, *kv)

    wide_count, depth = lax.axis_size(WIDE), lax.axis_size(DEEP)
    blocks = wide_count * depth
    block_rows, he = width // blocks, heads * experts
    hidden_units = w_up.shape[1]
    wide_bits, deep_bits = bit_names(wide_count, depth)
    gate_v, gate_o, sig_v, sig_o = gate[:he], gate[he:], sig[:he], sig[he:]
    gain_two, bias_two = ln2_gain.reshape(1, width), ln2_bias.reshape(1, width)
    sem = pltpu.SemaphoreType.DMA

    def shapes(*pairs):
        return [jax.ShapeDtypeStruct(shape, dtype) for shape, dtype in pairs]

    half = (2, rows, hidden_units // 2)
    first_half = (blocks // 2, block_rows, hidden_units // 2)
    cot_in = swapped(cotangent, WIDE, 1)
    mixed, gated, act, pre, two_t, cot_t, up_a, up_b, two_out, ffn_out = pl.pallas_call(
        functools.partial(
            feed_kernel, heads=heads, experts=experts, dh=dh, wide_bits=wide_bits, share=width // wide_count,
            block=block_rows,
        ),
        out_shape=shapes(
            ((rows, width), F32), ((hed, rows), BF16), (half, BF16), (half, BF16), ((width, rows), BF16),
            ((width, 2 * rows), BF16), (first_half, BF16), (first_half, BF16), ((rows, width), BF16),
            ((rows, width), BF16),
        ),
        scratch_shapes=[pltpu.VMEM((rows, width), BF16)] * 3 + [sem((1,)), sem((1,))],
        compiler_params=pltpu.CompilerParams(collective_id=1, has_side_effects=True, vmem_limit_bytes=56 << 20),
        cost_estimate=pl.CostEstimate(flops=2 * 10**10, bytes_accessed=3 * 10**7, transcendentals=10**6),
    )(att, gate_o, layer_input, cotangent, cot_in, wo, gain_two, bias_two, w_up, w_down)

    flip = jnp.asarray(np.eye(block // 2, dtype=np.float32)[::-1].astype(BF16))
    hid = jnp.transpose(hidden).reshape(blocks // 2, 2, block_rows, rows)
    inputs = dict(
        two_out=two_out, ffn_out=ffn_out, act=act, up_a=up_a, up_b=up_b, hid=hid, gates=gate_v, mixed=mixed,
        cot=cotangent, gain_two=gain_two, att=att, gate_o=gate_o, sig_o=sig_o, wo=wo, gated=gated,
        flip=flip, probs=probs, qu=qu, qv=qv, rel=rel,
        key_own=key_own, part_k=part_k, mem_k=mem_k, part_mem_k=part_mem_k,
        value_own=value_own, part_v=part_v, mem_v=mem_v, part_mem_v=part_mem_v,
        table=table, two_t=two_t, pre=pre, cot_t=cot_t, sigs=sig_v, each=value_each, wv=wv, wq=wq, wk=wk, rt=rt,
        x=layer_input, gain=ln1_gain.reshape(1, width),
    )
    done = late_call(inputs, types.SimpleNamespace(
        heads=heads, experts=experts, dh=dh, rows=rows, width=width, wide=wide_count, deep=depth, block=block_rows,
        hidden_units=hidden_units, scale=scale, query_rows=block // 2,
    ))
    first = (lax.axis_index(WIDE) * depth + lax.axis_index(DEEP)) * block_rows
    ln = lax.dynamic_slice_in_dim(done.small_out, first, block_rows, axis=1)
    biases = done.small_out[4:, :dh].reshape(2, heads, dh)
    routers = done.g_router.reshape(block_rows, 2, heads, experts)

    def by_expert(values):
        return values.reshape(heads, experts, block_rows, dh)

    return (
        done.output, done.grad_input, ln[0], ln[1], done.g_query, done.g_key, done.g_rel, biases[0], biases[1],
        by_expert(done.g_value), jnp.transpose(by_expert(done.g_out), (0, 1, 3, 2)), routers[:, 0], routers[:, 1],
        ln[2], ln[3], done.g_up, jnp.transpose(done.g_down),
    )


def solution(mesh):
    tokens = ("wide", "dp")
    return jax.shard_map(
        body,
        mesh=mesh,
        in_specs=(
            P(tokens, None), P(tokens, "head", None), P(tokens, "head", None), P("head", tokens, None),
            P("head", tokens, None), P(), P(), P(None, "head", None), P(None, "head", None), P(None, "head", None),
            P("head", None), P("head", None), P("head", None, None, None), P("head", None, None, None),
            P(None, "head", None), P(None, "head", None), P(), P(), P(None, "head"), P("head", None), P(tokens, None),
        ),
        out_specs=(
            P(tokens, None), P(tokens, None), P(tokens), P(tokens), P(tokens, "head", None), P(tokens, "head", None),
            P(tokens, "head", None), P("head", None), P("head", None), P("head", None, tokens, None),
            P("head", None, None, tokens), P(tokens, "head", None), P(tokens, "head", None), P(tokens), P(tokens),
            P(tokens, "head"), P("head", tokens),
        ),
        check_vma=False,
    )
```

```python
import functools
import math
import types

import jax
import jax.numpy as jnp
import numpy as np
from jax import lax
from jax.experimental import pallas as pl
from jax.experimental.pallas import tpu as pltpu
from jax.sharding import PartitionSpec as P

EPSILON = 1e-05
NEG_LARGE = -1e30
F32 = jnp.float32
BF16 = jnp.bfloat16
WIDE, DEEP = "wide", "dp"

NN = (((1,), (0,)), ((), ()))
NT = (((1,), (1,)), ((), ()))
TN = (((0,), (0,)), ((), ()))


def mm(a, b, dims=NN):
    return lax.dot_general(a, b, dims, preferred_element_type=F32)


def swapped(block, axis, bit):
    count = lax.axis_size(axis)
    return lax.ppermute(block, axis, [(i, i ^ bit) for i in range(count)])


def normalize(values):
    row_mean = jnp.mean(values, axis=-1, keepdims=True)
    centered = values - row_mean
    variance = jnp.mean(centered * centered, axis=-1, keepdims=True)
    inverse = lax.rsqrt(variance + EPSILON)
    return (centered * inverse, inverse)


def norm_back(grad_normed, normed, inverse):
    first_mean = jnp.mean(grad_normed, axis=-1, keepdims=True)
    second_mean = jnp.mean(grad_normed * normed, axis=-1, keepdims=True)
    return inverse * (grad_normed - first_mean - normed * second_mean)


def position_table(extent, model_width):
    half_width = model_width // 2
    frequencies = np.exp(
        np.arange(half_width, dtype=np.float32) * np.float32(-2.0 * math.log(10000.0) / model_width)
    ).astype(np.float32)
    distance = np.arange(extent - 1, -1, -1).astype(np.float32)
    angles = (frequencies[:, None] * distance[None, :]).astype(np.float64)
    return np.concatenate([np.sin(angles), np.cos(angles)], axis=0).astype(np.float32).astype(BF16)


def whole(array):
    return pl.BlockSpec(array.shape, lambda *_: (0,) * len(array.shape))


def pre_kernel(x_ref, gain_ref, bias_ref, wq_ref, wk_ref, wv_ref, rt_ref, cb_ref, pb_ref, rv_ref, ro_ref,
               hid_ref, qu_ref, qv_ref, k_ref, v_ref, each_ref, sig_ref, gate_ref, *, heads, experts, dh):
    normed, _ = normalize(x_ref[...].astype(F32))
    hid = (normed * gain_ref[...] + bias_ref[...]).astype(BF16)
    hid_ref[...] = hid
    logits = mm(rt_ref[...], hid, NT)
    sig = 1.0 / (1.0 + jnp.exp(-logits))
    masks = []
    for routes in (rv_ref, ro_ref):
        for h in range(heads):
            for e in range(experts):
                hit = (routes[h, 0:1, :] == e) | (routes[h, 1:2, :] == e)
                masks.append(jnp.where(hit, 1.0, 0.0))
    gate = sig * jnp.concatenate(masks, axis=0)
    sig_ref[...] = sig
    gate_ref[...] = gate
    k_ref[...] = mm(wk_ref[...], hid, NT).astype(BF16)
    for h in range(heads):
        total = None
        for e in range(experts):
            rows = pl.ds((h * experts + e) * dh, dh)
            each = mm(wv_ref[rows, :], hid, NT)
            each_ref[rows, :] = each.astype(BF16)
            term = gate[h * experts + e:h * experts + e + 1, :] * each
            total = term if total is None else total + term
        v_ref[pl.ds(h * dh, dh), :] = total.astype(BF16)
    queries = mm(wq_ref[...], hid, NT)
    qu_ref[...] = (queries + cb_ref[...]).astype(BF16)
    qv_ref[...] = (queries + pb_ref[...]).astype(BF16)


def attend_kernel(odd_ref, qu_ref, qv_ref, rel_ref, ko_ref, kp_ref, km_ref, kn_ref, vo_ref, vp_ref, vm_ref, vn_ref,
                  probs_ref, att_ref, *, scale, rows, block):
    odd = odd_ref[0] == 1
    k_one = jnp.where(odd, kp_ref[0], kn_ref[0])
    v_one = jnp.where(odd, vp_ref[0], vn_ref[0])
    keys = (kn_ref[0], km_ref[0], k_one, ko_ref[0])
    values = (vn_ref[0], vm_ref[0], v_one, vo_ref[0])
    total_keys = 4 * rows
    first = jnp.where(odd, 0, rows)
    for base in range(0, rows, block):
        here = slice(base, base + block)
        positional = mm(qv_ref[0, :, here], rel_ref[0], TN)
        positional = pltpu.roll(positional, total_keys - rows + 1 + base, 1, stride=1, stride_axis=0)
        content = jnp.concatenate([mm(qu_ref[0, :, here], k, TN) for k in keys], axis=1)
        row = lax.broadcasted_iota(jnp.int32, (block, total_keys), 0) + base
        col = lax.broadcasted_iota(jnp.int32, (block, total_keys), 1)
        visible = (col <= row + (total_keys - rows)) & (col >= first)
        scores = jnp.where(visible, (content + positional) * scale, NEG_LARGE)
        peak = jnp.max(scores, axis=1, keepdims=True)
        exponents = jnp.exp(scores - peak)
        total = jnp.sum(exponents, axis=1, keepdims=True)
        probs = (exponents * (1.0 / total)).astype(BF16)
        probs_ref[0, here, :] = probs
        att = None
        for i, v in enumerate(values):
            part = mm(v, probs[:, i * rows:(i + 1) * rows], NT)
            att = part if att is None else att + part
        att_ref[0, :, here] = att.astype(BF16)


def gelu_both(x):
    c = math.sqrt(2.0 / math.pi)
    square = x * x
    t = jnp.tanh(c * x * (1.0 + 0.044715 * square))
    half = 0.5 * (1.0 + t)
    return x * half, half + 0.5 * x * (1.0 - t * t) * (c * (1.0 + 3.0 * 0.044715 * square))


def meet(*devices):
    barrier = pltpu.get_barrier_semaphore()
    for device in devices:
        pl.semaphore_signal(barrier, inc=1, device_id=device, device_id_type=pl.DeviceIdType.MESH)
    pl.semaphore_wait(barrier, len(devices))


def other_core():
    return (1 - lax.axis_index("head"), lax.axis_index("wide"), lax.axis_index("dp"))


class Swap:
    def __init__(self, src, dst, sems, slot, device):
        self.parts = (src, dst, sems, slot, device)
        self.copy().start()

    def copy(self):
        src, dst, sems, slot, device = self.parts
        return pltpu.make_async_remote_copy(
            src_ref=src, dst_ref=dst, send_sem=sems[0].at[slot], recv_sem=sems[1].at[slot],
            device_id=device() if callable(device) else device, device_id_type=pl.DeviceIdType.MESH,
        )

    def wait(self):
        self.copy().wait()


remote = Swap


def feed_kernel(att_ref, gate_ref, gate_v_ref, hid_ref, x_ref, cot_ref, cot_in_ref, wo_ref, gain_ref, bias_ref, up_ref,
                down_ref,
                mixed_ref, gated_ref, act_ref, pre_ref, two_t_ref, cot_t_ref, first_ref, second_ref, two_out_ref, ffn_ref,
                hid_in_ref, att_in_ref, gate_in_ref, gate_v_in_ref,
                part_ref, got_ref, two_ref, send_sem, recv_sem, *, heads, experts, dh, wide_bits, share, block):
    there = other_core()
    rows = x_ref.shape[0]
    deep = lax.axis_index(DEEP)
    near = deep % 2
    beside = (lax.axis_index("head"), lax.axis_index(WIDE), deep + 1 - 2 * near)
    sems = (send_sem, recv_sem)
    meet(there, beside)
    early = [
        remote(att_ref, att_in_ref, sems, 1, beside), remote(gate_ref, gate_in_ref, sems, 2, beside),
        remote(gate_v_ref, gate_v_in_ref, sems, 3, beside),
        remote(hid_ref.at[:, 1 - near], hid_in_ref, sems, 4, beside),
    ]
    for h in range(heads):
        for e in range(experts):
            at = h * experts + e
            gated_ref[at * dh:(at + 1) * dh, :] = (gate_ref[at:at + 1, :] * att_ref[h].astype(F32)).astype(BF16)
    part_ref[...] = mm(gated_ref[...], wo_ref[...], TN).astype(BF16)
    swap = remote(part_ref, got_ref, sems, 0, there)
    cot_t_ref[:, 0:rows] = cot_ref[...].T
    cot_t_ref[:, rows:] = cot_in_ref[...].T
    swap.wait()
    mixed = x_ref[...].astype(F32) + (part_ref[...].astype(F32) + got_ref[...].astype(F32))
    mixed_ref[...] = mixed
    normed, _ = normalize(mixed)
    two = (normed * gain_ref[...] + bias_ref[...]).astype(BF16)
    two_ref[...] = two
    two_t_ref[...] = two.T.reshape(two_t_ref.shape)
    chunk = act_ref.shape[2] // 2
    for part in range(4):
        here = slice(part * chunk, (part + 1) * chunk)
        value, slope = gelu_both(mm(two_ref[...], up_ref[:, here]))
        inner = slice(part % 2 * chunk, part % 2 * chunk + chunk)
        act_ref[part // 2, :, inner] = value.astype(BF16)
        pre_ref[part // 2, :, inner] = (mm(cot_ref[...], down_ref[here, :], NT) * slope).astype(BF16)
    total = None
    for k in range(2):
        half = slice(k * 2 * chunk, (k + 1) * 2 * chunk)
        term = mm(pre_ref[k], up_ref[:, half], NT)
        total = term if total is None else total + term
    two_out_ref[...] = total.astype(BF16)
    bit = bit_order("y", wide_bits, [])[0]
    other = 1 - (lax.axis_index(WIDE) // (1 << bit[1])) % 2
    count = share // block
    for number, run in enumerate(picks(natural(wide_bits), {bit: other})):
        left = two_t_ref[pl.ds(pl.multiple_of(run * (count // 2), count // 2), count // 2)].reshape(share, rows)
        piece = mm(left, pre_ref[0]).astype(BF16)
        for j in range(count):
            first_ref[number * count + j] = piece[j * block:(j + 1) * block]
    piece = mm(two_t_ref[:, 1 - near].reshape(-1, rows), pre_ref[1]).astype(BF16)
    for j in range(second_ref.shape[0]):
        second_ref[j] = piece[j * block:(j + 1) * block]
    total = None
    for k in range(2):
        term = mm(act_ref[k], down_ref[k * 2 * chunk:(k + 1) * 2 * chunk, :])
        total = term if total is None else total + term
    ffn_ref[...] = total.astype(BF16)
    for swap in early:
        swap.wait()


def bit_names(wide_count, depth):
    wide_bits = [(WIDE, b) for b in range(int(math.log2(wide_count)))]
    deep_bits = [(DEEP, b) for b in range(int(math.log2(depth)))]
    return wide_bits, deep_bits


def bit_order(axes, wide_bits, deep_bits):
    half = len(wide_bits) // 2
    groups = dict(x=wide_bits[:half], y=wide_bits[half:], n=deep_bits[:1], f=deep_bits[1:])
    return [bit for axis in axes for bit in groups[axis]]


def natural(bits):
    return [b for b in sorted(bits, key=lambda b: (b[0] == WIDE, b[1]), reverse=True)]


def picks(left, fixed):
    free = [b for b in left if b not in fixed]
    found = []
    for number in range(1 << len(free)):
        index = 0
        for place, b in enumerate(left):
            if b in fixed:
                digit = fixed[b]
            else:
                digit = (number >> (len(free) - 1 - free.index(b))) & 1
            index = index + digit * (1 << (len(left) - 1 - place))
        found.append(index)
    return found


class Tree:
    def __init__(self, order, left, acc, send, got, slots, me):
        self.order, self.left, self.acc, self.send, self.got, self.slots, self.me = order, left, acc, send, got, slots, me
        self.level = 0
        self.copies = {}

    def fixed(self, own):
        bit = self.order[self.level]
        return {bit: self.me[bit] if own else 1 - self.me[bit]}

    def launch(self, sems, partner, src=None):
        got = self.got[self.level]
        src = self.send.at[pl.ds(0, got.shape[0])] if src is None else src
        bit = self.order[self.level]
        self.copies[self.level] = remote(src, got, sems, self.slots[self.level], lambda: partner(bit))

    def step(self):
        self.left = [b for b in self.left if b != self.order[self.level]]
        self.level += 1

    def arrive(self):
        self.copies[self.level - 1].wait()
        return self.got[self.level - 1]

    def advance(self, sems, partner):
        got = self.arrive() if self.level else None

        def piece(index):
            mine = self.acc[index].astype(F32)
            return mine if got is None else mine + got[index].astype(F32)

        for place, index in enumerate(picks(self.left, self.fixed(False))):
            self.send[place] = piece(index).astype(BF16)
        self.launch(sems, partner)
        for place, index in enumerate(picks(self.left, self.fixed(True))):
            self.acc[place] = piece(index).astype(self.acc.dtype)
        self.step()

    def finish(self, index=0):
        return self.acc[index].astype(F32) + self.got[self.level - 1][index].astype(F32)


def late_kernel(*refs, names, loaded, sizes, plan):
    r = types.SimpleNamespace(**dict(zip(names, refs)))
    given = types.SimpleNamespace(**dict(zip(loaded, refs)))
    heads, experts, dh, rows, width = sizes.heads, sizes.experts, sizes.dh, sizes.rows, sizes.width
    wide_count, depth, block = sizes.wide, sizes.deep, sizes.block
    hd, he, hed = heads * dh, heads * experts, heads * experts * dh
    blocks = wide_count * depth
    wide_bits, deep_bits = bit_names(wide_count, depth)
    bits = wide_bits + deep_bits
    place = {WIDE: lax.axis_index(WIDE), DEEP: lax.axis_index(DEEP)}
    head = lax.axis_index("head")
    me = {b: (place[b[0]] // (1 << b[1])) % 2 for b in bits}
    x_bit, near = wide_bits[0], deep_bits[0]

    def partner(bit):
        axis, number = bit
        other = place[axis] + (1 - 2 * me[bit]) * (1 << number)
        return (head, other, place[DEEP]) if axis == WIDE else (head, place[WIDE], other)

    across = other_core()
    sems = (r.send_sem, r.recv_sem)
    loads = {}

    def fetch(target, name, slot):
        loads[name] = pltpu.make_async_copy(getattr(given, name), target, r.load_sem.at[slot])
        loads[name].start()

    order = {name: number for number, name in enumerate(loaded)}

    def fetch_all(**targets):
        for name, target in targets.items():
            fetch(target, name, order[name])

    def ready(*wanted):
        for name in wanted:
            if loads.get(name) is not None:
                loads[name].wait()
                loads[name] = None

    def tree_of(axes, left, acc, send, got, slots):
        return Tree(bit_order(axes, wide_bits, deep_bits), natural(left), acc, send, got, slots, me)

    up_a = tree_of("yxnf", bits, None, None, r.got_up_a, plan.up_a)
    up_b = tree_of("nxyf", bits, None, None, r.got_up_b, plan.up_b)
    share = width // wide_count
    per_share = share // block

    def runs(fixed):
        return picks(natural(wide_bits), {b: v for b, v in fixed.items() if b[0] == WIDE})

    def rows_of(run):
        return pl.ds(pl.multiple_of(run * share, share), share)

    meet(across, *[partner(b) for b in bits])
    two_swap = remote(given.two_out, r.two_in, sems, plan.two, across)
    act_swap = remote(given.act.at[1 - me[x_bit]], r.act_in, sems, plan.act, partner(x_bit))
    up_b.launch(sems, partner, given.up_b)
    up_a.launch(sems, partner, given.up_a)
    fetch_all(two_out=r.two_own, hid=r.hid, hid_in=r.hid_in, two_t=r.two_t, pre=r.pre, cot_t=r.cot_t)
    loads["act"] = pltpu.make_async_copy(given.act.at[me[x_bit]], r.act, r.load_sem.at[len(loaded) + 2])
    loads["act"].start()

    def attention(probs, qu, qv, rel, key_own, part_k, mem_k, part_mem_k, value_own, part_v, mem_v, part_mem_v, flip,
                  acc):
        fetch_all(
            probs=probs, qu=qu, qv=qv, rel=rel, key_own=key_own, part_k=part_k, mem_k=mem_k, part_mem_k=part_mem_k,
            value_own=value_own, part_v=part_v, mem_v=mem_v, part_mem_v=part_mem_v, flip=flip,
        )

        def out_back(mixed_ref, cot, gain, att_ref, gate_ref, sig_ref, wo, low_ref, ffn_own):
            fetch_all(
                mixed=mixed_ref, cot=cot, gain_two=gain, att=att_ref, gate_o=gate_ref, sig_o=sig_ref, wo=wo,
                ffn_out=ffn_own,
            )
            ready("mixed")
            normed, inverse = normalize(mixed_ref[...])
            two_swap.wait()
            ffn_swap = remote(given.ffn_out, r.ffn_in, sems, plan.ffn, across)
            ready("two_out", "cot", "gain_two")
            grad_two = r.two_own[...].astype(F32) + r.two_in[...].astype(F32)
            r.small[2:3, :] = jnp.sum(grad_two * normed, axis=0, keepdims=True)
            r.small[3:4, :] = jnp.sum(grad_two, axis=0, keepdims=True)
            grad_mixed = cot[...].astype(F32) + norm_back(grad_two * gain[...], normed, inverse)
            r.grad_mixed[...] = grad_mixed
            low_ref[...] = grad_mixed.astype(BF16)
            low_t = low_ref[...].T.reshape(blocks // 2, 2, block, rows)
            first, second = low_t[:, 0], low_t[:, 1]
            r.gm_out[...] = jnp.where(me[near] == 1, first, second)
            r.gm[...] = jnp.where(me[near] == 1, second, first)
            gm_swap.append(remote(r.gm_out, r.gm_in, sems, plan.gm, lambda: partner(near)))
            ready("att", "gate_o", "sig_o", "wo")
            for h in range(heads):
                att = att_ref[h].astype(F32)
                total = None
                for e in range(experts):
                    at = h * experts + e
                    back = mm(wo[at * dh:(at + 1) * dh, :], low_ref[...], NT)
                    gate = gate_ref[at:at + 1, :]
                    grad_gate = jnp.sum(att * back, axis=0, keepdims=True)
                    r.logits[he + at:he + at + 1, :] = grad_gate * gate * (1.0 - sig_ref[at:at + 1, :])
                    total = gate * back if total is None else total + gate * back
                r.ga[h] = total.astype(BF16)
            ffn_swap.wait()
            ready("ffn_out")
            ffn_own[...] = (mixed_ref[...] + (ffn_own[...].astype(F32) + r.ffn_in[...].astype(F32))).astype(BF16)
            written = pltpu.make_async_copy(ffn_own, r.output, r.load_sem.at[len(loaded)])
            written.start()
            written.wait()

        pl.run_scoped(
            out_back, pltpu.VMEM((rows, width), F32), pltpu.VMEM((rows, width), BF16), pltpu.VMEM((1, width), F32),
            pltpu.VMEM((heads, dh, rows), BF16), pltpu.VMEM((he, rows), F32), pltpu.VMEM((he, rows), F32),
            pltpu.VMEM((hed, width), BF16), pltpu.VMEM((rows, width), BF16), pltpu.VMEM((rows, width), BF16),
        )
        ready("probs", "qu", "qv", "rel", "key_own", "part_k", "mem_k", "part_mem_k")
        ready("value_own", "part_v", "mem_v", "part_mem_v", "flip")
        odd = place[DEEP] % 2 == 1
        size = sizes.query_rows
        for h in range(heads):
            k_one = jnp.where(odd, part_k[h], part_mem_k[h])
            v_one = jnp.where(odd, part_v[h], part_mem_v[h])
            keys = (part_mem_k[h], mem_k[h], k_one, key_own[h])
            values = (part_mem_v[h], mem_v[h], v_one, value_own[h])
            bias_u = bias_v = None
            for base in range(0, rows, size):
                here = slice(base, base + size)
                turned = mm(flip[...], probs[h, here, :])
                ga = mm(r.ga[h, :, here], flip[...]).astype(BF16)
                queries_u = mm(qu[h, :, here], flip[...]).astype(BF16)
                queries_v = mm(qv[h, :, here], flip[...]).astype(BF16)
                gp = jnp.concatenate([mm(ga, v, TN) for v in values], axis=1)
                weighted = turned * gp
                delta = jnp.sum(weighted, axis=1, keepdims=True)
                gs = ((weighted - turned * delta) * sizes.scale).astype(BF16)
                gk = mm(queries_u, gs[:, 2 * rows:])
                gv = mm(ga, turned[:, 2 * rows:].astype(BF16))
                gqu = None
                for i, k in enumerate(keys):
                    part = mm(k, gs[:, i * rows:(i + 1) * rows], NT)
                    gqu = part if gqu is None else gqu + part
                gpos = pltpu.roll(gs, rows - size - base, 1, stride=1, stride_axis=0)
                gqv = mm(rel[h], gpos, NT)
                grel = mm(queries_v, gpos)
                r.gq[h * dh:(h + 1) * dh, here] = mm((gqu + gqv).astype(BF16), flip[...]).astype(BF16)
                ones = jnp.ones((8, size), F32)
                sum_u, sum_v = [
                    lax.dot_general(ones, g, NT, precision=lax.Precision.HIGHEST, preferred_element_type=F32)
                    for g in (gqu, gqv)
                ]
                if base == 0:
                    r.gk[h] = gk
                    r.gv[h] = gv
                    acc[...] = grel
                    bias_u, bias_v = sum_u, sum_v
                else:
                    r.gk[h] += gk
                    r.gv[h] += gv
                    acc[...] += grel
                    bias_u, bias_v = bias_u + sum_u, bias_v + sum_v
            r.grel[h * dh:(h + 1) * dh, :] = acc[...].astype(BF16)
            r.small[4 + h:5 + h, 0:dh] = bias_u[0:1]
            r.small[4 + heads + h:5 + heads + h, 0:dh] = bias_v[0:1]
        r.cross_out[0] = r.gk[:, :, :rows].astype(BF16)
        r.cross_out[1] = r.gv[:, :, :rows].astype(BF16)
        crossing.append(remote(r.cross_out, r.cross_in, sems, plan.cross, lambda: partner(near)))

    crossing, gm_swap = [], []
    hd_up = sizes.hd_up
    r.small[4:8, :] = jnp.zeros((4, width), F32)
    total_keys = 4 * rows
    chunk_shape = pltpu.VMEM((heads, dh, rows), BF16)
    pl.run_scoped(
        attention, pltpu.VMEM((heads, rows, total_keys), BF16), chunk_shape, chunk_shape,
        pltpu.VMEM((heads, dh, total_keys), BF16), *([chunk_shape] * 8),
        pltpu.VMEM((sizes.query_rows, sizes.query_rows), BF16), pltpu.VMEM((dh, total_keys), F32),
    )

    def rest(*held):
        b = types.SimpleNamespace(**dict(zip(sizes.late_names, held)))
        fetch_all(
            gated=b.gated, att_in=b.att_in, gate_o_in=b.gate_o_in, each=b.each, sigs=b.sigs, gates=b.gates, wv=b.wv,
            wq=b.wq, wk=b.wk, rt=b.rt, x=b.x, gain=b.gain, gates_in=b.gates_in, table=b.table,
        )
        up_a.acc, up_a.send, up_b.acc, up_b.send = b.acc_up_a, b.send_up_a, b.acc_up_b, b.send_up_b
        far = [v for v in bits if v != near]
        out = tree_of("xyf", far, b.acc_out, b.send_out, r.got_out, plan.out)
        value = tree_of("yxf", far, b.acc_value, b.send_value, r.got_value, plan.value)
        query = tree_of("xynf", bits, b.acc_query, b.send_query, r.got_query, plan.query)
        down = tree_of("ynf", bits, b.acc_down, b.send_down, r.got_down, plan.down)
        half_count = len(wide_bits) // 2
        down.order = down.order[:half_count] + wide_bits[1:half_count] + down.order[half_count:]
        near_rows = blocks // 2 * block
        half = sizes.hidden_units // 2
        small = r.small
        state = []

        def down_part(own):
            for number, run in enumerate(runs(down.fixed(own))):
                at_rows = rows_of(run)
                part = mm(r.cot_t[at_rows, 0:rows], r.act[...]) + mm(r.cot_t[at_rows, rows:], r.act_in[...])
                for k in range(per_share):
                    at = number * per_share + k
                    piece = part[k * block:(k + 1) * block]
                    if own:
                        down.acc[at] = piece.astype(BF16)
                    else:
                        down.send[at] = piece.astype(BF16)
            if own:
                down.step()
            else:
                down.launch(sems, partner)

        def run_rows(ref, run):
            count = per_share // 2
            return ref[pl.ds(pl.multiple_of(run * count, count), count)].reshape(share, rows)

        def up_a_keep():
            for number, run in enumerate(runs(up_a.fixed(True))):
                part = mm(run_rows(r.two_t, run), r.pre[0])
                for k in range(per_share):
                    up_a.acc[number * per_share + k] = part[k * block:(k + 1) * block].astype(BF16)
            up_a.step()

        def up_b_keep():
            part = mm(r.two_t[:, me[near]].reshape(near_rows, rows), r.pre[1])
            for at in range(blocks // 2):
                up_b.acc[at] = part[at * block:(at + 1) * block].astype(BF16)
            up_b.step()

        def out_part():
            ready("gated", "att_in", "gate_o_in")
            mine = mm(r.gm[...].reshape(near_rows, rows), b.gated[...], NT)
            for at in range(blocks // 2):
                out.acc[at] = mine[at * block:(at + 1) * block].astype(BF16)
            for h in range(heads):
                for e in range(experts):
                    at = h * experts + e
                    b.gated[at * dh:(at + 1) * dh, :] = (
                        b.gate_o_in[at:at + 1, :] * b.att_in[h].astype(F32)
                    ).astype(BF16)
            gm_swap[0].wait()
            theirs = mm(r.gm_in[...].reshape(near_rows, rows), b.gated[...], NT)
            for at in range(blocks // 2):
                out.acc[at] = (out.acc[at].astype(F32) + theirs[at * block:(at + 1) * block]).astype(BF16)
            out.advance(sems, partner)

        def own_part():
            ready("each", "sigs", "gates")
            crossing[0].wait()
            even = jnp.where(place[DEEP] % 2 == 0, 1.0, 0.0)
            for h in range(heads):
                gk = r.gk[h, :, rows:] + even * r.cross_in[0, h].astype(F32)
                gv = r.gv[h, :, rows:] + even * r.cross_in[1, h].astype(F32)
                b.own_out[h * dh:(h + 1) * dh, :] = gv.astype(BF16)
                b.own_out[hd + h * dh:hd + (h + 1) * dh, :] = gk.astype(BF16)
                for e in range(experts):
                    at = h * experts + e
                    gate = b.gates[at:at + 1, :]
                    grad_gate = jnp.sum(gv * b.each[at * dh:(at + 1) * dh, :].astype(F32), axis=0, keepdims=True)
                    r.logits[at:at + 1, :] = grad_gate * gate * (1.0 - b.sigs[at:at + 1, :])
                    b.grads[at * dh:(at + 1) * dh, :] = (gate * gv).astype(BF16)
            tail = b.own_out.shape[0] - 2 * hd
            logits = jnp.concatenate([r.logits[0:2 * he, :], jnp.zeros((tail - 2 * he, rows), F32)], axis=0)
            b.own_out[2 * hd:, :] = logits.astype(BF16)
            state_own.append(remote(b.own_out, r.own_in, sems, plan.own, partner(near)))
            b.grads[hed:, :] = b.own_out[hd:, :]

        def hidden_part():
            ready("wv", "wq", "wk", "rt")
            grad_hidden = mm(b.grads[0:hed, :], b.wv[...], TN)
            grad_hidden += mm(r.gq[...], b.wq[...], TN)
            grad_hidden += mm(b.grads[hed:hed + hd, :], b.wk[...], TN)
            grad_hidden += mm(b.grads[hed + hd:hed + hd + 2 * he, :], b.rt[...], TN)
            r.two_own[...] = grad_hidden.astype(BF16)
            state_head.append(remote(r.two_own, r.head_in, sems, plan.head, across))

        def norm_part():
            ready("x", "gain")
            state_head[0].wait()
            grad_hidden = r.two_own[...].astype(F32) + r.head_in[...].astype(F32)
            normed, inverse = normalize(b.x[...].astype(F32))
            small[0:1, :] = jnp.sum(grad_hidden * normed, axis=0, keepdims=True)
            small[1:2, :] = jnp.sum(grad_hidden, axis=0, keepdims=True)
            state.append(remote(small, r.small_in.at[0], sems, plan.small[0], partner(bits[0])))
            r.grad_mixed[...] += norm_back(grad_hidden * b.gain[...], normed, inverse)
            input_copy = pltpu.make_async_copy(r.grad_mixed, r.grad_input, r.load_sem.at[len(loaded) + 1])
            input_copy.start()
            state_input.append(input_copy)

        def small_step():
            at = len(state) - 1
            if at == len(bits):
                return
            state[at].wait()
            small[...] = small[...] + r.small_in[at]
            state.append(
                None if at + 1 == len(bits)
                else remote(small, r.small_in.at[at + 1], sems, plan.small[at + 1], partner(bits[at + 1]))
            )

        def value_own():
            ready("hid")
            mine = mm(r.hid[:, me[near]].reshape(near_rows, rows), b.grads[...], NT)
            for at in range(blocks // 2):
                value.acc[at] = mine[at * block:(at + 1) * block]

        def value_part():
            ready("hid_in", "gates_in")
            state_own[0].wait()
            for at in range(he):
                h = at // experts
                b.grads[at * dh:(at + 1) * dh, :] = (
                    b.gates_in[at:at + 1, :] * r.own_in[h * dh:(h + 1) * dh, :].astype(F32)
                ).astype(BF16)
            b.grads[hed:, :] = r.own_in[hd:, :]
            theirs = mm(r.hid_in[...].reshape(near_rows, rows), b.grads[...], NT)
            for at in range(blocks // 2):
                value.acc[at] += theirs[at * block:(at + 1) * block]
            value.advance(sems, partner)

        def query_part(own):
            if not own and hd_up > hd:
                for at in range(blocks // 2):
                    query.send[at, :, hd:hd_up] = jnp.zeros((block, hd_up - hd), BF16)
                    query.acc[at, :, hd:hd_up] = jnp.zeros((block, hd_up - hd), BF16)
            ready("hid", "table")
            for number, run in enumerate(runs(query.fixed(own))):
                part = mm(run_rows(r.hid, run), r.gq[...], NT)
                part_rel = mm(b.table[rows_of(run), :], r.grel[...], NT)
                for k in range(per_share):
                    at = number * per_share + k
                    piece, piece_rel = part[k * block:(k + 1) * block], part_rel[k * block:(k + 1) * block]
                    if own:
                        query.acc[at, :, 0:hd] = piece.astype(BF16)
                        query.acc[at, :, hd_up:] = piece_rel.astype(BF16)
                    else:
                        query.send[at, :, 0:hd] = piece.astype(BF16)
                        query.send[at, :, hd_up:] = piece_rel.astype(BF16)
            if own:
                query.step()
            else:
                query.launch(sems, partner)

        state_own, state_head, state_input = [], [], []
        keep, leave = me[x_bit], 1 - me[x_bit]

        def half_part():
            down.arrive()
            r.half_out[...] = down.finish(leave).astype(BF16)
            state_own.append(remote(r.half_out, r.half_in, sems, plan.half, partner(x_bit)))
            r.g_down[:, pl.ds(pl.multiple_of(keep * half, half), half)] = down.finish(keep)

        def next_level(tree):
            if tree.level < len(tree.order):
                tree.advance(sems, partner)

        ready("two_t", "pre")
        up_b_keep()
        ready("act", "cot_t")
        act_swap.wait()
        down_part(False)
        up_a_keep()
        next_level(up_a)
        out_part()
        next_level(up_a)
        own_part()
        next_level(up_b)
        down_part(True)
        hidden_part()
        norm_part()
        next_level(down)
        next_level(up_a)
        next_level(out)
        next_level(up_b)
        value_own()
        value_part()
        next_level(up_b)
        query_part(False)
        query_part(True)
        next_level(out)
        next_level(down)
        next_level(value)
        next_level(query)
        small_step()
        small_step()
        next_level(query)
        small_step()
        next_level(value)
        next_level(query)
        while any(tree.level < len(tree.order) for tree in (up_a, up_b, out, query, value, down)):
            for tree in (up_a, up_b, out, query, value, down):
                next_level(tree)
        half_part()
        while len(state) <= len(bits):
            small_step()
        r.small_out[...] = small[...]
        for number, tree in enumerate((up_a, up_b)):
            tree.arrive()
            r.g_up[:, number * half:(number + 1) * half] = tree.finish()
        out.arrive()
        total = out.finish()
        for at in range(he):
            r.g_out[at] = total[:, at * dh:(at + 1) * dh]
        value.arrive()
        total = value.finish()
        for at in range(he):
            r.g_value[at] = total[:, at * dh:(at + 1) * dh]
        for h in range(heads):
            r.g_key[:, h, :] = total[:, hed + h * dh:hed + (h + 1) * dh]
        r.g_router[...] = total[:, hed + hd:hed + hd + 2 * he]
        query.arrive()
        total = query.finish()
        for h in range(heads):
            r.g_query[:, h, :] = total[:, h * dh:(h + 1) * dh]
            r.g_rel[:, h, :] = total[:, hd_up + h * dh:hd_up + (h + 1) * dh]
        state_own[1].wait()
        r.g_down[:, pl.ds(pl.multiple_of(leave * half, half), half)] = r.half_in[...].astype(F32)
        state_input[0].wait()

    pl.run_scoped(rest, *sizes.late_scratch)


def late_call(inputs, sizes):
    wide_bits, deep_bits = bit_names(sizes.wide, sizes.deep)
    bits = len(wide_bits) + len(deep_bits)
    blocks = sizes.wide * sizes.deep
    block, rows, width, heads, dh = sizes.block, sizes.rows, sizes.width, sizes.heads, sizes.dh
    he, hd = heads * sizes.experts, heads * dh
    hed, half = he * dh, sizes.hidden_units // 2
    tail = 32
    sizes.hd_up = -(-hd // 128) * 128
    sizes.value_n = hed + hd + tail
    query_n = sizes.hd_up + hd
    count = 10 + 7 * bits
    slots = iter(range(count))

    def levels():
        return [next(slots) for _ in range(bits)]

    plan = types.SimpleNamespace(
        two=next(slots), ffn=next(slots), act=next(slots), gm=next(slots), cross=next(slots),
        own=next(slots), head=next(slots), half=next(slots), small=levels(), up_a=levels(), up_b=levels(),
        out=levels(), query=levels(), down=levels(), value=levels(),
    )

    def got(n, start, stop):
        return [pltpu.VMEM((blocks >> (level + 1), block, n), BF16) for level in range(start, stop)]

    def taken(name):
        return pltpu.VMEM(inputs[name].shape, inputs[name].dtype)

    sem = pltpu.SemaphoreType.DMA
    token_rows = pltpu.VMEM((rows, width), BF16)
    scratch = dict(
        act=pltpu.VMEM((rows, half), BF16), hid=taken("hid"), two_t=taken("two_t"), pre=taken("pre"),
        cot_t=taken("cot_t"), two_own=token_rows, two_in=token_rows, ffn_in=token_rows, head_in=token_rows,
        act_in=pltpu.VMEM((rows, half), BF16), hid_in=taken("hid_in"), gm=taken("hid_in"), gm_in=taken("hid_in"),
        gm_out=taken("hid_in"), grad_mixed=pltpu.VMEM((rows, width), F32),
        small=pltpu.VMEM((8, width), F32), small_in=pltpu.VMEM((bits, 8, width), F32),
        logits=pltpu.VMEM((2 * he, rows), F32), ga=pltpu.VMEM((heads, dh, rows), BF16),
        gq=pltpu.VMEM((hd, rows), BF16), gk=pltpu.VMEM((heads, dh, 2 * rows), F32),
        gv=pltpu.VMEM((heads, dh, 2 * rows), F32), grel=pltpu.VMEM((hd, 4 * rows), BF16),
        cross_out=pltpu.VMEM((2, heads, dh, rows), BF16), cross_in=pltpu.VMEM((2, heads, dh, rows), BF16),
        own_in=pltpu.VMEM((2 * hd + tail, rows), BF16), half_in=pltpu.VMEM((block, half), BF16),
        half_out=pltpu.VMEM((block, half), BF16),
        got_up_a=got(half, 0, bits), got_up_b=got(half, 0, bits), got_out=got(hed, 1, bits),
        got_query=got(query_n, 0, bits), got_down=got(half, 0, bits - 1), got_value=got(sizes.value_n, 1, bits),
        load_sem=sem((len(inputs) + 3,)), send_sem=sem((count,)), recv_sem=sem((count,)),
    )
    late = dict(
        gated=taken("gated"), att_in=taken("att_in"), gate_o_in=taken("gate_o_in"), gates_in=taken("gates_in"),
        send_out=pltpu.VMEM((blocks >> 2, block, hed), BF16), acc_out=pltpu.VMEM((blocks >> 1, block, hed), BF16),
        table=taken("table"), each=taken("each"), sigs=taken("sigs"), gates=taken("gates"), wv=taken("wv"),
        wq=taken("wq"), wk=taken("wk"), rt=taken("rt"), x=taken("x"), gain=taken("gain"),
        own_out=pltpu.VMEM((2 * hd + tail, rows), BF16), grads=pltpu.VMEM((sizes.value_n, rows), BF16),
        send_up_a=pltpu.VMEM((blocks >> 2, block, half), BF16), send_up_b=pltpu.VMEM((blocks >> 2, block, half), BF16),
        acc_up_a=pltpu.VMEM((blocks >> 1, block, half), BF16), acc_up_b=pltpu.VMEM((blocks >> 1, block, half), BF16),
        send_query=pltpu.VMEM((blocks >> 1, block, query_n), BF16),
        acc_query=pltpu.VMEM((blocks >> 1, block, query_n), BF16),
        send_down=pltpu.VMEM((blocks >> 1, block, half), BF16), acc_down=pltpu.VMEM((blocks >> 1, block, half), BF16),
        send_value=pltpu.VMEM((blocks >> 2, block, sizes.value_n), BF16),
        acc_value=pltpu.VMEM((blocks >> 1, block, sizes.value_n), F32),
    )
    sizes.late_names, sizes.late_scratch = list(late), list(late.values())
    outs = dict(
        g_down=((block, 2 * half), F32), g_up=((block, 2 * half), F32), g_out=((he, block, dh), F32),
        g_value=((he, block, dh), F32), g_query=((block, heads, dh), F32), g_key=((block, heads, dh), F32),
        g_rel=((block, heads, dh), F32), g_router=((block, 2 * he), F32), small_out=((8, width), F32),
        grad_input=((rows, width), F32), output=((rows, width), BF16),
    )
    flat, tree = jax.tree.flatten(list(scratch.values()))

    def kernel(*refs):
        held = jax.tree.unflatten(tree, refs[len(inputs) + len(outs):])
        late_kernel(
            *refs[:len(inputs) + len(outs)], *held, names=[None] * 0 + [n + "_" for n in inputs] + list(outs) + list(scratch),
            loaded=list(inputs), sizes=sizes, plan=plan,
        )

    vmem, anywhere = pl.BlockSpec(memory_space=pltpu.VMEM), pl.BlockSpec(memory_space=pl.ANY)
    results = pl.pallas_call(
        kernel,
        in_specs=[anywhere] * len(inputs),
        out_specs=[vmem] * (len(outs) - 2) + [anywhere] * 2,
        out_shape=[jax.ShapeDtypeStruct(shape, dtype) for shape, dtype in outs.values()],
        scratch_shapes=flat,
        compiler_params=pltpu.CompilerParams(collective_id=0, has_side_effects=True, vmem_limit_bytes=60 << 20),
        cost_estimate=pl.CostEstimate(flops=4 * 10**10, bytes_accessed=10**8, transcendentals=0),
    )(*inputs.values())
    return types.SimpleNamespace(**dict(zip(outs, results)))


def body(
    layer_input, mem_keys, mem_values, route_value, route_output, ln1_gain, ln1_bias, w_query, w_key, w_rel,
    content_bias, position_bias, w_value, w_out, router_value, router_output, ln2_gain, ln2_bias, w_up, w_down,
    cotangent,
):
    rows, width = layer_input.shape
    heads, dh = content_bias.shape
    experts = w_value.shape[1]
    odd = (lax.axis_index("dp") % 2).astype(jnp.int32)
    scale = 1.0 / math.sqrt(dh)
    total_keys = 4 * rows
    block = rows // 2
    hd = heads * dh
    hed = heads * experts * dh

    wq = jnp.transpose(w_query, (1, 2, 0)).reshape(hd, width)
    wk = jnp.transpose(w_key, (1, 2, 0)).reshape(hd, width)
    wr = jnp.transpose(w_rel, (1, 2, 0)).reshape(hd, width)
    wv = jnp.transpose(w_value, (0, 1, 3, 2)).reshape(hed, width)
    wo = w_out.reshape(hed, width)
    rt = jnp.concatenate(
        [jnp.transpose(r, (1, 2, 0)).reshape(heads * experts, width) for r in (router_value, router_output)], axis=0
    )
    mem_k = jnp.transpose(mem_keys, (1, 2, 0))
    mem_v = jnp.transpose(mem_values, (1, 2, 0))
    part_mem_k = swapped(mem_k, "dp", 1)
    part_mem_v = swapped(mem_v, "dp", 1)
    rv = jnp.transpose(route_value, (0, 2, 1))
    ro = jnp.transpose(route_output, (0, 2, 1))
    he2 = 2 * heads * experts

    pre_args = (
        layer_input, ln1_gain.reshape(1, width), ln1_bias.reshape(1, width), wq, wk, wv, rt,
        content_bias.reshape(hd, 1), position_bias.reshape(hd, 1), rv, ro,
    )
    pre_shapes = [
        ((rows, width), BF16), ((hd, rows), BF16), ((hd, rows), BF16), ((hd, rows), BF16), ((hd, rows), BF16),
        ((hed, rows), BF16), ((he2, rows), F32), ((he2, rows), F32),
    ]
    hidden, qu, qv, key_own, value_own, value_each, sig, gate = pl.pallas_call(
        functools.partial(pre_kernel, heads=heads, experts=experts, dh=dh),
        out_shape=[jax.ShapeDtypeStruct(s, t) for s, t in pre_shapes],
        compiler_params=pltpu.CompilerParams(vmem_limit_bytes=50 << 20),
        cost_estimate=pl.CostEstimate(flops=4 * 10**9, bytes_accessed=8 * 10**6, transcendentals=10**5),
    )(*pre_args)

    qu = qu.reshape(heads, dh, rows)
    qv = qv.reshape(heads, dh, rows)
    key_own = key_own.reshape(heads, dh, rows)
    value_own = value_own.reshape(heads, dh, rows)
    part_k = swapped(key_own, "dp", 1)
    part_v = swapped(value_own, "dp", 1)
    table = jnp.asarray(position_table(total_keys, width))
    rel = mm(wr, table).astype(BF16).reshape(heads, dh, total_keys)

    odd_arg = odd.reshape(1)
    kv = (key_own, part_k, mem_k, part_mem_k, value_own, part_v, mem_v, part_mem_v)
    smem = pl.BlockSpec(memory_space=pltpu.SMEM)

    def per_head(last):
        return pl.BlockSpec((1, dh, last), lambda h: (h, 0, 0))

    per_block = per_head(rows)
    probs_spec = pl.BlockSpec((1, rows, total_keys), lambda h: (h, 0, 0))
    probs, att = pl.pallas_call(
        functools.partial(attend_kernel, scale=scale, rows=rows, block=block),
        grid=(heads,),
        in_specs=[smem, per_block, per_block, per_head(total_keys)] + [per_head(rows)] * 8,
        out_specs=[probs_spec, per_block],
        out_shape=[
            jax.ShapeDtypeStruct((heads, rows, total_keys), BF16), jax.ShapeDtypeStruct((heads, dh, rows), BF16),
        ],
        compiler_params=pltpu.CompilerParams(vmem_limit_bytes=50 << 20),
        cost_estimate=pl.CostEstimate(flops=10**10, bytes_accessed=10**7, transcendentals=2 * 10**6),
    )(odd_arg, qu, qv, rel, *kv)

    wide_count, depth = lax.axis_size(WIDE), lax.axis_size(DEEP)
    blocks = wide_count * depth
    block_rows, he = width // blocks, heads * experts
    hidden_units = w_up.shape[1]
    wide_bits, deep_bits = bit_names(wide_count, depth)
    gate_v, gate_o, sig_v, sig_o = gate[:he], gate[he:], sig[:he], sig[he:]
    gain_two, bias_two = ln2_gain.reshape(1, width), ln2_bias.reshape(1, width)
    sem = pltpu.SemaphoreType.DMA

    def shapes(*pairs):
        return [jax.ShapeDtypeStruct(shape, dtype) for shape, dtype in pairs]

    half = (2, rows, hidden_units // 2)
    first_half = (blocks // 2, block_rows, hidden_units // 2)
    cot_in = swapped(cotangent, WIDE, 1)
    hid = jnp.transpose(hidden).reshape(blocks // 2, 2, block_rows, rows)
    (mixed, gated, act, pre, two_t, cot_t, up_a, up_b, two_out, ffn_out, hid_in, att_in, gate_o_in,
     gates_in) = pl.pallas_call(
        functools.partial(
            feed_kernel, heads=heads, experts=experts, dh=dh, wide_bits=wide_bits, share=width // wide_count,
            block=block_rows,
        ),
        out_shape=shapes(
            ((rows, width), F32), ((hed, rows), BF16), (half, BF16), (half, BF16), (hid.shape, BF16),
            ((width, 2 * rows), BF16), (first_half, BF16), (first_half, BF16), ((rows, width), BF16),
            ((rows, width), BF16), ((blocks // 2, block_rows, rows), BF16), (att.shape, BF16), (gate_o.shape, F32),
            (gate_v.shape, F32),
        ),
        scratch_shapes=[pltpu.VMEM((rows, width), BF16)] * 3 + [sem((5,)), sem((5,))],
        compiler_params=pltpu.CompilerParams(collective_id=1, has_side_effects=True, vmem_limit_bytes=56 << 20),
        cost_estimate=pl.CostEstimate(flops=2 * 10**10, bytes_accessed=3 * 10**7, transcendentals=10**6),
    )(att, gate_o, gate_v, hid, layer_input, cotangent, cot_in, wo, gain_two, bias_two, w_up, w_down)

    flip = jnp.asarray(np.eye(block // 2, dtype=np.float32)[::-1].astype(BF16))
    inputs = dict(
        two_out=two_out, ffn_out=ffn_out, act=act, up_a=up_a, up_b=up_b, hid=hid, hid_in=hid_in, gates=gate_v,
        gates_in=gates_in, gate_o_in=gate_o_in, att_in=att_in, mixed=mixed,
        cot=cotangent, gain_two=gain_two, att=att, gate_o=gate_o, sig_o=sig_o, wo=wo, gated=gated,
        flip=flip, probs=probs, qu=qu, qv=qv, rel=rel,
        key_own=key_own, part_k=part_k, mem_k=mem_k, part_mem_k=part_mem_k,
        value_own=value_own, part_v=part_v, mem_v=mem_v, part_mem_v=part_mem_v,
        table=table, two_t=two_t, pre=pre, cot_t=cot_t, sigs=sig_v, each=value_each, wv=wv, wq=wq, wk=wk, rt=rt,
        x=layer_input, gain=ln1_gain.reshape(1, width),
    )
    done = late_call(inputs, types.SimpleNamespace(
        heads=heads, experts=experts, dh=dh, rows=rows, width=width, wide=wide_count, deep=depth, block=block_rows,
        hidden_units=hidden_units, scale=scale, query_rows=block // 2,
    ))
    first = (lax.axis_index(WIDE) * depth + lax.axis_index(DEEP)) * block_rows
    ln = lax.dynamic_slice_in_dim(done.small_out, first, block_rows, axis=1)
    biases = done.small_out[4:, :dh].reshape(2, heads, dh)
    routers = done.g_router.reshape(block_rows, 2, heads, experts)

    def by_expert(values):
        return values.reshape(heads, experts, block_rows, dh)

    return (
        done.output, done.grad_input, ln[0], ln[1], done.g_query, done.g_key, done.g_rel, biases[0], biases[1],
        by_expert(done.g_value), jnp.transpose(by_expert(done.g_out), (0, 1, 3, 2)), routers[:, 0], routers[:, 1],
        ln[2], ln[3], done.g_up, jnp.transpose(done.g_down),
    )


def solution(mesh):
    tokens = ("wide", "dp")
    return jax.shard_map(
        body,
        mesh=mesh,
        in_specs=(
            P(tokens, None), P(tokens, "head", None), P(tokens, "head", None), P("head", tokens, None),
            P("head", tokens, None), P(), P(), P(None, "head", None), P(None, "head", None), P(None, "head", None),
            P("head", None), P("head", None), P("head", None, None, None), P("head", None, None, None),
            P(None, "head", None), P(None, "head", None), P(), P(), P(None, "head"), P("head", None), P(tokens, None),
        ),
        out_specs=(
            P(tokens, None), P(tokens, None), P(tokens), P(tokens), P(tokens, "head", None), P(tokens, "head", None),
            P(tokens, "head", None), P("head", None), P("head", None), P("head", None, tokens, None),
            P("head", None, None, tokens), P(tokens, "head", None), P(tokens, "head", None), P(tokens), P(tokens),
            P(tokens, "head"), P("head", tokens),
        ),
        check_vma=False,
    )
```

```python
import functools
import math
import types

import jax
import jax.numpy as jnp
import numpy as np
from jax import lax
from jax.experimental import pallas as pl
from jax.experimental.pallas import tpu as pltpu
from jax.sharding import PartitionSpec as P

EPSILON = 1e-05
NEG_LARGE = -1e30
F32 = jnp.float32
BF16 = jnp.bfloat16
WIDE, DEEP = "wide", "dp"

NN = (((1,), (0,)), ((), ()))
NT = (((1,), (1,)), ((), ()))
TN = (((0,), (0,)), ((), ()))


def mm(a, b, dims=NN):
    return lax.dot_general(a, b, dims, preferred_element_type=F32)


def normalize(values):
    row_mean = jnp.mean(values, axis=-1, keepdims=True)
    centered = values - row_mean
    variance = jnp.mean(centered * centered, axis=-1, keepdims=True)
    inverse = lax.rsqrt(variance + EPSILON)
    return (centered * inverse, inverse)


def norm_back(grad_normed, normed, inverse):
    first_mean = jnp.mean(grad_normed, axis=-1, keepdims=True)
    second_mean = jnp.mean(grad_normed * normed, axis=-1, keepdims=True)
    return inverse * (grad_normed - first_mean - normed * second_mean)


def position_table(extent, model_width):
    half_width = model_width // 2
    frequencies = np.exp(
        np.arange(half_width, dtype=np.float32) * np.float32(-2.0 * math.log(10000.0) / model_width)
    ).astype(np.float32)
    distance = np.arange(extent - 1, -1, -1).astype(np.float32)
    angles = (frequencies[:, None] * distance[None, :]).astype(np.float64)
    return np.concatenate([np.sin(angles), np.cos(angles)], axis=0).astype(np.float32).astype(BF16)


def whole(array):
    return pl.BlockSpec(array.shape, lambda *_: (0,) * len(array.shape))


def gelu_both(x):
    c = math.sqrt(2.0 / math.pi)
    square = x * x
    t = jnp.tanh(c * x * (1.0 + 0.044715 * square))
    half = 0.5 * (1.0 + t)
    return x * half, half + 0.5 * x * (1.0 - t * t) * (c * (1.0 + 3.0 * 0.044715 * square))


def meet(*devices):
    barrier = pltpu.get_barrier_semaphore()
    for device in devices:
        pl.semaphore_signal(barrier, inc=1, device_id=device, device_id_type=pl.DeviceIdType.MESH)
    pl.semaphore_wait(barrier, len(devices))


def other_core():
    return (1 - lax.axis_index("head"), lax.axis_index("wide"), lax.axis_index("dp"))


class Swap:
    def __init__(self, src, dst, sems, slot, device):
        self.parts = (src, dst, sems, slot, device)
        self.copy().start()

    def copy(self):
        src, dst, sems, slot, device = self.parts
        return pltpu.make_async_remote_copy(
            src_ref=src, dst_ref=dst, send_sem=sems[0].at[slot], recv_sem=sems[1].at[slot],
            device_id=device() if callable(device) else device, device_id_type=pl.DeviceIdType.MESH,
        )

    def wait(self):
        self.copy().wait()


remote = Swap


def early_kernel(*refs, given_names, out_names, held_names, sizes):
    count = len(given_names)
    given = types.SimpleNamespace(**dict(zip(given_names, refs)))
    out = types.SimpleNamespace(**dict(zip(out_names, refs[count:])))
    r = types.SimpleNamespace(**dict(zip(held_names, refs[count + len(out_names):])))
    heads, experts, dh, rows, width = sizes.heads, sizes.experts, sizes.dh, sizes.rows, sizes.width
    deep, wide = lax.axis_index(DEEP), lax.axis_index(WIDE)
    near = deep % 2
    beside = (lax.axis_index("head"), wide, deep + 1 - 2 * near)
    across = (lax.axis_index("head"), wide + 1 - 2 * (wide % 2), deep)
    sems = (r.send_sem, r.recv_sem)
    loads, writes = {}, []

    def fetch(*names):
        for name in names:
            slot = given_names.index(name)
            loads[name] = pltpu.make_async_copy(getattr(given, name), getattr(r, name), r.load_sem.at[slot])
            loads[name].start()

    def ready(*names):
        for name in names:
            loads[name].wait()

    def put(name, source, *at):
        target = getattr(out, name)
        if at:
            source, target = source.at[at], target.at[at]
        writes.append(pltpu.make_async_copy(source, target, r.write_sem.at[len(writes)]))
        writes[-1].start()

    fetch(*sizes.loaded)
    meet(beside, across)
    part = rows // 2
    swaps = [
        Swap(given.mem_k, r.part_mem_k, sems, 0, beside), Swap(given.mem_v, r.part_mem_v, sems, 1, beside),
        Swap(given.cot.at[pl.ds(0, part)], out.cot_in, sems, 2, across),
    ]
    ready("x", "gain", "bias")
    normed, _ = normalize(r.x[...].astype(F32))
    hid = (normed * r.gain[...] + r.bias[...]).astype(BF16)
    r.hid[...] = hid
    ready("wk")
    for h in range(heads):
        r.key_own[h] = mm(r.wk[h * dh:(h + 1) * dh, :], r.hid[...], NT).astype(BF16)
    swaps.append(Swap(r.key_own, r.part_k, sems, 3, beside))
    ready("rt", "rv", "ro")
    logits = mm(r.rt[...], r.hid[...], NT)
    sig = 1.0 / (1.0 + jnp.exp(-logits))
    masks = []
    for routes in (r.rv, r.ro):
        for h in range(heads):
            for e in range(experts):
                hit = (routes[h, 0:1, :] == e) | (routes[h, 1:2, :] == e)
                masks.append(jnp.where(hit, 1.0, 0.0))
    gate = sig * jnp.concatenate(masks, axis=0)
    he = heads * experts
    r.gate[...] = gate
    out.gate_v[...] = gate[:he]
    out.gate_o[...] = gate[he:]
    out.sig_v[...] = sig[:he]
    out.sig_o[...] = sig[he:]
    ready("wv")
    for h in range(heads):
        total = None
        for e in range(experts):
            at = h * experts + e
            each = mm(r.wv[at * dh:(at + 1) * dh, :], r.hid[...], NT)
            r.each[at * dh:(at + 1) * dh, :] = each.astype(BF16)
            term = r.gate[at:at + 1, :] * each
            total = term if total is None else total + term
        r.value_own[h] = total.astype(BF16)
    swaps.append(Swap(r.value_own, r.part_v, sems, 4, beside))
    put("each", r.each)
    put("key_own", r.key_own)
    put("value_own", r.value_own)
    ready("wq", "cb", "pb")
    eye = (
        lax.broadcasted_iota(jnp.int32, (dh, dh), 0) == lax.broadcasted_iota(jnp.int32, (dh, dh), 1)
    ).astype(F32)

    def column(row):
        spread = jnp.broadcast_to(row, (8, dh))
        return lax.dot_general(
            eye, spread, NT, precision=lax.Precision.HIGHEST, preferred_element_type=F32
        )[:, 0:1]

    for h in range(heads):
        queries = mm(r.wq[h * dh:(h + 1) * dh, :], r.hid[...], NT)
        r.qu[h] = (queries + column(r.cb[h:h + 1, :])).astype(BF16)
        r.qv[h] = (queries + column(r.pb[h:h + 1, :])).astype(BF16)
    put("qu", r.qu)
    put("qv", r.qv)
    ready("wr", "table")
    for h in range(heads):
        r.rel[h] = mm(r.wr[h * dh:(h + 1) * dh, :], r.table[...]).astype(BF16)
    put("rel", r.rel)
    r.hid_t[...] = r.hid[...].T.reshape(r.hid_t.shape)
    put("hid", r.hid_t)
    total_keys, size = 4 * rows, sizes.query_rows
    for h in range(heads):
        for base in range(0, rows, size):
            here = slice(base, base + size)
            positional = mm(r.qv[h, :, here], r.rel[h], TN)
            r.scores[h, here, :] = pltpu.roll(
                positional, total_keys - rows + 1 + base, 1, stride=1, stride_axis=0
            )
    odd = near == 1
    ready("mem_k", "mem_v")
    for swap in swaps[:2] + swaps[3:]:
        swap.wait()
    put("part_k", r.part_k)
    put("part_v", r.part_v)
    put("part_mem_k", r.part_mem_k)
    put("part_mem_v", r.part_mem_v)
    first = jnp.where(odd, 0, rows)
    for h in range(heads):
        k_one = jnp.where(odd, r.part_k[h], r.part_mem_k[h])
        v_one = jnp.where(odd, r.part_v[h], r.part_mem_v[h])
        keys = (r.part_mem_k[h], r.mem_k[h], k_one, r.key_own[h])
        values = (r.part_mem_v[h], r.mem_v[h], v_one, r.value_own[h])
        for base in range(0, rows, size):
            here = slice(base, base + size)
            content = jnp.concatenate([mm(r.qu[h, :, here], k, TN) for k in keys], axis=1)
            row = lax.broadcasted_iota(jnp.int32, (size, total_keys), 0) + base
            col = lax.broadcasted_iota(jnp.int32, (size, total_keys), 1)
            visible = (col <= row + (total_keys - rows)) & (col >= first)
            scores = jnp.where(visible, (content + r.scores[h, here, :]) * sizes.scale, NEG_LARGE)
            peak = jnp.max(scores, axis=1, keepdims=True)
            exponents = jnp.exp(scores - peak)
            total = jnp.sum(exponents, axis=1, keepdims=True)
            probs = (exponents * (1.0 / total)).astype(BF16)
            r.probs[h, here, :] = probs
            put("probs", r.probs, h, pl.ds(base, size))
            att = None
            for i, v in enumerate(values):
                term = mm(v, probs[:, i * rows:(i + 1) * rows], NT)
                att = term if att is None else att + term
            out.att[h, :, here] = att.astype(BF16)
    swaps[2].wait()
    for write in writes:
        write.wait()


def early_call(inputs, sizes):
    heads, experts, dh, rows, width = sizes.heads, sizes.experts, sizes.dh, sizes.rows, sizes.width
    he, hed, hd = heads * experts, heads * experts * dh, heads * dh
    tokens = (heads, dh, rows)
    blocks = sizes.wide * sizes.deep
    hid_shape = (blocks // 2, 2, width // blocks, rows)
    anywhere = dict(
        each=((hed, rows), BF16), key_own=(tokens, BF16), value_own=(tokens, BF16), qu=(tokens, BF16),
        qv=(tokens, BF16), rel=((heads, dh, 4 * rows), BF16), hid=(hid_shape, BF16), part_k=(tokens, BF16),
        part_v=(tokens, BF16), part_mem_k=(tokens, BF16), part_mem_v=(tokens, BF16),
        probs=((heads, rows, 4 * rows), BF16), cot_in=((rows // 2, width), BF16),
    )
    near = dict(
        att=(tokens, BF16), gate_v=((he, rows), F32), gate_o=((he, rows), F32), sig_v=((he, rows), F32),
        sig_o=((he, rows), F32),
    )
    outs = {**anywhere, **near}
    sem = pltpu.SemaphoreType.DMA
    sizes.loaded = [name for name in inputs if name != "cot"]
    held = {name: pltpu.VMEM(inputs[name].shape, inputs[name].dtype) for name in sizes.loaded}
    held.update({name: pltpu.VMEM(shape, dtype) for name, (shape, dtype) in anywhere.items() if name != "cot_in"})
    held.update(
        hid=pltpu.VMEM((rows, width), BF16), hid_t=pltpu.VMEM(hid_shape, BF16),
        scores=pltpu.VMEM((heads, rows, 4 * rows), F32), gate=pltpu.VMEM((2 * he, rows), F32),
        load_sem=sem((len(inputs),)), write_sem=sem((24,)), send_sem=sem((5,)), recv_sem=sem((5,)),
    )
    vmem, hbm = pl.BlockSpec(memory_space=pltpu.VMEM), pl.BlockSpec(memory_space=pl.ANY)
    results = pl.pallas_call(
        functools.partial(
            early_kernel, given_names=list(inputs), out_names=list(outs), held_names=list(held), sizes=sizes
        ),
        in_specs=[hbm] * len(inputs),
        out_specs=[hbm] * len(anywhere) + [vmem] * len(near),
        out_shape=[jax.ShapeDtypeStruct(shape, dtype) for shape, dtype in outs.values()],
        scratch_shapes=list(held.values()),
        compiler_params=pltpu.CompilerParams(collective_id=2, has_side_effects=True, vmem_limit_bytes=58 << 20),
        cost_estimate=pl.CostEstimate(flops=2 * 10**10, bytes_accessed=3 * 10**7, transcendentals=2 * 10**6),
    )(*inputs.values())
    return types.SimpleNamespace(**dict(zip(outs, results)))


def finish_kernel(*refs):
    load_sem, write_sem = refs[-2:]
    count = (len(refs) - 2) // 3
    given, outs, held = refs[:count], refs[count:2 * count], refs[2 * count:3 * count]
    loads = [pltpu.make_async_copy(given[i], held[i], load_sem.at[i]) for i in range(count)]
    writes = [pltpu.make_async_copy(held[i], outs[i], write_sem.at[i]) for i in range(count)]
    for copy in loads:
        copy.start()
    for load, write in zip(loads, writes):
        load.wait()
        write.start()
    for write in writes:
        write.wait()


def finished(*arrays):
    hbm = pl.BlockSpec(memory_space=pl.ANY)
    return pl.pallas_call(
        finish_kernel,
        in_specs=[hbm] * len(arrays),
        out_specs=[hbm] * len(arrays),
        out_shape=[jax.ShapeDtypeStruct(a.shape, a.dtype) for a in arrays],
        scratch_shapes=[pltpu.VMEM(a.shape, a.dtype) for a in arrays] + [pltpu.SemaphoreType.DMA((len(arrays),))] * 2,
        compiler_params=pltpu.CompilerParams(vmem_limit_bytes=60 << 20),
        cost_estimate=pl.CostEstimate(flops=0, bytes_accessed=10**7, transcendentals=0),
    )(*arrays)


def feed_kernel(att_ref, gate_ref, gate_v_ref, hid_ref, x_ref, cot_ref, cot_in_ref, wo_ref, gain_ref, bias_ref, up_ref,
                down_ref,
                mixed_ref, gated_ref, act_ref, pre_ref, two_t_ref, cot_t_ref, first_ref, second_ref, two_out_ref, ffn_ref,
                hid_in_ref, att_in_ref, gate_in_ref, gate_v_in_ref,
                part_ref, got_ref, two_ref, cot_more_ref, send_sem, recv_sem, *, heads, experts, dh, wide_bits, share, block):
    there = other_core()
    rows = x_ref.shape[0]
    deep = lax.axis_index(DEEP)
    near = deep % 2
    beside = (lax.axis_index("head"), lax.axis_index(WIDE), deep + 1 - 2 * near)
    wide = lax.axis_index(WIDE)
    across = (lax.axis_index("head"), wide + 1 - 2 * (wide % 2), deep)
    sems = (send_sem, recv_sem)
    meet(there, beside, across)
    split = rows // 2
    cot_swap = remote(cot_ref.at[pl.ds(split, split)], cot_more_ref, sems, 5, across)
    early = [
        remote(att_ref, att_in_ref, sems, 1, beside), remote(gate_ref, gate_in_ref, sems, 2, beside),
        remote(gate_v_ref, gate_v_in_ref, sems, 3, beside),
        remote(hid_ref.at[:, 1 - near], hid_in_ref, sems, 4, beside),
    ]
    for h in range(heads):
        for e in range(experts):
            at = h * experts + e
            gated_ref[at * dh:(at + 1) * dh, :] = (gate_ref[at:at + 1, :] * att_ref[h].astype(F32)).astype(BF16)
    part_ref[...] = mm(gated_ref[...], wo_ref[...], TN).astype(BF16)
    swap = remote(part_ref, got_ref, sems, 0, there)
    cot_t_ref[:, 0:rows] = cot_ref[...].T
    cot_t_ref[:, rows:rows + split] = cot_in_ref[...].T
    swap.wait()
    mixed = x_ref[...].astype(F32) + (part_ref[...].astype(F32) + got_ref[...].astype(F32))
    mixed_ref[...] = mixed
    normed, _ = normalize(mixed)
    two = (normed * gain_ref[...] + bias_ref[...]).astype(BF16)
    two_ref[...] = two
    two_t_ref[...] = two.T.reshape(two_t_ref.shape)
    chunk = act_ref.shape[2] // 2
    for part in range(4):
        here = slice(part * chunk, (part + 1) * chunk)
        value, slope = gelu_both(mm(two_ref[...], up_ref[:, here]))
        inner = slice(part % 2 * chunk, part % 2 * chunk + chunk)
        act_ref[part // 2, :, inner] = value.astype(BF16)
        pre_ref[part // 2, :, inner] = (mm(cot_ref[...], down_ref[here, :], NT) * slope).astype(BF16)
    total = None
    for k in range(2):
        half = slice(k * 2 * chunk, (k + 1) * 2 * chunk)
        term = mm(pre_ref[k], up_ref[:, half], NT)
        total = term if total is None else total + term
    two_out_ref[...] = total.astype(BF16)
    bit = bit_order("y", wide_bits, [])[0]
    other = 1 - (lax.axis_index(WIDE) // (1 << bit[1])) % 2
    count = share // block
    for number, run in enumerate(picks(natural(wide_bits), {bit: other})):
        left = two_t_ref[pl.ds(pl.multiple_of(run * (count // 2), count // 2), count // 2)].reshape(share, rows)
        piece = mm(left, pre_ref[0]).astype(BF16)
        for j in range(count):
            first_ref[number * count + j] = piece[j * block:(j + 1) * block]
    piece = mm(two_t_ref[:, 1 - near].reshape(-1, rows), pre_ref[1]).astype(BF16)
    for j in range(second_ref.shape[0]):
        second_ref[j] = piece[j * block:(j + 1) * block]
    total = None
    for k in range(2):
        term = mm(act_ref[k], down_ref[k * 2 * chunk:(k + 1) * 2 * chunk, :])
        total = term if total is None else total + term
    ffn_ref[...] = total.astype(BF16)
    cot_swap.wait()
    cot_t_ref[:, rows + split:] = cot_more_ref[...].T
    for swap in early:
        swap.wait()


def bit_names(wide_count, depth):
    wide_bits = [(WIDE, b) for b in range(int(math.log2(wide_count)))]
    deep_bits = [(DEEP, b) for b in range(int(math.log2(depth)))]
    return wide_bits, deep_bits


def bit_order(axes, wide_bits, deep_bits):
    half = len(wide_bits) // 2
    groups = dict(x=wide_bits[:half], y=wide_bits[half:], n=deep_bits[:1], f=deep_bits[1:])
    return [bit for axis in axes for bit in groups[axis]]


def natural(bits):
    return [b for b in sorted(bits, key=lambda b: (b[0] == WIDE, b[1]), reverse=True)]


def picks(left, fixed):
    free = [b for b in left if b not in fixed]
    found = []
    for number in range(1 << len(free)):
        index = 0
        for place, b in enumerate(left):
            if b in fixed:
                digit = fixed[b]
            else:
                digit = (number >> (len(free) - 1 - free.index(b))) & 1
            index = index + digit * (1 << (len(left) - 1 - place))
        found.append(index)
    return found


class Tree:
    def __init__(self, order, left, acc, send, got, slots, me):
        self.order, self.left, self.acc, self.send, self.got, self.slots, self.me = order, left, acc, send, got, slots, me
        self.level = 0
        self.copies = {}

    def fixed(self, own):
        bit = self.order[self.level]
        return {bit: self.me[bit] if own else 1 - self.me[bit]}

    def launch(self, sems, partner, src=None):
        got = self.got[self.level]
        src = self.send.at[pl.ds(0, got.shape[0])] if src is None else src
        bit = self.order[self.level]
        self.copies[self.level] = remote(src, got, sems, self.slots[self.level], lambda: partner(bit))

    def step(self):
        self.left = [b for b in self.left if b != self.order[self.level]]
        self.level += 1

    def arrive(self):
        self.copies[self.level - 1].wait()
        return self.got[self.level - 1]

    def advance(self, sems, partner):
        got = self.arrive() if self.level else None

        def piece(index):
            mine = self.acc[index].astype(F32)
            return mine if got is None else mine + got[index].astype(F32)

        for place, index in enumerate(picks(self.left, self.fixed(False))):
            self.send[place] = piece(index).astype(BF16)
        self.launch(sems, partner)
        for place, index in enumerate(picks(self.left, self.fixed(True))):
            self.acc[place] = piece(index).astype(self.acc.dtype)
        self.step()

    def finish(self, index=0):
        return self.acc[index].astype(F32) + self.got[self.level - 1][index].astype(F32)


def late_kernel(*refs, names, loaded, sizes, plan):
    r = types.SimpleNamespace(**dict(zip(names, refs)))
    given = types.SimpleNamespace(**dict(zip(loaded, refs)))
    heads, experts, dh, rows, width = sizes.heads, sizes.experts, sizes.dh, sizes.rows, sizes.width
    wide_count, depth, block = sizes.wide, sizes.deep, sizes.block
    hd, he, hed = heads * dh, heads * experts, heads * experts * dh
    blocks = wide_count * depth
    wide_bits, deep_bits = bit_names(wide_count, depth)
    bits = wide_bits + deep_bits
    place = {WIDE: lax.axis_index(WIDE), DEEP: lax.axis_index(DEEP)}
    head = lax.axis_index("head")
    me = {b: (place[b[0]] // (1 << b[1])) % 2 for b in bits}
    x_bit, near = wide_bits[0], deep_bits[0]

    def partner(bit):
        axis, number = bit
        other = place[axis] + (1 - 2 * me[bit]) * (1 << number)
        return (head, other, place[DEEP]) if axis == WIDE else (head, place[WIDE], other)

    across = other_core()
    sems = (r.send_sem, r.recv_sem)
    loads = {}

    def fetch(target, name, slot):
        loads[name] = pltpu.make_async_copy(getattr(given, name), target, r.load_sem.at[slot])
        loads[name].start()

    order = {name: number for number, name in enumerate(loaded)}

    def fetch_all(**targets):
        for name, target in targets.items():
            fetch(target, name, order[name])

    def ready(*wanted):
        for name in wanted:
            if loads.get(name) is not None:
                loads[name].wait()
                loads[name] = None

    def tree_of(axes, left, acc, send, got, slots):
        return Tree(bit_order(axes, wide_bits, deep_bits), natural(left), acc, send, got, slots, me)

    up_a = tree_of("yxnf", bits, None, None, r.got_up_a, plan.up_a)
    up_b = tree_of("nxyf", bits, None, None, r.got_up_b, plan.up_b)
    share = width // wide_count
    per_share = share // block

    def runs(fixed):
        return picks(natural(wide_bits), {b: v for b, v in fixed.items() if b[0] == WIDE})

    def rows_of(run):
        return pl.ds(pl.multiple_of(run * share, share), share)

    meet(across, *[partner(b) for b in bits])
    two_swap = remote(given.two_out, r.two_in, sems, plan.two, across)
    act_swap = remote(given.act.at[1 - me[x_bit]], r.act_in, sems, plan.act, partner(x_bit))
    up_b.launch(sems, partner, given.up_b)
    up_a.launch(sems, partner, given.up_a)
    fetch_all(two_out=r.two_own, hid=r.hid, hid_in=r.hid_in, two_t=r.two_t, pre=r.pre, cot_t=r.cot_t)
    loads["act"] = pltpu.make_async_copy(given.act.at[me[x_bit]], r.act, r.load_sem.at[len(loaded) + 2])
    loads["act"].start()

    def attention(probs, qu, qv, rel, key_own, part_k, mem_k, part_mem_k, value_own, part_v, mem_v, part_mem_v, flip,
                  acc):
        fetch_all(
            probs=probs, qu=qu, qv=qv, rel=rel, key_own=key_own, part_k=part_k, mem_k=mem_k, part_mem_k=part_mem_k,
            value_own=value_own, part_v=part_v, mem_v=mem_v, part_mem_v=part_mem_v, flip=flip,
        )

        def out_back(mixed_ref, cot, gain, att_ref, gate_ref, sig_ref, wo, low_ref, ffn_own):
            fetch_all(
                mixed=mixed_ref, cot=cot, gain_two=gain, att=att_ref, gate_o=gate_ref, sig_o=sig_ref, wo=wo,
                ffn_out=ffn_own,
            )
            ready("mixed")
            normed, inverse = normalize(mixed_ref[...])
            two_swap.wait()
            ffn_swap = remote(given.ffn_out, r.ffn_in, sems, plan.ffn, across)
            ready("two_out", "cot", "gain_two")
            grad_two = r.two_own[...].astype(F32) + r.two_in[...].astype(F32)
            r.small[2:3, :] = jnp.sum(grad_two * normed, axis=0, keepdims=True)
            r.small[3:4, :] = jnp.sum(grad_two, axis=0, keepdims=True)
            grad_mixed = cot[...].astype(F32) + norm_back(grad_two * gain[...], normed, inverse)
            r.grad_mixed[...] = grad_mixed
            low_ref[...] = grad_mixed.astype(BF16)
            low_t = low_ref[...].T.reshape(blocks // 2, 2, block, rows)
            first, second = low_t[:, 0], low_t[:, 1]
            r.gm_out[...] = jnp.where(me[near] == 1, first, second)
            r.gm[...] = jnp.where(me[near] == 1, second, first)
            gm_swap.append(remote(r.gm_out, r.gm_in, sems, plan.gm, lambda: partner(near)))
            ready("att", "gate_o", "sig_o", "wo")
            for h in range(heads):
                att = att_ref[h].astype(F32)
                total = None
                for e in range(experts):
                    at = h * experts + e
                    back = mm(wo[at * dh:(at + 1) * dh, :], low_ref[...], NT)
                    gate = gate_ref[at:at + 1, :]
                    grad_gate = jnp.sum(att * back, axis=0, keepdims=True)
                    r.logits[he + at:he + at + 1, :] = grad_gate * gate * (1.0 - sig_ref[at:at + 1, :])
                    total = gate * back if total is None else total + gate * back
                r.ga[h] = total.astype(BF16)
            ffn_swap.wait()
            ready("ffn_out")
            ffn_own[...] = (mixed_ref[...] + (ffn_own[...].astype(F32) + r.ffn_in[...].astype(F32))).astype(BF16)
            written = pltpu.make_async_copy(ffn_own, r.output, r.load_sem.at[len(loaded)])
            written.start()
            written.wait()

        pl.run_scoped(
            out_back, pltpu.VMEM((rows, width), F32), pltpu.VMEM((rows, width), BF16), pltpu.VMEM((1, width), F32),
            pltpu.VMEM((heads, dh, rows), BF16), pltpu.VMEM((he, rows), F32), pltpu.VMEM((he, rows), F32),
            pltpu.VMEM((hed, width), BF16), pltpu.VMEM((rows, width), BF16), pltpu.VMEM((rows, width), BF16),
        )
        ready("probs", "qu", "qv", "rel", "key_own", "part_k", "mem_k", "part_mem_k")
        ready("value_own", "part_v", "mem_v", "part_mem_v", "flip")
        odd = place[DEEP] % 2 == 1
        size = sizes.query_rows
        for h in range(heads):
            k_one = jnp.where(odd, part_k[h], part_mem_k[h])
            v_one = jnp.where(odd, part_v[h], part_mem_v[h])
            keys = (part_mem_k[h], mem_k[h], k_one, key_own[h])
            values = (part_mem_v[h], mem_v[h], v_one, value_own[h])
            bias_u = bias_v = None
            for base in range(0, rows, size):
                here = slice(base, base + size)
                turned = mm(flip[...], probs[h, here, :])
                ga = mm(r.ga[h, :, here], flip[...]).astype(BF16)
                queries_u = mm(qu[h, :, here], flip[...]).astype(BF16)
                queries_v = mm(qv[h, :, here], flip[...]).astype(BF16)
                gp = jnp.concatenate([mm(ga, v, TN) for v in values], axis=1)
                weighted = turned * gp
                delta = jnp.sum(weighted, axis=1, keepdims=True)
                gs = ((weighted - turned * delta) * sizes.scale).astype(BF16)
                gk = mm(queries_u, gs[:, 2 * rows:])
                gv = mm(ga, turned[:, 2 * rows:].astype(BF16))
                gqu = None
                for i, k in enumerate(keys):
                    part = mm(k, gs[:, i * rows:(i + 1) * rows], NT)
                    gqu = part if gqu is None else gqu + part
                gpos = pltpu.roll(gs, rows - size - base, 1, stride=1, stride_axis=0)
                gqv = mm(rel[h], gpos, NT)
                grel = mm(queries_v, gpos)
                r.gq[h * dh:(h + 1) * dh, here] = mm((gqu + gqv).astype(BF16), flip[...]).astype(BF16)
                ones = jnp.ones((8, size), F32)
                sum_u, sum_v = [
                    lax.dot_general(ones, g, NT, precision=lax.Precision.HIGHEST, preferred_element_type=F32)
                    for g in (gqu, gqv)
                ]
                if base == 0:
                    r.gk[h] = gk
                    r.gv[h] = gv
                    acc[...] = grel
                    bias_u, bias_v = sum_u, sum_v
                else:
                    r.gk[h] += gk
                    r.gv[h] += gv
                    acc[...] += grel
                    bias_u, bias_v = bias_u + sum_u, bias_v + sum_v
            r.grel[h * dh:(h + 1) * dh, :] = acc[...].astype(BF16)
            r.small[4 + h:5 + h, 0:dh] = bias_u[0:1]
            r.small[4 + heads + h:5 + heads + h, 0:dh] = bias_v[0:1]
        r.cross_out[0] = r.gk[:, :, :rows].astype(BF16)
        r.cross_out[1] = r.gv[:, :, :rows].astype(BF16)
        crossing.append(remote(r.cross_out, r.cross_in, sems, plan.cross, lambda: partner(near)))

    crossing, gm_swap = [], []
    hd_up = sizes.hd_up
    r.small[4:8, :] = jnp.zeros((4, width), F32)
    total_keys = 4 * rows
    chunk_shape = pltpu.VMEM((heads, dh, rows), BF16)
    pl.run_scoped(
        attention, pltpu.VMEM((heads, rows, total_keys), BF16), chunk_shape, chunk_shape,
        pltpu.VMEM((heads, dh, total_keys), BF16), *([chunk_shape] * 8),
        pltpu.VMEM((sizes.query_rows, sizes.query_rows), BF16), pltpu.VMEM((dh, total_keys), F32),
    )

    def rest(*held):
        b = types.SimpleNamespace(**dict(zip(sizes.late_names, held)))
        fetch_all(
            gated=b.gated, att_in=b.att_in, gate_o_in=b.gate_o_in, each=b.each, sigs=b.sigs, gates=b.gates, wv=b.wv,
            wq=b.wq, wk=b.wk, rt=b.rt, x=b.x, gain=b.gain, gates_in=b.gates_in, table=b.table,
        )
        up_a.acc, up_a.send, up_b.acc, up_b.send = b.acc_up_a, b.send_up_a, b.acc_up_b, b.send_up_b
        far = [v for v in bits if v != near]
        out = tree_of("xyf", far, b.acc_out, b.send_out, r.got_out, plan.out)
        value = tree_of("yxf", far, b.acc_value, b.send_value, r.got_value, plan.value)
        query = tree_of("xynf", bits, b.acc_query, b.send_query, r.got_query, plan.query)
        down = tree_of("ynf", bits, b.acc_down, b.send_down, r.got_down, plan.down)
        half_count = len(wide_bits) // 2
        down.order = down.order[:half_count] + wide_bits[1:half_count] + down.order[half_count:]
        near_rows = blocks // 2 * block
        half = sizes.hidden_units // 2
        small = r.small
        state = []

        def down_part(own):
            for number, run in enumerate(runs(down.fixed(own))):
                at_rows = rows_of(run)
                part = mm(r.cot_t[at_rows, 0:rows], r.act[...]) + mm(r.cot_t[at_rows, rows:], r.act_in[...])
                for k in range(per_share):
                    at = number * per_share + k
                    piece = part[k * block:(k + 1) * block]
                    if own:
                        down.acc[at] = piece.astype(BF16)
                    else:
                        down.send[at] = piece.astype(BF16)
            if own:
                down.step()
            else:
                down.launch(sems, partner)

        def run_rows(ref, run):
            count = per_share // 2
            return ref[pl.ds(pl.multiple_of(run * count, count), count)].reshape(share, rows)

        def up_a_keep():
            for number, run in enumerate(runs(up_a.fixed(True))):
                part = mm(run_rows(r.two_t, run), r.pre[0])
                for k in range(per_share):
                    up_a.acc[number * per_share + k] = part[k * block:(k + 1) * block].astype(BF16)
            up_a.step()

        def up_b_keep():
            part = mm(r.two_t[:, me[near]].reshape(near_rows, rows), r.pre[1])
            for at in range(blocks // 2):
                up_b.acc[at] = part[at * block:(at + 1) * block].astype(BF16)
            up_b.step()

        def out_part():
            ready("gated", "att_in", "gate_o_in")
            mine = mm(r.gm[...].reshape(near_rows, rows), b.gated[...], NT)
            for at in range(blocks // 2):
                out.acc[at] = mine[at * block:(at + 1) * block].astype(BF16)
            for h in range(heads):
                for e in range(experts):
                    at = h * experts + e
                    b.gated[at * dh:(at + 1) * dh, :] = (
                        b.gate_o_in[at:at + 1, :] * b.att_in[h].astype(F32)
                    ).astype(BF16)
            gm_swap[0].wait()
            theirs = mm(r.gm_in[...].reshape(near_rows, rows), b.gated[...], NT)
            for at in range(blocks // 2):
                out.acc[at] = (out.acc[at].astype(F32) + theirs[at * block:(at + 1) * block]).astype(BF16)
            out.advance(sems, partner)

        def own_part():
            ready("each", "sigs", "gates")
            crossing[0].wait()
            even = jnp.where(place[DEEP] % 2 == 0, 1.0, 0.0)
            for h in range(heads):
                gk = r.gk[h, :, rows:] + even * r.cross_in[0, h].astype(F32)
                gv = r.gv[h, :, rows:] + even * r.cross_in[1, h].astype(F32)
                b.own_out[h * dh:(h + 1) * dh, :] = gv.astype(BF16)
                b.own_out[hd + h * dh:hd + (h + 1) * dh, :] = gk.astype(BF16)
                for e in range(experts):
                    at = h * experts + e
                    gate = b.gates[at:at + 1, :]
                    grad_gate = jnp.sum(gv * b.each[at * dh:(at + 1) * dh, :].astype(F32), axis=0, keepdims=True)
                    r.logits[at:at + 1, :] = grad_gate * gate * (1.0 - b.sigs[at:at + 1, :])
                    b.grads[at * dh:(at + 1) * dh, :] = (gate * gv).astype(BF16)
            tail = b.own_out.shape[0] - 2 * hd
            logits = jnp.concatenate([r.logits[0:2 * he, :], jnp.zeros((tail - 2 * he, rows), F32)], axis=0)
            b.own_out[2 * hd:, :] = logits.astype(BF16)
            state_own.append(remote(b.own_out, r.own_in, sems, plan.own, partner(near)))
            b.grads[hed:, :] = b.own_out[hd:, :]

        def hidden_part():
            ready("wv", "wq", "wk", "rt")
            grad_hidden = mm(b.grads[0:hed, :], b.wv[...], TN)
            grad_hidden += mm(r.gq[...], b.wq[...], TN)
            grad_hidden += mm(b.grads[hed:hed + hd, :], b.wk[...], TN)
            grad_hidden += mm(b.grads[hed + hd:hed + hd + 2 * he, :], b.rt[...], TN)
            r.two_own[...] = grad_hidden.astype(BF16)
            state_head.append(remote(r.two_own, r.head_in, sems, plan.head, across))

        def norm_part():
            ready("x", "gain")
            state_head[0].wait()
            grad_hidden = r.two_own[...].astype(F32) + r.head_in[...].astype(F32)
            normed, inverse = normalize(b.x[...].astype(F32))
            small[0:1, :] = jnp.sum(grad_hidden * normed, axis=0, keepdims=True)
            small[1:2, :] = jnp.sum(grad_hidden, axis=0, keepdims=True)
            state.append(remote(small, r.small_in.at[0], sems, plan.small[0], partner(bits[0])))
            r.grad_mixed[...] += norm_back(grad_hidden * b.gain[...], normed, inverse)
            input_copy = pltpu.make_async_copy(r.grad_mixed, r.grad_input, r.load_sem.at[len(loaded) + 1])
            input_copy.start()
            state_input.append(input_copy)

        def small_step():
            at = len(state) - 1
            if at == len(bits):
                return
            state[at].wait()
            small[...] = small[...] + r.small_in[at]
            state.append(
                None if at + 1 == len(bits)
                else remote(small, r.small_in.at[at + 1], sems, plan.small[at + 1], partner(bits[at + 1]))
            )

        def value_own():
            ready("hid")
            mine = mm(r.hid[:, me[near]].reshape(near_rows, rows), b.grads[...], NT)
            for at in range(blocks // 2):
                value.acc[at] = mine[at * block:(at + 1) * block]

        def value_part():
            ready("hid_in", "gates_in")
            state_own[0].wait()
            for at in range(he):
                h = at // experts
                b.grads[at * dh:(at + 1) * dh, :] = (
                    b.gates_in[at:at + 1, :] * r.own_in[h * dh:(h + 1) * dh, :].astype(F32)
                ).astype(BF16)
            b.grads[hed:, :] = r.own_in[hd:, :]
            theirs = mm(r.hid_in[...].reshape(near_rows, rows), b.grads[...], NT)
            for at in range(blocks // 2):
                value.acc[at] += theirs[at * block:(at + 1) * block]
            value.advance(sems, partner)

        def query_part(own):
            if not own and hd_up > hd:
                for at in range(blocks // 2):
                    query.send[at, :, hd:hd_up] = jnp.zeros((block, hd_up - hd), BF16)
                    query.acc[at, :, hd:hd_up] = jnp.zeros((block, hd_up - hd), BF16)
            ready("hid", "table")
            for number, run in enumerate(runs(query.fixed(own))):
                part = mm(run_rows(r.hid, run), r.gq[...], NT)
                part_rel = mm(b.table[rows_of(run), :], r.grel[...], NT)
                for k in range(per_share):
                    at = number * per_share + k
                    piece, piece_rel = part[k * block:(k + 1) * block], part_rel[k * block:(k + 1) * block]
                    if own:
                        query.acc[at, :, 0:hd] = piece.astype(BF16)
                        query.acc[at, :, hd_up:] = piece_rel.astype(BF16)
                    else:
                        query.send[at, :, 0:hd] = piece.astype(BF16)
                        query.send[at, :, hd_up:] = piece_rel.astype(BF16)
            if own:
                query.step()
            else:
                query.launch(sems, partner)

        state_own, state_head, state_input = [], [], []
        keep, leave = me[x_bit], 1 - me[x_bit]

        def half_part():
            down.arrive()
            r.half_out[...] = down.finish(leave).astype(BF16)
            state_own.append(remote(r.half_out, r.half_in, sems, plan.half, partner(x_bit)))
            r.g_down[:, pl.ds(pl.multiple_of(keep * half, half), half)] = down.finish(keep)

        def next_level(tree):
            if tree.level < len(tree.order):
                tree.advance(sems, partner)

        ready("two_t", "pre")
        up_b_keep()
        ready("act", "cot_t")
        act_swap.wait()
        down_part(False)
        up_a_keep()
        next_level(up_a)
        out_part()
        next_level(up_a)
        own_part()
        next_level(up_b)
        down_part(True)
        hidden_part()
        norm_part()
        next_level(down)
        next_level(up_a)
        next_level(out)
        next_level(up_b)
        value_own()
        value_part()
        next_level(up_b)
        query_part(False)
        query_part(True)
        next_level(out)
        next_level(down)
        next_level(value)
        next_level(query)
        small_step()
        small_step()
        next_level(query)
        small_step()
        next_level(value)
        next_level(query)
        while any(tree.level < len(tree.order) for tree in (up_a, up_b, out, query, value, down)):
            for tree in (up_a, up_b, out, query, value, down):
                next_level(tree)
        half_part()
        while len(state) <= len(bits):
            small_step()
        r.small_out[...] = small[...]
        for number, tree in enumerate((up_a, up_b)):
            tree.arrive()
            r.g_up[:, number * half:(number + 1) * half] = tree.finish()
        out.arrive()
        total = out.finish()
        for at in range(he):
            r.g_out[at] = total[:, at * dh:(at + 1) * dh]
        value.arrive()
        total = value.finish()
        for at in range(he):
            r.g_value[at] = total[:, at * dh:(at + 1) * dh]
        for h in range(heads):
            r.g_key[:, h, :] = total[:, hed + h * dh:hed + (h + 1) * dh]
        r.g_router[...] = total[:, hed + hd:hed + hd + 2 * he]
        query.arrive()
        total = query.finish()
        for h in range(heads):
            r.g_query[:, h, :] = total[:, h * dh:(h + 1) * dh]
            r.g_rel[:, h, :] = total[:, hd_up + h * dh:hd_up + (h + 1) * dh]
        state_own[1].wait()
        r.g_down[:, pl.ds(pl.multiple_of(leave * half, half), half)] = r.half_in[...].astype(F32)
        state_input[0].wait()

    pl.run_scoped(rest, *sizes.late_scratch)


def late_call(inputs, sizes):
    wide_bits, deep_bits = bit_names(sizes.wide, sizes.deep)
    bits = len(wide_bits) + len(deep_bits)
    blocks = sizes.wide * sizes.deep
    block, rows, width, heads, dh = sizes.block, sizes.rows, sizes.width, sizes.heads, sizes.dh
    he, hd = heads * sizes.experts, heads * dh
    hed, half = he * dh, sizes.hidden_units // 2
    tail = 32
    sizes.hd_up = -(-hd // 128) * 128
    sizes.value_n = hed + hd + tail
    query_n = sizes.hd_up + hd
    count = 10 + 7 * bits
    slots = iter(range(count))

    def levels():
        return [next(slots) for _ in range(bits)]

    plan = types.SimpleNamespace(
        two=next(slots), ffn=next(slots), act=next(slots), gm=next(slots), cross=next(slots),
        own=next(slots), head=next(slots), half=next(slots), small=levels(), up_a=levels(), up_b=levels(),
        out=levels(), query=levels(), down=levels(), value=levels(),
    )

    def got(n, start, stop):
        return [pltpu.VMEM((blocks >> (level + 1), block, n), BF16) for level in range(start, stop)]

    def taken(name):
        return pltpu.VMEM(inputs[name].shape, inputs[name].dtype)

    sem = pltpu.SemaphoreType.DMA
    token_rows = pltpu.VMEM((rows, width), BF16)
    scratch = dict(
        act=pltpu.VMEM((rows, half), BF16), hid=taken("hid"), two_t=taken("two_t"), pre=taken("pre"),
        cot_t=taken("cot_t"), two_own=token_rows, two_in=token_rows, ffn_in=token_rows, head_in=token_rows,
        act_in=pltpu.VMEM((rows, half), BF16), hid_in=taken("hid_in"), gm=taken("hid_in"), gm_in=taken("hid_in"),
        gm_out=taken("hid_in"), grad_mixed=pltpu.VMEM((rows, width), F32),
        small=pltpu.VMEM((8, width), F32), small_in=pltpu.VMEM((bits, 8, width), F32),
        logits=pltpu.VMEM((2 * he, rows), F32), ga=pltpu.VMEM((heads, dh, rows), BF16),
        gq=pltpu.VMEM((hd, rows), BF16), gk=pltpu.VMEM((heads, dh, 2 * rows), F32),
        gv=pltpu.VMEM((heads, dh, 2 * rows), F32), grel=pltpu.VMEM((hd, 4 * rows), BF16),
        cross_out=pltpu.VMEM((2, heads, dh, rows), BF16), cross_in=pltpu.VMEM((2, heads, dh, rows), BF16),
        own_in=pltpu.VMEM((2 * hd + tail, rows), BF16), half_in=pltpu.VMEM((block, half), BF16),
        half_out=pltpu.VMEM((block, half), BF16),
        got_up_a=got(half, 0, bits), got_up_b=got(half, 0, bits), got_out=got(hed, 1, bits),
        got_query=got(query_n, 0, bits), got_down=got(half, 0, bits - 1), got_value=got(sizes.value_n, 1, bits),
        load_sem=sem((len(inputs) + 3,)), send_sem=sem((count,)), recv_sem=sem((count,)),
    )
    late = dict(
        gated=taken("gated"), att_in=taken("att_in"), gate_o_in=taken("gate_o_in"), gates_in=taken("gates_in"),
        send_out=pltpu.VMEM((blocks >> 2, block, hed), BF16), acc_out=pltpu.VMEM((blocks >> 1, block, hed), BF16),
        table=taken("table"), each=taken("each"), sigs=taken("sigs"), gates=taken("gates"), wv=taken("wv"),
        wq=taken("wq"), wk=taken("wk"), rt=taken("rt"), x=taken("x"), gain=taken("gain"),
        own_out=pltpu.VMEM((2 * hd + tail, rows), BF16), grads=pltpu.VMEM((sizes.value_n, rows), BF16),
        send_up_a=pltpu.VMEM((blocks >> 2, block, half), BF16), send_up_b=pltpu.VMEM((blocks >> 2, block, half), BF16),
        acc_up_a=pltpu.VMEM((blocks >> 1, block, half), BF16), acc_up_b=pltpu.VMEM((blocks >> 1, block, half), BF16),
        send_query=pltpu.VMEM((blocks >> 1, block, query_n), BF16),
        acc_query=pltpu.VMEM((blocks >> 1, block, query_n), BF16),
        send_down=pltpu.VMEM((blocks >> 1, block, half), BF16), acc_down=pltpu.VMEM((blocks >> 1, block, half), BF16),
        send_value=pltpu.VMEM((blocks >> 2, block, sizes.value_n), BF16),
        acc_value=pltpu.VMEM((blocks >> 1, block, sizes.value_n), F32),
    )
    sizes.late_names, sizes.late_scratch = list(late), list(late.values())
    outs = dict(
        g_down=((block, 2 * half), F32), g_up=((block, 2 * half), F32), g_out=((he, block, dh), F32),
        g_value=((he, block, dh), F32), g_query=((block, heads, dh), F32), g_key=((block, heads, dh), F32),
        g_rel=((block, heads, dh), F32), g_router=((block, 2 * he), F32), small_out=((8, width), F32),
        grad_input=((rows, width), F32), output=((rows, width), BF16),
    )
    flat, tree = jax.tree.flatten(list(scratch.values()))

    def kernel(*refs):
        held = jax.tree.unflatten(tree, refs[len(inputs) + len(outs):])
        late_kernel(
            *refs[:len(inputs) + len(outs)], *held, names=[None] * 0 + [n + "_" for n in inputs] + list(outs) + list(scratch),
            loaded=list(inputs), sizes=sizes, plan=plan,
        )

    vmem, anywhere = pl.BlockSpec(memory_space=pltpu.VMEM), pl.BlockSpec(memory_space=pl.ANY)
    results = pl.pallas_call(
        kernel,
        in_specs=[anywhere] * len(inputs),
        out_specs=[vmem] * (len(outs) - 2) + [anywhere] * 2,
        out_shape=[jax.ShapeDtypeStruct(shape, dtype) for shape, dtype in outs.values()],
        scratch_shapes=flat,
        compiler_params=pltpu.CompilerParams(collective_id=0, has_side_effects=True, vmem_limit_bytes=60 << 20),
        cost_estimate=pl.CostEstimate(flops=4 * 10**10, bytes_accessed=10**8, transcendentals=0),
    )(*inputs.values())
    return types.SimpleNamespace(**dict(zip(outs, results)))


def body(
    layer_input, mem_keys, mem_values, route_value, route_output, ln1_gain, ln1_bias, w_query, w_key, w_rel,
    content_bias, position_bias, w_value, w_out, router_value, router_output, ln2_gain, ln2_bias, w_up, w_down,
    cotangent,
):
    rows, width = layer_input.shape
    heads, dh = content_bias.shape
    experts = w_value.shape[1]
    odd = (lax.axis_index("dp") % 2).astype(jnp.int32)
    scale = 1.0 / math.sqrt(dh)
    total_keys = 4 * rows
    block = rows // 2
    hd = heads * dh
    hed = heads * experts * dh

    wq = jnp.transpose(w_query, (1, 2, 0)).reshape(hd, width)
    wk = jnp.transpose(w_key, (1, 2, 0)).reshape(hd, width)
    wr = jnp.transpose(w_rel, (1, 2, 0)).reshape(hd, width)
    wv = jnp.transpose(w_value, (0, 1, 3, 2)).reshape(hed, width)
    wo = w_out.reshape(hed, width)
    rt = jnp.concatenate(
        [jnp.transpose(r, (1, 2, 0)).reshape(heads * experts, width) for r in (router_value, router_output)], axis=0
    )
    mem_k = jnp.transpose(mem_keys, (1, 2, 0))
    mem_v = jnp.transpose(mem_values, (1, 2, 0))
    rv = jnp.transpose(route_value, (0, 2, 1))
    ro = jnp.transpose(route_output, (0, 2, 1))
    rt = jnp.concatenate(
        [jnp.transpose(r, (1, 2, 0)).reshape(heads * experts, width) for r in (router_value, router_output)], axis=0
    )
    table = jnp.asarray(position_table(total_keys, width))
    first = early_call(dict(
        x=layer_input, gain=ln1_gain.reshape(1, width), bias=ln1_bias.reshape(1, width), wk=wk, rt=rt, rv=rv, ro=ro,
        wv=wv, wq=wq, cb=content_bias, pb=position_bias, wr=wr, table=table, mem_k=mem_k, mem_v=mem_v, cot=cotangent,
    ), types.SimpleNamespace(
        heads=heads, experts=experts, dh=dh, rows=rows, width=width, wide=lax.axis_size(WIDE),
        deep=lax.axis_size(DEEP), scale=scale, query_rows=block,
    ))
    att, gate_v, gate_o, sig_v, sig_o, hid = first.att, first.gate_v, first.gate_o, first.sig_v, first.sig_o, first.hid
    wide_count, depth = lax.axis_size(WIDE), lax.axis_size(DEEP)
    blocks = wide_count * depth
    block_rows, he = width // blocks, heads * experts
    hidden_units = w_up.shape[1]
    wide_bits, deep_bits = bit_names(wide_count, depth)
    gain_two, bias_two = ln2_gain.reshape(1, width), ln2_bias.reshape(1, width)
    sem = pltpu.SemaphoreType.DMA

    def shapes(*pairs):
        return [jax.ShapeDtypeStruct(shape, dtype) for shape, dtype in pairs]

    half = (2, rows, hidden_units // 2)
    first_half = (blocks // 2, block_rows, hidden_units // 2)
    (mixed, gated, act, pre, two_t, cot_t, up_a, up_b, two_out, ffn_out, hid_in, att_in, gate_o_in,
     gates_in) = pl.pallas_call(
        functools.partial(
            feed_kernel, heads=heads, experts=experts, dh=dh, wide_bits=wide_bits, share=width // wide_count,
            block=block_rows,
        ),
        out_shape=shapes(
            ((rows, width), F32), ((hed, rows), BF16), (half, BF16), (half, BF16), (hid.shape, BF16),
            ((width, 2 * rows), BF16), (first_half, BF16), (first_half, BF16), ((rows, width), BF16),
            ((rows, width), BF16), ((blocks // 2, block_rows, rows), BF16), (att.shape, BF16), (gate_o.shape, F32),
            (gate_v.shape, F32),
        ),
        scratch_shapes=[pltpu.VMEM((rows, width), BF16)] * 3 + [pltpu.VMEM((rows // 2, width), BF16), sem((6,)), sem((6,))],
        compiler_params=pltpu.CompilerParams(collective_id=1, has_side_effects=True, vmem_limit_bytes=56 << 20),
        cost_estimate=pl.CostEstimate(flops=2 * 10**10, bytes_accessed=3 * 10**7, transcendentals=10**6),
    )(att, gate_o, gate_v, hid, layer_input, cotangent, first.cot_in, wo, gain_two, bias_two, w_up, w_down)

    flip = jnp.asarray(np.eye(block // 2, dtype=np.float32)[::-1].astype(BF16))
    inputs = dict(
        two_out=two_out, ffn_out=ffn_out, act=act, up_a=up_a, up_b=up_b, hid=hid, hid_in=hid_in, gates=gate_v,
        gates_in=gates_in, gate_o_in=gate_o_in, att_in=att_in, mixed=mixed,
        cot=cotangent, gain_two=gain_two, att=att, gate_o=gate_o, sig_o=sig_o, wo=wo, gated=gated,
        flip=flip, probs=first.probs, qu=first.qu, qv=first.qv, rel=first.rel,
        key_own=first.key_own, part_k=first.part_k, mem_k=mem_k, part_mem_k=first.part_mem_k,
        value_own=first.value_own, part_v=first.part_v, mem_v=mem_v, part_mem_v=first.part_mem_v,
        table=table, two_t=two_t, pre=pre, cot_t=cot_t, sigs=sig_v, each=first.each, wv=wv, wq=wq, wk=wk, rt=rt,
        x=layer_input, gain=ln1_gain.reshape(1, width),
    )
    done = late_call(inputs, types.SimpleNamespace(
        heads=heads, experts=experts, dh=dh, rows=rows, width=width, wide=wide_count, deep=depth, block=block_rows,
        hidden_units=hidden_units, scale=scale, query_rows=block // 2,
    ))
    start = (lax.axis_index(WIDE) * depth + lax.axis_index(DEEP)) * block_rows
    ln = lax.dynamic_slice_in_dim(done.small_out, start, block_rows, axis=1)
    biases = done.small_out[4:, :dh].reshape(2, heads, dh)
    routers = done.g_router.reshape(block_rows, 2, heads, experts)

    output, grad_input, g_query, g_key, g_rel, g_value, g_out, g_up, g_down = finished(
        done.output, done.grad_input, done.g_query, done.g_key, done.g_rel, done.g_value, done.g_out, done.g_up,
        done.g_down,
    )

    def by_expert(values):
        return values.reshape(heads, experts, block_rows, dh)

    return (
        output, grad_input, ln[0], ln[1], g_query, g_key, g_rel, biases[0], biases[1],
        by_expert(g_value), jnp.transpose(by_expert(g_out), (0, 1, 3, 2)), routers[:, 0], routers[:, 1],
        ln[2], ln[3], g_up, jnp.transpose(g_down),
    )


def solution(mesh):
    tokens = ("wide", "dp")
    return jax.shard_map(
        body,
        mesh=mesh,
        in_specs=(
            P(tokens, None), P(tokens, "head", None), P(tokens, "head", None), P("head", tokens, None),
            P("head", tokens, None), P(), P(), P(None, "head", None), P(None, "head", None), P(None, "head", None),
            P("head", None), P("head", None), P("head", None, None, None), P("head", None, None, None),
            P(None, "head", None), P(None, "head", None), P(), P(), P(None, "head"), P("head", None), P(tokens, None),
        ),
        out_specs=(
            P(tokens, None), P(tokens, None), P(tokens), P(tokens), P(tokens, "head", None), P(tokens, "head", None),
            P(tokens, "head", None), P("head", None), P("head", None), P("head", None, tokens, None),
            P("head", None, None, tokens), P(tokens, "head", None), P(tokens, "head", None), P(tokens), P(tokens),
            P(tokens, "head"), P("head", tokens),
        ),
        check_vma=False,
    )
```

```python
import functools
import math
import types

import jax
import jax.numpy as jnp
import numpy as np
from jax import lax
from jax.experimental import pallas as pl
from jax.experimental.pallas import tpu as pltpu
from jax.sharding import PartitionSpec as P

EPSILON = 1e-05
NEG_LARGE = -1e30
F32 = jnp.float32
BF16 = jnp.bfloat16
WIDE, DEEP = "wide", "dp"

NN = (((1,), (0,)), ((), ()))
NT = (((1,), (1,)), ((), ()))
TN = (((0,), (0,)), ((), ()))


def mm(a, b, dims=NN):
    return lax.dot_general(a, b, dims, preferred_element_type=F32)


def normalize(values):
    row_mean = jnp.mean(values, axis=-1, keepdims=True)
    centered = values - row_mean
    variance = jnp.mean(centered * centered, axis=-1, keepdims=True)
    inverse = lax.rsqrt(variance + EPSILON)
    return (centered * inverse, inverse)


def norm_back(grad_normed, normed, inverse):
    first_mean = jnp.mean(grad_normed, axis=-1, keepdims=True)
    second_mean = jnp.mean(grad_normed * normed, axis=-1, keepdims=True)
    return inverse * (grad_normed - first_mean - normed * second_mean)


def position_table(extent, model_width):
    half_width = model_width // 2
    frequencies = np.exp(
        np.arange(half_width, dtype=np.float32) * np.float32(-2.0 * math.log(10000.0) / model_width)
    ).astype(np.float32)
    distance = np.arange(extent - 1, -1, -1).astype(np.float32)
    angles = (frequencies[:, None] * distance[None, :]).astype(np.float64)
    return np.concatenate([np.sin(angles), np.cos(angles)], axis=0).astype(np.float32).astype(BF16)


def whole(array):
    return pl.BlockSpec(array.shape, lambda *_: (0,) * len(array.shape))


def gelu_both(x):
    c = math.sqrt(2.0 / math.pi)
    square = x * x
    t = jnp.tanh(c * x * (1.0 + 0.044715 * square))
    half = 0.5 * (1.0 + t)
    return x * half, half + 0.5 * x * (1.0 - t * t) * (c * (1.0 + 3.0 * 0.044715 * square))


def meet(*devices):
    barrier = pltpu.get_barrier_semaphore()
    for device in devices:
        pl.semaphore_signal(barrier, inc=1, device_id=device, device_id_type=pl.DeviceIdType.MESH)
    pl.semaphore_wait(barrier, len(devices))


def other_core():
    return (1 - lax.axis_index("head"), lax.axis_index("wide"), lax.axis_index("dp"))


class Swap:
    def __init__(self, src, dst, sems, slot, device):
        self.parts = (src, dst, sems, slot, device)
        self.copy().start()

    def copy(self):
        src, dst, sems, slot, device = self.parts
        return pltpu.make_async_remote_copy(
            src_ref=src, dst_ref=dst, send_sem=sems[0].at[slot], recv_sem=sems[1].at[slot],
            device_id=device() if callable(device) else device, device_id_type=pl.DeviceIdType.MESH,
        )

    def wait(self):
        self.copy().wait()


remote = Swap


def early_kernel(*refs, given_names, out_names, held_names, sizes):
    count = len(given_names)
    given = types.SimpleNamespace(**dict(zip(given_names, refs)))
    out = types.SimpleNamespace(**dict(zip(out_names, refs[count:])))
    r = types.SimpleNamespace(**dict(zip(held_names, refs[count + len(out_names):])))
    heads, experts, dh, rows, width = sizes.heads, sizes.experts, sizes.dh, sizes.rows, sizes.width
    deep, wide = lax.axis_index(DEEP), lax.axis_index(WIDE)
    near = deep % 2
    beside = (lax.axis_index("head"), wide, deep + 1 - 2 * near)
    across = (lax.axis_index("head"), wide + 1 - 2 * (wide % 2), deep)
    sems = (r.send_sem, r.recv_sem)
    loads, writes = {}, []

    def fetch(*names):
        for name in names:
            slot = given_names.index(name)
            loads[name] = pltpu.make_async_copy(getattr(given, name), getattr(r, name), r.load_sem.at[slot])
            loads[name].start()

    def ready(*names):
        for name in names:
            loads[name].wait()

    def put(name, source, *at):
        target = getattr(out, name)
        if at:
            source, target = source.at[at], target.at[at]
        writes.append(pltpu.make_async_copy(source, target, r.write_sem.at[len(writes)]))
        writes[-1].start()

    fetch(*sizes.loaded)
    meet(beside, across)
    part = rows // 2
    swaps = [
        Swap(given.mem_k, r.part_mem_k, sems, 0, beside), Swap(given.mem_v, r.part_mem_v, sems, 1, beside),
        Swap(given.cot.at[pl.ds(0, part)], out.cot_in, sems, 2, across),
    ]
    ready("x", "gain", "bias")
    normed, _ = normalize(r.x[...].astype(F32))
    hid = (normed * r.gain[...] + r.bias[...]).astype(BF16)
    r.hid[...] = hid
    ready("wk")
    for h in range(heads):
        r.key_own[h] = mm(r.wk[h * dh:(h + 1) * dh, :], r.hid[...], NT).astype(BF16)
    swaps.append(Swap(r.key_own, r.part_k, sems, 3, beside))
    ready("rt", "rv", "ro")
    logits = mm(r.rt[...], r.hid[...], NT)
    sig = 1.0 / (1.0 + jnp.exp(-logits))
    masks = []
    for routes in (r.rv, r.ro):
        for h in range(heads):
            for e in range(experts):
                hit = (routes[h, 0:1, :] == e) | (routes[h, 1:2, :] == e)
                masks.append(jnp.where(hit, 1.0, 0.0))
    gate = sig * jnp.concatenate(masks, axis=0)
    he = heads * experts
    r.gate[...] = gate
    out.gate_v[...] = gate[:he]
    out.gate_o[...] = gate[he:]
    out.sig_v[...] = sig[:he]
    out.sig_o[...] = sig[he:]
    ready("wv")
    for h in range(heads):
        total = None
        for e in range(experts):
            at = h * experts + e
            each = mm(r.wv[at * dh:(at + 1) * dh, :], r.hid[...], NT)
            r.each[at * dh:(at + 1) * dh, :] = each.astype(BF16)
            term = r.gate[at:at + 1, :] * each
            total = term if total is None else total + term
        r.value_own[h] = total.astype(BF16)
    swaps.append(Swap(r.value_own, r.part_v, sems, 4, beside))
    put("each", r.each)
    put("key_own", r.key_own)
    put("value_own", r.value_own)
    ready("wq", "cb", "pb")
    eye = (
        lax.broadcasted_iota(jnp.int32, (dh, dh), 0) == lax.broadcasted_iota(jnp.int32, (dh, dh), 1)
    ).astype(F32)

    def column(row):
        spread = jnp.broadcast_to(row, (8, dh))
        return lax.dot_general(
            eye, spread, NT, precision=lax.Precision.HIGHEST, preferred_element_type=F32
        )[:, 0:1]

    for h in range(heads):
        queries = mm(r.wq[h * dh:(h + 1) * dh, :], r.hid[...], NT)
        r.qu[h] = (queries + column(r.cb[h:h + 1, :])).astype(BF16)
        r.qv[h] = (queries + column(r.pb[h:h + 1, :])).astype(BF16)
    put("qu", r.qu)
    put("qv", r.qv)
    ready("wr", "table")
    for h in range(heads):
        r.rel[h] = mm(r.wr[h * dh:(h + 1) * dh, :], r.table[...]).astype(BF16)
    put("rel", r.rel)
    r.hid_t[...] = r.hid[...].T.reshape(r.hid_t.shape)
    put("hid", r.hid_t)
    total_keys, size = 4 * rows, sizes.query_rows
    for h in range(heads):
        for base in range(0, rows, size):
            here = slice(base, base + size)
            positional = mm(r.qv[h, :, here], r.rel[h], TN)
            r.scores[h, here, :] = pltpu.roll(
                positional, total_keys - rows + 1 + base, 1, stride=1, stride_axis=0
            )
    odd = near == 1
    ready("mem_k", "mem_v")
    for swap in swaps[:2] + swaps[3:]:
        swap.wait()
    put("part_k", r.part_k)
    put("part_v", r.part_v)
    put("part_mem_k", r.part_mem_k)
    put("part_mem_v", r.part_mem_v)
    first = jnp.where(odd, 0, rows)
    for h in range(heads):
        k_one = jnp.where(odd, r.part_k[h], r.part_mem_k[h])
        v_one = jnp.where(odd, r.part_v[h], r.part_mem_v[h])
        keys = (r.part_mem_k[h], r.mem_k[h], k_one, r.key_own[h])
        values = (r.part_mem_v[h], r.mem_v[h], v_one, r.value_own[h])
        for base in range(0, rows, size):
            here = slice(base, base + size)
            content = jnp.concatenate([mm(r.qu[h, :, here], k, TN) for k in keys], axis=1)
            row = lax.broadcasted_iota(jnp.int32, (size, total_keys), 0) + base
            col = lax.broadcasted_iota(jnp.int32, (size, total_keys), 1)
            visible = (col <= row + (total_keys - rows)) & (col >= first)
            scores = jnp.where(visible, (content + r.scores[h, here, :]) * sizes.scale, NEG_LARGE)
            peak = jnp.max(scores, axis=1, keepdims=True)
            exponents = jnp.exp(scores - peak)
            total = jnp.sum(exponents, axis=1, keepdims=True)
            probs = (exponents * (1.0 / total)).astype(BF16)
            r.probs[h, here, :] = probs
            put("probs", r.probs, h, pl.ds(base, size))
            att = None
            for i, v in enumerate(values):
                term = mm(v, probs[:, i * rows:(i + 1) * rows], NT)
                att = term if att is None else att + term
            out.att[h, :, here] = att.astype(BF16)
    swaps[2].wait()
    for write in writes:
        write.wait()


def early_call(inputs, sizes):
    heads, experts, dh, rows, width = sizes.heads, sizes.experts, sizes.dh, sizes.rows, sizes.width
    he, hed, hd = heads * experts, heads * experts * dh, heads * dh
    tokens = (heads, dh, rows)
    blocks = sizes.wide * sizes.deep
    hid_shape = (blocks // 2, 2, width // blocks, rows)
    anywhere = dict(
        each=((hed, rows), BF16), key_own=(tokens, BF16), value_own=(tokens, BF16), qu=(tokens, BF16),
        qv=(tokens, BF16), rel=((heads, dh, 4 * rows), BF16), hid=(hid_shape, BF16), part_k=(tokens, BF16),
        part_v=(tokens, BF16), part_mem_k=(tokens, BF16), part_mem_v=(tokens, BF16),
        probs=((heads, rows, 4 * rows), BF16), cot_in=((rows // 2, width), BF16),
    )
    near = dict(
        att=(tokens, BF16), gate_v=((he, rows), F32), gate_o=((he, rows), F32), sig_v=((he, rows), F32),
        sig_o=((he, rows), F32),
    )
    outs = {**anywhere, **near}
    sem = pltpu.SemaphoreType.DMA
    sizes.loaded = [name for name in inputs if name != "cot"]
    held = {name: pltpu.VMEM(inputs[name].shape, inputs[name].dtype) for name in sizes.loaded}
    held.update({name: pltpu.VMEM(shape, dtype) for name, (shape, dtype) in anywhere.items() if name != "cot_in"})
    held.update(
        hid=pltpu.VMEM((rows, width), BF16), hid_t=pltpu.VMEM(hid_shape, BF16),
        scores=pltpu.VMEM((heads, rows, 4 * rows), F32), gate=pltpu.VMEM((2 * he, rows), F32),
        load_sem=sem((len(inputs),)), write_sem=sem((24,)), send_sem=sem((5,)), recv_sem=sem((5,)),
    )
    vmem, hbm = pl.BlockSpec(memory_space=pltpu.VMEM), pl.BlockSpec(memory_space=pl.ANY)
    results = pl.pallas_call(
        functools.partial(
            early_kernel, given_names=list(inputs), out_names=list(outs), held_names=list(held), sizes=sizes
        ),
        in_specs=[hbm] * len(inputs),
        out_specs=[hbm] * len(anywhere) + [vmem] * len(near),
        out_shape=[jax.ShapeDtypeStruct(shape, dtype) for shape, dtype in outs.values()],
        scratch_shapes=list(held.values()),
        compiler_params=pltpu.CompilerParams(collective_id=2, has_side_effects=True, vmem_limit_bytes=58 << 20),
        cost_estimate=pl.CostEstimate(flops=2 * 10**10, bytes_accessed=3 * 10**7, transcendentals=2 * 10**6),
    )(*inputs.values())
    return types.SimpleNamespace(**dict(zip(outs, results)))


def finish_kernel(*refs):
    load_sem, write_sem = refs[-2:]
    count = (len(refs) - 2) // 3
    given, outs, held = refs[:count], refs[count:2 * count], refs[2 * count:3 * count]
    loads = [pltpu.make_async_copy(given[i], held[i], load_sem.at[i]) for i in range(count)]
    writes = [pltpu.make_async_copy(held[i], outs[i], write_sem.at[i]) for i in range(count)]
    for copy in loads:
        copy.start()
    for load, write in zip(loads, writes):
        load.wait()
        write.start()
    for write in writes:
        write.wait()


def finished(*arrays):
    hbm = pl.BlockSpec(memory_space=pl.ANY)
    return pl.pallas_call(
        finish_kernel,
        in_specs=[hbm] * len(arrays),
        out_specs=[hbm] * len(arrays),
        out_shape=[jax.ShapeDtypeStruct(a.shape, a.dtype) for a in arrays],
        scratch_shapes=[pltpu.VMEM(a.shape, a.dtype) for a in arrays] + [pltpu.SemaphoreType.DMA((len(arrays),))] * 2,
        compiler_params=pltpu.CompilerParams(vmem_limit_bytes=60 << 20),
        cost_estimate=pl.CostEstimate(flops=0, bytes_accessed=10**7, transcendentals=0),
    )(*arrays)


def bit_names(wide_count, depth):
    wide_bits = [(WIDE, b) for b in range(int(math.log2(wide_count)))]
    deep_bits = [(DEEP, b) for b in range(int(math.log2(depth)))]
    return wide_bits, deep_bits


def bit_order(axes, wide_bits, deep_bits):
    half = len(wide_bits) // 2
    groups = dict(x=wide_bits[:half], y=wide_bits[half:], n=deep_bits[:1], f=deep_bits[1:])
    return [bit for axis in axes for bit in groups[axis]]


def natural(bits):
    return [b for b in sorted(bits, key=lambda b: (b[0] == WIDE, b[1]), reverse=True)]


def picks(left, fixed):
    free = [b for b in left if b not in fixed]
    found = []
    for number in range(1 << len(free)):
        index = 0
        for place, b in enumerate(left):
            if b in fixed:
                digit = fixed[b]
            else:
                digit = (number >> (len(free) - 1 - free.index(b))) & 1
            index = index + digit * (1 << (len(left) - 1 - place))
        found.append(index)
    return found


class Tree:
    def __init__(self, order, left, acc, send, got, slots, me):
        self.order, self.left, self.acc, self.send, self.got, self.slots, self.me = order, left, acc, send, got, slots, me
        self.level = 0
        self.copies = {}

    def fixed(self, own):
        bit = self.order[self.level]
        return {bit: self.me[bit] if own else 1 - self.me[bit]}

    def launch(self, sems, partner, src=None):
        got = self.got[self.level]
        src = self.send.at[pl.ds(0, got.shape[0])] if src is None else src
        bit = self.order[self.level]
        self.copies[self.level] = remote(src, got, sems, self.slots[self.level], lambda: partner(bit))

    def step(self):
        self.left = [b for b in self.left if b != self.order[self.level]]
        self.level += 1

    def arrive(self):
        self.copies[self.level - 1].wait()
        return self.got[self.level - 1]

    def advance(self, sems, partner):
        got = self.arrive() if self.level else None

        def piece(index):
            mine = self.acc[index].astype(F32)
            return mine if got is None else mine + got[index].astype(F32)

        for place, index in enumerate(picks(self.left, self.fixed(False))):
            self.send[place] = piece(index).astype(BF16)
        self.launch(sems, partner)
        for place, index in enumerate(picks(self.left, self.fixed(True))):
            self.acc[place] = piece(index).astype(self.acc.dtype)
        self.step()

    def finish(self, index=0):
        return self.acc[index].astype(F32) + self.got[self.level - 1][index].astype(F32)


def late_kernel(*refs, names, loaded, sizes, plan):
    r = types.SimpleNamespace(**dict(zip(names, refs)))
    given = types.SimpleNamespace(**dict(zip(loaded, refs)))
    heads, experts, dh, rows, width = sizes.heads, sizes.experts, sizes.dh, sizes.rows, sizes.width
    wide_count, depth, block = sizes.wide, sizes.deep, sizes.block
    hd, he, hed = heads * dh, heads * experts, heads * experts * dh
    blocks = wide_count * depth
    wide_bits, deep_bits = bit_names(wide_count, depth)
    bits = wide_bits + deep_bits
    place = {WIDE: lax.axis_index(WIDE), DEEP: lax.axis_index(DEEP)}
    head = lax.axis_index("head")
    me = {b: (place[b[0]] // (1 << b[1])) % 2 for b in bits}
    x_bit, near = wide_bits[0], deep_bits[0]

    def partner(bit):
        axis, number = bit
        other = place[axis] + (1 - 2 * me[bit]) * (1 << number)
        return (head, other, place[DEEP]) if axis == WIDE else (head, place[WIDE], other)

    across = other_core()
    sems = (r.send_sem, r.recv_sem)
    loads = {}

    def fetch(target, name, slot):
        loads[name] = pltpu.make_async_copy(getattr(given, name), target, r.load_sem.at[slot])
        loads[name].start()

    order = {name: number for number, name in enumerate(loaded)}

    def fetch_all(**targets):
        for name, target in targets.items():
            fetch(target, name, order[name])

    def ready(*wanted):
        for name in wanted:
            if loads.get(name) is not None:
                loads[name].wait()
                loads[name] = None

    def tree_of(axes, left, acc, send, got, slots):
        return Tree(bit_order(axes, wide_bits, deep_bits), natural(left), acc, send, got, slots, me)

    up_a = tree_of("yxnf", bits, None, None, r.got_up_a, plan.up_a)
    up_b = tree_of("nxyf", bits, None, None, r.got_up_b, plan.up_b)
    share = width // wide_count
    per_share = share // block

    def runs(fixed):
        return picks(natural(wide_bits), {b: v for b, v in fixed.items() if b[0] == WIDE})

    def rows_of(run):
        return pl.ds(pl.multiple_of(run * share, share), share)

    half = sizes.hidden_units // 2
    keep, leave = me[x_bit], 1 - me[x_bit]
    split = rows // 2
    meet(across, *[partner(b) for b in bits])
    beside = partner(near)
    early = [
        remote(given.att, r.att_in, sems, plan.att, beside), remote(given.gate_o, r.gate_o_in, sems, plan.gate_o, beside),
        remote(given.gates, r.gates_in, sems, plan.gates, beside),
        remote(given.hid.at[:, 1 - me[near]], r.hid_in, sems, plan.hid, beside),
    ]
    cot_swap = remote(given.cot.at[pl.ds(split, split)], r.cot_more, sems, plan.cot, partner(x_bit))
    fetch_all(hid=r.hid)

    def run_rows(ref, run):
        count = per_share // 2
        return ref[pl.ds(pl.multiple_of(run * count, count), count)].reshape(share, rows)

    near_rows = blocks // 2 * block
    small = r.small
    crossing, gm_swap, ffn_swap, two_swap, act_swap = [], [], [], [], []

    def middle(att_ref, gate_ref, sig_ref, wo, cot, mixed_ref, gain, low_ref, ffn_own):
        fetch_all(att=att_ref, gate_o=gate_ref, wo=wo, cot=cot, gain_two=gain, sig_o=sig_ref)

        def feed(x, cot_first, bias, up, down, two_ref):
            fetch_all(x=x, cot_in=cot_first, bias_two=bias, w_up=up, w_down=down)
            ready("att", "gate_o", "wo")
            for h in range(heads):
                for e in range(experts):
                    at = h * experts + e
                    r.gated[at * dh:(at + 1) * dh, :] = (
                        gate_ref[at:at + 1, :] * att_ref[h].astype(F32)
                    ).astype(BF16)
            r.two_own[...] = mm(r.gated[...], wo[...], TN).astype(BF16)
            part_swap = remote(r.two_own, r.head_in, sems, plan.part, across)
            ready("cot", "cot_in", "x", "gain_two", "bias_two")
            r.cot_t[:, 0:rows] = cot[...].T
            r.cot_t[:, rows:rows + split] = cot_first[...].T
            part_swap.wait()
            mixed = x[...].astype(F32) + (r.two_own[...].astype(F32) + r.head_in[...].astype(F32))
            mixed_ref[...] = mixed
            normed, _ = normalize(mixed)
            two = (normed * gain[...] + bias[...]).astype(BF16)
            two_ref[...] = two
            r.two_t[...] = two.T.reshape(r.two_t.shape)
            ready("w_up", "w_down")
            chunk = half // 2
            for which, target in ((leave, r.act_out), (keep, r.act)):
                for part in range(2):
                    units = pl.ds(pl.multiple_of(which * half + part * chunk, chunk), chunk)
                    inner = slice(part * chunk, (part + 1) * chunk)
                    value, slope = gelu_both(mm(two_ref[...], up[:, units]))
                    if target is r.act:
                        target[:, inner] = value.astype(BF16)
                    else:
                        target[:, :, inner] = value.astype(BF16).reshape(target.shape[0], target.shape[1], chunk)
                    r.pre[which, :, inner] = (mm(cot[...], down[units, :], NT) * slope).astype(BF16)
                if target is r.act_out:
                    act_swap.append(remote(r.act_out, r.act_in, sems, plan.act, lambda: partner(x_bit)))
            piece = mm(r.two_t[:, 1 - me[near]].reshape(near_rows, rows), r.pre[1]).astype(BF16)
            for at in range(blocks // 2):
                r.up_b_out[at] = piece[at * block:(at + 1) * block]
            up_b.launch(sems, partner, r.up_b_out)
            total = None
            for k in range(2):
                term = mm(r.pre[k], up[:, k * half:(k + 1) * half], NT)
                total = term if total is None else total + term
            r.two_own[...] = total.astype(BF16)
            two_swap.append(remote(r.two_own, r.two_in, sems, plan.two, across))
            for number, run in enumerate(runs(up_a.fixed(False))):
                piece = mm(run_rows(r.two_t, run), r.pre[0]).astype(BF16)
                for k in range(per_share):
                    r.up_a_out[number * per_share + k] = piece[k * block:(k + 1) * block]
            up_a.launch(sems, partner, r.up_a_out)
            mine = mm(r.act[...], down[pl.ds(pl.multiple_of(keep * half, half), half), :])
            theirs = mm(
                r.act_out[...].reshape(rows, half), down[pl.ds(pl.multiple_of(leave * half, half), half), :]
            )
            ffn_own[...] = (mine + theirs).astype(BF16)
            ffn_swap.append(remote(ffn_own, r.ffn_in, sems, plan.ffn, across))

        pl.run_scoped(
            feed, pltpu.VMEM((rows, width), BF16), pltpu.VMEM((split, width), BF16), pltpu.VMEM((1, width), F32),
            pltpu.VMEM((width, 2 * half), BF16), pltpu.VMEM((2 * half, width), BF16), pltpu.VMEM((rows, width), BF16),
        )

        def out_back():
            normed, inverse = normalize(mixed_ref[...])
            two_swap[0].wait()
            grad_two = r.two_own[...].astype(F32) + r.two_in[...].astype(F32)
            small[2:3, :] = jnp.sum(grad_two * normed, axis=0, keepdims=True)
            small[3:4, :] = jnp.sum(grad_two, axis=0, keepdims=True)
            grad_mixed = cot[...].astype(F32) + norm_back(grad_two * gain[...], normed, inverse)
            r.grad_mixed[...] = grad_mixed
            low_ref[...] = grad_mixed.astype(BF16)
            low_t = low_ref[...].T.reshape(blocks // 2, 2, block, rows)
            first, second = low_t[:, 0], low_t[:, 1]
            r.gm_out[...] = jnp.where(me[near] == 1, first, second)
            r.gm[...] = jnp.where(me[near] == 1, second, first)
            gm_swap.append(remote(r.gm_out, r.gm_in, sems, plan.gm, lambda: partner(near)))
            ready("sig_o")
            for h in range(heads):
                att = att_ref[h].astype(F32)
                total = None
                for e in range(experts):
                    at = h * experts + e
                    back = mm(wo[at * dh:(at + 1) * dh, :], low_ref[...], NT)
                    gate = gate_ref[at:at + 1, :]
                    grad_gate = jnp.sum(att * back, axis=0, keepdims=True)
                    r.logits[he + at:he + at + 1, :] = grad_gate * gate * (1.0 - sig_ref[at:at + 1, :])
                    total = gate * back if total is None else total + gate * back
                r.ga[h] = total.astype(BF16)
            ffn_swap[0].wait()
            ffn_own[...] = (mixed_ref[...] + (ffn_own[...].astype(F32) + r.ffn_in[...].astype(F32))).astype(BF16)
            pltpu.make_async_copy(ffn_own, r.output, r.load_sem.at[len(loaded)]).start()

        total_keys = 4 * rows
        chunk_shape = pltpu.VMEM((heads, dh, rows), BF16)
        pl.run_scoped(
            functools.partial(attention, out_back), pltpu.VMEM((heads, rows, total_keys), BF16), chunk_shape,
            chunk_shape, pltpu.VMEM((heads, dh, total_keys), BF16), *([chunk_shape] * 8),
            pltpu.VMEM((sizes.query_rows, sizes.query_rows), BF16), pltpu.VMEM((dh, total_keys), F32),
        )
        pltpu.make_async_copy(ffn_own, r.output, r.load_sem.at[len(loaded)]).wait()

    def attention(out_back, probs, qu, qv, rel, key_own, part_k, mem_k, part_mem_k, value_own, part_v, mem_v, part_mem_v, flip,
                  acc):
        fetch_all(
            probs=probs, qu=qu, qv=qv, rel=rel, key_own=key_own, part_k=part_k, mem_k=mem_k, part_mem_k=part_mem_k,
            value_own=value_own, part_v=part_v, mem_v=mem_v, part_mem_v=part_mem_v, flip=flip,
        )

        out_back()
        ready("probs", "qu", "qv", "rel", "key_own", "part_k", "mem_k", "part_mem_k")
        ready("value_own", "part_v", "mem_v", "part_mem_v", "flip")
        odd = place[DEEP] % 2 == 1
        size = sizes.query_rows
        for h in range(heads):
            k_one = jnp.where(odd, part_k[h], part_mem_k[h])
            v_one = jnp.where(odd, part_v[h], part_mem_v[h])
            keys = (part_mem_k[h], mem_k[h], k_one, key_own[h])
            values = (part_mem_v[h], mem_v[h], v_one, value_own[h])
            bias_u = bias_v = None
            for base in range(0, rows, size):
                here = slice(base, base + size)
                turned = mm(flip[...], probs[h, here, :])
                ga = mm(r.ga[h, :, here], flip[...]).astype(BF16)
                queries_u = mm(qu[h, :, here], flip[...]).astype(BF16)
                queries_v = mm(qv[h, :, here], flip[...]).astype(BF16)
                gp = jnp.concatenate([mm(ga, v, TN) for v in values], axis=1)
                weighted = turned * gp
                delta = jnp.sum(weighted, axis=1, keepdims=True)
                gs = ((weighted - turned * delta) * sizes.scale).astype(BF16)
                gk = mm(queries_u, gs[:, 2 * rows:])
                gv = mm(ga, turned[:, 2 * rows:].astype(BF16))
                gqu = None
                for i, k in enumerate(keys):
                    part = mm(k, gs[:, i * rows:(i + 1) * rows], NT)
                    gqu = part if gqu is None else gqu + part
                gpos = pltpu.roll(gs, rows - size - base, 1, stride=1, stride_axis=0)
                gqv = mm(rel[h], gpos, NT)
                grel = mm(queries_v, gpos)
                r.gq[h * dh:(h + 1) * dh, here] = mm((gqu + gqv).astype(BF16), flip[...]).astype(BF16)
                ones = jnp.ones((8, size), F32)
                sum_u, sum_v = [
                    lax.dot_general(ones, g, NT, precision=lax.Precision.HIGHEST, preferred_element_type=F32)
                    for g in (gqu, gqv)
                ]
                if base == 0:
                    r.gk[h] = gk
                    r.gv[h] = gv
                    acc[...] = grel
                    bias_u, bias_v = sum_u, sum_v
                else:
                    r.gk[h] += gk
                    r.gv[h] += gv
                    acc[...] += grel
                    bias_u, bias_v = bias_u + sum_u, bias_v + sum_v
            r.grel[h * dh:(h + 1) * dh, :] = acc[...].astype(BF16)
            r.small[4 + h:5 + h, 0:dh] = bias_u[0:1]
            r.small[4 + heads + h:5 + heads + h, 0:dh] = bias_v[0:1]
        r.cross_out[0] = r.gk[:, :, :rows].astype(BF16)
        r.cross_out[1] = r.gv[:, :, :rows].astype(BF16)
        crossing.append(remote(r.cross_out, r.cross_in, sems, plan.cross, lambda: partner(near)))

    hd_up = sizes.hd_up
    small[4:8, :] = jnp.zeros((4, width), F32)
    tokens_of = pltpu.VMEM((heads, dh, rows), BF16)
    pl.run_scoped(
        middle, tokens_of, pltpu.VMEM((he, rows), F32), pltpu.VMEM((he, rows), F32), pltpu.VMEM((hed, width), BF16),
        pltpu.VMEM((rows, width), BF16), pltpu.VMEM((rows, width), F32), pltpu.VMEM((1, width), F32),
        pltpu.VMEM((rows, width), BF16), pltpu.VMEM((rows, width), BF16),
    )

    def rest(*held):
        b = types.SimpleNamespace(**dict(zip(sizes.late_names, held)))
        fetch_all(each=b.each, sigs=b.sigs, gates=b.gates, wv=b.wv, wq=b.wq, wk=b.wk, rt=b.rt, x=b.x, gain=b.gain)
        up_a.acc, up_a.send, up_b.acc, up_b.send = r.act_out, b.send_up_a, b.acc_up_b, b.send_up_b
        far = [v for v in bits if v != near]
        out = tree_of("xyf", far, b.acc_out, b.send_out, r.got_out, plan.out)
        value = tree_of("xyf", far, b.acc_value, b.send_value, r.got_value, plan.value)
        query = tree_of("yxnf", bits, b.acc_query, b.send_query, r.got_query, plan.query)
        down = tree_of("ynf", bits, r.up_b_out, r.up_a_out, r.got_down, plan.down)
        half_count = len(wide_bits) // 2
        down.order = down.order[:half_count] + wide_bits[1:half_count] + down.order[half_count:]
        state = []

        def down_part(own):
            for number, run in enumerate(runs(down.fixed(own))):
                at_rows = rows_of(run)
                part = mm(r.cot_t[at_rows, 0:rows], r.act[...]) + mm(
                    r.cot_t[at_rows, rows:], r.act_in[...].reshape(rows, half)
                )
                for k in range(per_share):
                    at = number * per_share + k
                    piece = part[k * block:(k + 1) * block]
                    if own:
                        down.acc[at] = piece.astype(BF16)
                    else:
                        down.send[at] = piece.astype(BF16)
            if own:
                down.step()
            else:
                down.launch(sems, partner)

        def up_a_keep():
            for number, run in enumerate(runs(up_a.fixed(True))):
                part = mm(run_rows(r.two_t, run), r.pre[0])
                for k in range(per_share):
                    up_a.acc[number * per_share + k] = part[k * block:(k + 1) * block].astype(BF16)
            up_a.step()

        def up_b_keep():
            part = mm(r.two_t[:, me[near]].reshape(near_rows, rows), r.pre[1])
            for at in range(blocks // 2):
                up_b.acc[at] = part[at * block:(at + 1) * block].astype(BF16)
            up_b.step()

        def out_part():
            mine = mm(r.gm[...].reshape(near_rows, rows), r.gated[...], NT)
            for at in range(blocks // 2):
                out.acc[at] = mine[at * block:(at + 1) * block].astype(BF16)
            early[0].wait()
            early[1].wait()
            for h in range(heads):
                for e in range(experts):
                    at = h * experts + e
                    r.gated[at * dh:(at + 1) * dh, :] = (
                        r.gate_o_in[at:at + 1, :] * r.att_in[h].astype(F32)
                    ).astype(BF16)
            gm_swap[0].wait()
            theirs = mm(r.gm_in[...].reshape(near_rows, rows), r.gated[...], NT)
            for at in range(blocks // 2):
                out.acc[at] = (out.acc[at].astype(F32) + theirs[at * block:(at + 1) * block]).astype(BF16)
            out.advance(sems, partner)

        def own_part():
            ready("each", "sigs", "gates")
            crossing[0].wait()
            even = jnp.where(place[DEEP] % 2 == 0, 1.0, 0.0)
            for h in range(heads):
                gk = r.gk[h, :, rows:] + even * r.cross_in[0, h].astype(F32)
                gv = r.gv[h, :, rows:] + even * r.cross_in[1, h].astype(F32)
                b.own_out[h * dh:(h + 1) * dh, :] = gv.astype(BF16)
                b.own_out[hd + h * dh:hd + (h + 1) * dh, :] = gk.astype(BF16)
                for e in range(experts):
                    at = h * experts + e
                    gate = b.gates[at:at + 1, :]
                    grad_gate = jnp.sum(gv * b.each[at * dh:(at + 1) * dh, :].astype(F32), axis=0, keepdims=True)
                    r.logits[at:at + 1, :] = grad_gate * gate * (1.0 - b.sigs[at:at + 1, :])
                    b.grads[at * dh:(at + 1) * dh, :] = (gate * gv).astype(BF16)
            tail = b.own_out.shape[0] - 2 * hd
            logits = jnp.concatenate([r.logits[0:2 * he, :], jnp.zeros((tail - 2 * he, rows), F32)], axis=0)
            b.own_out[2 * hd:, :] = logits.astype(BF16)
            state_own.append(remote(b.own_out, r.own_in, sems, plan.own, partner(near)))
            b.grads[hed:, :] = b.own_out[hd:, :]

        def hidden_part():
            ready("wv", "wq", "wk", "rt")
            grad_hidden = mm(b.grads[0:hed, :], b.wv[...], TN)
            grad_hidden += mm(r.gq[...], b.wq[...], TN)
            grad_hidden += mm(b.grads[hed:hed + hd, :], b.wk[...], TN)
            grad_hidden += mm(b.grads[hed + hd:hed + hd + 2 * he, :], b.rt[...], TN)
            r.two_own[...] = grad_hidden.astype(BF16)
            state_head.append(remote(r.two_own, r.head_in, sems, plan.head, across))

        def norm_part():
            ready("x", "gain")
            state_head[0].wait()
            grad_hidden = r.two_own[...].astype(F32) + r.head_in[...].astype(F32)
            normed, inverse = normalize(b.x[...].astype(F32))
            small[0:1, :] = jnp.sum(grad_hidden * normed, axis=0, keepdims=True)
            small[1:2, :] = jnp.sum(grad_hidden, axis=0, keepdims=True)
            state.append(remote(small, r.small_in.at[0], sems, plan.small[0], partner(bits[0])))
            r.grad_mixed[...] += norm_back(grad_hidden * b.gain[...], normed, inverse)
            input_copy = pltpu.make_async_copy(r.grad_mixed, r.grad_input, r.load_sem.at[len(loaded) + 1])
            input_copy.start()
            state_input.append(input_copy)

        def small_step():
            at = len(state) - 1
            if at == len(bits):
                return
            state[at].wait()
            small[...] = small[...] + r.small_in[at]
            state.append(
                None if at + 1 == len(bits)
                else remote(small, r.small_in.at[at + 1], sems, plan.small[at + 1], partner(bits[at + 1]))
            )

        def value_own():
            ready("hid")
            mine = mm(r.hid[:, me[near]].reshape(near_rows, rows), b.grads[...], NT)
            for at in range(blocks // 2):
                value.acc[at] = mine[at * block:(at + 1) * block]

        def value_part():
            early[2].wait()
            early[3].wait()
            state_own[0].wait()
            for at in range(he):
                h = at // experts
                b.grads[at * dh:(at + 1) * dh, :] = (
                    r.gates_in[at:at + 1, :] * r.own_in[h * dh:(h + 1) * dh, :].astype(F32)
                ).astype(BF16)
            b.grads[hed:, :] = r.own_in[hd:, :]
            theirs = mm(r.hid_in[...].reshape(near_rows, rows), b.grads[...], NT)
            for at in range(blocks // 2):
                value.acc[at] += theirs[at * block:(at + 1) * block]
            value.advance(sems, partner)

        def table_copy(number, run):
            return pltpu.make_async_copy(
                given.table.at[rows_of(run)], b.table.at[pl.ds(number * share, share)], r.table_sem.at[number]
            )

        for number, run in enumerate(runs(query.fixed(False))):
            table_copy(number, run).start()

        def query_part(own):
            if not own and hd_up > hd:
                for at in range(blocks // 2):
                    query.send[at, :, hd:hd_up] = jnp.zeros((block, hd_up - hd), BF16)
                    query.acc[at, :, hd:hd_up] = jnp.zeros((block, hd_up - hd), BF16)
            ready("hid")
            for number, run in enumerate(runs(query.fixed(own))):
                table_copy(number, run).wait()
                part = mm(run_rows(r.hid, run), r.gq[...], NT)
                part_rel = mm(b.table[number * share:(number + 1) * share, :], r.grel[...], NT)
                for k in range(per_share):
                    at = number * per_share + k
                    piece, piece_rel = part[k * block:(k + 1) * block], part_rel[k * block:(k + 1) * block]
                    if own:
                        query.acc[at, :, 0:hd] = piece.astype(BF16)
                        query.acc[at, :, hd_up:] = piece_rel.astype(BF16)
                    else:
                        query.send[at, :, 0:hd] = piece.astype(BF16)
                        query.send[at, :, hd_up:] = piece_rel.astype(BF16)
            if own:
                query.step()
            else:
                query.launch(sems, partner)
                for number, run in enumerate(runs(query.fixed(True))):
                    table_copy(number, run).start()

        state_own, state_head, state_input = [], [], []
        def half_part():
            down.arrive()
            r.half_out[...] = down.finish(leave).astype(BF16)
            state_own.append(remote(r.half_out, r.half_in, sems, plan.half, partner(x_bit)))
            r.g_down[:, pl.ds(pl.multiple_of(keep * half, half), half)] = down.finish(keep)

        def next_level(tree):
            if tree.level < len(tree.order):
                tree.advance(sems, partner)

        act_swap[0].wait()
        up_a_keep()
        query_part(False)
        next_level(up_a)
        up_b_keep()
        cot_swap.wait()
        r.cot_t[:, rows + split:] = r.cot_more[...].T
        down_part(False)
        next_level(up_b)
        next_level(up_a)
        own_part()
        hidden_part()
        out_part()
        next_level(up_a)
        query_part(True)
        norm_part()
        value_own()
        down_part(True)
        next_level(up_b)
        next_level(down)
        small_step()
        value_part()
        small_step()
        next_level(out)
        next_level(up_b)
        small_step()
        next_level(out)
        next_level(down)
        next_level(query)
        next_level(value)
        next_level(query)
        next_level(value)
        next_level(query)
        while any(tree.level < len(tree.order) for tree in (up_a, up_b, out, query, value, down)):
            for tree in (up_a, up_b, out, query, value, down):
                next_level(tree)
        half_part()
        while len(state) <= len(bits):
            small_step()
        r.small_out[...] = small[...]
        for number, tree in enumerate((up_a, up_b)):
            tree.arrive()
            r.g_up[:, number * half:(number + 1) * half] = tree.finish()
        out.arrive()
        total = out.finish()
        for at in range(he):
            r.g_out[at] = total[:, at * dh:(at + 1) * dh]
        value.arrive()
        total = value.finish()
        for at in range(he):
            r.g_value[at] = total[:, at * dh:(at + 1) * dh]
        for h in range(heads):
            r.g_key[:, h, :] = total[:, hed + h * dh:hed + (h + 1) * dh]
        r.g_router[...] = total[:, hed + hd:hed + hd + 2 * he]
        query.arrive()
        total = query.finish()
        for h in range(heads):
            r.g_query[:, h, :] = total[:, h * dh:(h + 1) * dh]
            r.g_rel[:, h, :] = total[:, hd_up + h * dh:hd_up + (h + 1) * dh]
        state_own[1].wait()
        r.g_down[:, pl.ds(pl.multiple_of(leave * half, half), half)] = r.half_in[...].astype(F32)
        state_input[0].wait()

    pl.run_scoped(rest, *sizes.late_scratch)


def late_call(inputs, sizes):
    wide_bits, deep_bits = bit_names(sizes.wide, sizes.deep)
    bits = len(wide_bits) + len(deep_bits)
    blocks = sizes.wide * sizes.deep
    block, rows, width, heads, dh = sizes.block, sizes.rows, sizes.width, sizes.heads, sizes.dh
    he, hd = heads * sizes.experts, heads * dh
    hed, half = he * dh, sizes.hidden_units // 2
    tail = 32
    sizes.hd_up = -(-hd // 128) * 128
    sizes.value_n = hed + hd + tail
    query_n = sizes.hd_up + hd
    count = 16 + 7 * bits
    slots = iter(range(count))

    def levels():
        return [next(slots) for _ in range(bits)]

    plan = types.SimpleNamespace(
        two=next(slots), ffn=next(slots), act=next(slots), gm=next(slots), cross=next(slots), part=next(slots),
        att=next(slots), gate_o=next(slots), gates=next(slots), hid=next(slots), cot=next(slots),
        own=next(slots), head=next(slots), half=next(slots), small=levels(), up_a=levels(), up_b=levels(),
        out=levels(), query=levels(), down=levels(), value=levels(),
    )

    def got(n, start, stop):
        return [pltpu.VMEM((blocks >> (level + 1), block, n), BF16) for level in range(start, stop)]

    def taken(name):
        return pltpu.VMEM(inputs[name].shape, inputs[name].dtype)

    sem = pltpu.SemaphoreType.DMA
    token_rows = pltpu.VMEM((rows, width), BF16)
    near_half = pltpu.VMEM((blocks // 2, block, rows), BF16)
    first_half = pltpu.VMEM((blocks // 2, block, half), BF16)
    scratch = dict(
        act=pltpu.VMEM((rows, half), BF16), hid=taken("hid"), two_t=taken("hid"),
        pre=pltpu.VMEM((2, rows, half), BF16), cot_t=pltpu.VMEM((width, 2 * rows), BF16), cot_more=taken("cot_in"),
        gated=pltpu.VMEM((hed, rows), BF16), att_in=taken("att"), gate_o_in=taken("gate_o"), gates_in=taken("gates"),
        two_own=token_rows, two_in=token_rows, ffn_in=token_rows, head_in=token_rows,
        act_in=first_half, act_out=first_half, up_a_out=first_half, up_b_out=first_half,
        hid_in=near_half, gm=near_half, gm_in=near_half, gm_out=near_half,
        grad_mixed=pltpu.VMEM((rows, width), F32), table_sem=sem((sizes.wide // 2,)),
        small=pltpu.VMEM((8, width), F32), small_in=pltpu.VMEM((bits, 8, width), F32),
        logits=pltpu.VMEM((2 * he, rows), F32), ga=pltpu.VMEM((heads, dh, rows), BF16),
        gq=pltpu.VMEM((hd, rows), BF16), gk=pltpu.VMEM((heads, dh, 2 * rows), F32),
        gv=pltpu.VMEM((heads, dh, 2 * rows), F32), grel=pltpu.VMEM((hd, 4 * rows), BF16),
        cross_out=pltpu.VMEM((2, heads, dh, rows), BF16), cross_in=pltpu.VMEM((2, heads, dh, rows), BF16),
        own_in=pltpu.VMEM((2 * hd + tail, rows), BF16), half_in=pltpu.VMEM((block, half), BF16),
        half_out=pltpu.VMEM((block, half), BF16),
        got_up_a=got(half, 0, bits), got_up_b=got(half, 0, bits), got_out=got(hed, 1, bits),
        got_query=got(query_n, 0, bits), got_down=got(half, 0, bits - 1), got_value=got(sizes.value_n, 1, bits),
        load_sem=sem((len(inputs) + 3,)), send_sem=sem((count,)), recv_sem=sem((count,)),
    )
    late = dict(
        send_out=pltpu.VMEM((blocks >> 2, block, hed), BF16), acc_out=pltpu.VMEM((blocks >> 1, block, hed), BF16),
        table=pltpu.VMEM((width // 2, 4 * rows), BF16), each=taken("each"), sigs=taken("sigs"), gates=taken("gates"), wv=taken("wv"),
        wq=taken("wq"), wk=taken("wk"), rt=taken("rt"), x=taken("x"), gain=taken("gain"),
        own_out=pltpu.VMEM((2 * hd + tail, rows), BF16), grads=pltpu.VMEM((sizes.value_n, rows), BF16),
        send_up_a=pltpu.VMEM((blocks >> 2, block, half), BF16), send_up_b=pltpu.VMEM((blocks >> 2, block, half), BF16),
        acc_up_b=pltpu.VMEM((blocks >> 1, block, half), BF16),
        send_query=pltpu.VMEM((blocks >> 1, block, query_n), BF16),
        acc_query=pltpu.VMEM((blocks >> 1, block, query_n), BF16),
        send_value=pltpu.VMEM((blocks >> 2, block, sizes.value_n), BF16),
        acc_value=pltpu.VMEM((blocks >> 1, block, sizes.value_n), F32),
    )
    sizes.late_names, sizes.late_scratch = list(late), list(late.values())
    outs = dict(
        g_down=((block, 2 * half), F32), g_up=((block, 2 * half), F32), g_out=((he, block, dh), F32),
        g_value=((he, block, dh), F32), g_query=((block, heads, dh), F32), g_key=((block, heads, dh), F32),
        g_rel=((block, heads, dh), F32), g_router=((block, 2 * he), F32), small_out=((8, width), F32),
        grad_input=((rows, width), F32), output=((rows, width), BF16),
    )
    flat, tree = jax.tree.flatten(list(scratch.values()))

    def kernel(*refs):
        held = jax.tree.unflatten(tree, refs[len(inputs) + len(outs):])
        late_kernel(
            *refs[:len(inputs) + len(outs)], *held, names=[None] * 0 + [n + "_" for n in inputs] + list(outs) + list(scratch),
            loaded=list(inputs), sizes=sizes, plan=plan,
        )

    vmem, anywhere = pl.BlockSpec(memory_space=pltpu.VMEM), pl.BlockSpec(memory_space=pl.ANY)
    results = pl.pallas_call(
        kernel,
        in_specs=[anywhere] * len(inputs),
        out_specs=[vmem] * (len(outs) - 2) + [anywhere] * 2,
        out_shape=[jax.ShapeDtypeStruct(shape, dtype) for shape, dtype in outs.values()],
        scratch_shapes=flat,
        compiler_params=pltpu.CompilerParams(collective_id=0, has_side_effects=True, vmem_limit_bytes=60 << 20),
        cost_estimate=pl.CostEstimate(flops=4 * 10**10, bytes_accessed=10**8, transcendentals=0),
    )(*inputs.values())
    return types.SimpleNamespace(**dict(zip(outs, results)))


def body(
    layer_input, mem_keys, mem_values, route_value, route_output, ln1_gain, ln1_bias, w_query, w_key, w_rel,
    content_bias, position_bias, w_value, w_out, router_value, router_output, ln2_gain, ln2_bias, w_up, w_down,
    cotangent,
):
    rows, width = layer_input.shape
    heads, dh = content_bias.shape
    experts = w_value.shape[1]
    odd = (lax.axis_index("dp") % 2).astype(jnp.int32)
    scale = 1.0 / math.sqrt(dh)
    total_keys = 4 * rows
    block = rows // 2
    hd = heads * dh
    hed = heads * experts * dh

    wq = jnp.transpose(w_query, (1, 2, 0)).reshape(hd, width)
    wk = jnp.transpose(w_key, (1, 2, 0)).reshape(hd, width)
    wr = jnp.transpose(w_rel, (1, 2, 0)).reshape(hd, width)
    wv = jnp.transpose(w_value, (0, 1, 3, 2)).reshape(hed, width)
    wo = w_out.reshape(hed, width)
    rt = jnp.concatenate(
        [jnp.transpose(r, (1, 2, 0)).reshape(heads * experts, width) for r in (router_value, router_output)], axis=0
    )
    mem_k = jnp.transpose(mem_keys, (1, 2, 0))
    mem_v = jnp.transpose(mem_values, (1, 2, 0))
    rv = jnp.transpose(route_value, (0, 2, 1))
    ro = jnp.transpose(route_output, (0, 2, 1))
    rt = jnp.concatenate(
        [jnp.transpose(r, (1, 2, 0)).reshape(heads * experts, width) for r in (router_value, router_output)], axis=0
    )
    table = jnp.asarray(position_table(total_keys, width))
    first = early_call(dict(
        x=layer_input, gain=ln1_gain.reshape(1, width), bias=ln1_bias.reshape(1, width), wk=wk, rt=rt, rv=rv, ro=ro,
        wv=wv, wq=wq, cb=content_bias, pb=position_bias, wr=wr, table=table, mem_k=mem_k, mem_v=mem_v, cot=cotangent,
    ), types.SimpleNamespace(
        heads=heads, experts=experts, dh=dh, rows=rows, width=width, wide=lax.axis_size(WIDE),
        deep=lax.axis_size(DEEP), scale=scale, query_rows=block,
    ))
    att, gate_v, gate_o, sig_v, sig_o, hid = first.att, first.gate_v, first.gate_o, first.sig_v, first.sig_o, first.hid
    wide_count, depth = lax.axis_size(WIDE), lax.axis_size(DEEP)
    blocks = wide_count * depth
    block_rows, he = width // blocks, heads * experts
    hidden_units = w_up.shape[1]
    wide_bits, deep_bits = bit_names(wide_count, depth)
    gain_two, bias_two = ln2_gain.reshape(1, width), ln2_bias.reshape(1, width)
    sem = pltpu.SemaphoreType.DMA

    def shapes(*pairs):
        return [jax.ShapeDtypeStruct(shape, dtype) for shape, dtype in pairs]

    flip = jnp.asarray(np.eye(block // 2, dtype=np.float32)[::-1].astype(BF16))
    inputs = dict(
        hid=hid, gates=gate_v, cot=cotangent, cot_in=first.cot_in, gain_two=gain_two, bias_two=bias_two, w_up=w_up,
        w_down=w_down, att=att, gate_o=gate_o, sig_o=sig_o, wo=wo,
        flip=flip, probs=first.probs, qu=first.qu, qv=first.qv, rel=first.rel,
        key_own=first.key_own, part_k=first.part_k, mem_k=mem_k, part_mem_k=first.part_mem_k,
        value_own=first.value_own, part_v=first.part_v, mem_v=mem_v, part_mem_v=first.part_mem_v,
        table=table, sigs=sig_v, each=first.each, wv=wv, wq=wq, wk=wk, rt=rt,
        x=layer_input, gain=ln1_gain.reshape(1, width),
    )
    done = late_call(inputs, types.SimpleNamespace(
        heads=heads, experts=experts, dh=dh, rows=rows, width=width, wide=wide_count, deep=depth, block=block_rows,
        hidden_units=hidden_units, scale=scale, query_rows=block // 2,
    ))
    start = (lax.axis_index(WIDE) * depth + lax.axis_index(DEEP)) * block_rows
    ln = lax.dynamic_slice_in_dim(done.small_out, start, block_rows, axis=1)
    biases = done.small_out[4:, :dh].reshape(2, heads, dh)
    routers = done.g_router.reshape(block_rows, 2, heads, experts)

    output, grad_input, g_query, g_key, g_rel, g_value, g_out, g_up, g_down = finished(
        done.output, done.grad_input, done.g_query, done.g_key, done.g_rel, done.g_value, done.g_out, done.g_up,
        done.g_down,
    )

    def by_expert(values):
        return values.reshape(heads, experts, block_rows, dh)

    return (
        output, grad_input, ln[0], ln[1], g_query, g_key, g_rel, biases[0], biases[1],
        by_expert(g_value), jnp.transpose(by_expert(g_out), (0, 1, 3, 2)), routers[:, 0], routers[:, 1],
        ln[2], ln[3], g_up, jnp.transpose(g_down),
    )


def solution(mesh):
    tokens = ("wide", "dp")
    return jax.shard_map(
        body,
        mesh=mesh,
        in_specs=(
            P(tokens, None), P(tokens, "head", None), P(tokens, "head", None), P("head", tokens, None),
            P("head", tokens, None), P(), P(), P(None, "head", None), P(None, "head", None), P(None, "head", None),
            P("head", None), P("head", None), P("head", None, None, None), P("head", None, None, None),
            P(None, "head", None), P(None, "head", None), P(), P(), P(None, "head"), P("head", None), P(tokens, None),
        ),
        out_specs=(
            P(tokens, None), P(tokens, None), P(tokens), P(tokens), P(tokens, "head", None), P(tokens, "head", None),
            P(tokens, "head", None), P("head", None), P("head", None), P("head", None, tokens, None),
            P("head", None, None, tokens), P(tokens, "head", None), P(tokens, "head", None), P(tokens), P(tokens),
            P(tokens, "head"), P("head", tokens),
        ),
        check_vma=False,
    )
```

```python
import functools
import math
import types

import jax
import jax.numpy as jnp
import numpy as np
from jax import lax
from jax.experimental import pallas as pl
from jax.experimental.pallas import tpu as pltpu
from jax.sharding import PartitionSpec as P

EPSILON = 1e-05
NEG_LARGE = -1e30
F32 = jnp.float32
BF16 = jnp.bfloat16
WIDE, DEEP = "wide", "dp"

NN = (((1,), (0,)), ((), ()))
NT = (((1,), (1,)), ((), ()))
TN = (((0,), (0,)), ((), ()))


def mm(a, b, dims=NN):
    return lax.dot_general(a, b, dims, preferred_element_type=F32)


def normalize(values):
    row_mean = jnp.mean(values, axis=-1, keepdims=True)
    centered = values - row_mean
    variance = jnp.mean(centered * centered, axis=-1, keepdims=True)
    inverse = lax.rsqrt(variance + EPSILON)
    return (centered * inverse, inverse)


def norm_back(grad_normed, normed, inverse):
    first_mean = jnp.mean(grad_normed, axis=-1, keepdims=True)
    second_mean = jnp.mean(grad_normed * normed, axis=-1, keepdims=True)
    return inverse * (grad_normed - first_mean - normed * second_mean)


def position_table(extent, model_width):
    half_width = model_width // 2
    frequencies = np.exp(
        np.arange(half_width, dtype=np.float32) * np.float32(-2.0 * math.log(10000.0) / model_width)
    ).astype(np.float32)
    distance = np.arange(extent - 1, -1, -1).astype(np.float32)
    angles = (frequencies[:, None] * distance[None, :]).astype(np.float64)
    return np.concatenate([np.sin(angles), np.cos(angles)], axis=0).astype(np.float32).astype(BF16)


def whole(array):
    return pl.BlockSpec(array.shape, lambda *_: (0,) * len(array.shape))


def gelu_both(x):
    c = math.sqrt(2.0 / math.pi)
    square = x * x
    t = jnp.tanh(c * x * (1.0 + 0.044715 * square))
    half = 0.5 * (1.0 + t)
    return x * half, half + 0.5 * x * (1.0 - t * t) * (c * (1.0 + 3.0 * 0.044715 * square))


def meet(*devices):
    barrier = pltpu.get_barrier_semaphore()
    for device in devices:
        pl.semaphore_signal(barrier, inc=1, device_id=device, device_id_type=pl.DeviceIdType.MESH)
    pl.semaphore_wait(barrier, len(devices))


def other_core():
    return (1 - lax.axis_index("head"), lax.axis_index("wide"), lax.axis_index("dp"))


class Swap:
    def __init__(self, src, dst, sems, slot, device):
        self.parts = (src, dst, sems, slot, device)
        self.copy().start()

    def copy(self):
        src, dst, sems, slot, device = self.parts
        return pltpu.make_async_remote_copy(
            src_ref=src, dst_ref=dst, send_sem=sems[0].at[slot], recv_sem=sems[1].at[slot],
            device_id=device() if callable(device) else device, device_id_type=pl.DeviceIdType.MESH,
        )

    def wait(self):
        self.copy().wait()


remote = Swap


def early_kernel(*refs, given_names, out_names, held_names, sizes):
    count = len(given_names)
    given = types.SimpleNamespace(**dict(zip(given_names, refs)))
    out = types.SimpleNamespace(**dict(zip(out_names, refs[count:])))
    r = types.SimpleNamespace(**dict(zip(held_names, refs[count + len(out_names):])))
    heads, experts, dh, rows, width = sizes.heads, sizes.experts, sizes.dh, sizes.rows, sizes.width
    deep, wide = lax.axis_index(DEEP), lax.axis_index(WIDE)
    near = deep % 2
    beside = (lax.axis_index("head"), wide, deep + 1 - 2 * near)
    across = (lax.axis_index("head"), wide + 1 - 2 * (wide % 2), deep)
    sems = (r.send_sem, r.recv_sem)
    loads, writes = {}, []

    def fetch(*names):
        for name in names:
            slot = given_names.index(name)
            loads[name] = pltpu.make_async_copy(getattr(given, name), getattr(r, name), r.load_sem.at[slot])
            loads[name].start()

    def ready(*names):
        for name in names:
            loads[name].wait()

    def put(name, source, *at):
        target = getattr(out, name)
        if at:
            source, target = source.at[at], target.at[at]
        writes.append(pltpu.make_async_copy(source, target, r.write_sem.at[len(writes)]))
        writes[-1].start()

    fetch(*sizes.loaded)
    meet(beside, across)
    mem_k_swap = Swap(given.mem_k, r.part_mem_k, sems, 0, beside)
    cot_swap = Swap(given.cot, out.cot_in, sems, 2, across)
    ready("x", "gain", "bias")
    normed, _ = normalize(r.x[...].astype(F32))
    hid = (normed * r.gain[...] + r.bias[...]).astype(BF16)
    r.hid[...] = hid
    ready("wk")
    for h in range(heads):
        r.key_own[h] = mm(r.wk[h * dh:(h + 1) * dh, :], r.hid[...], NT).astype(BF16)
    key_swap = Swap(r.key_own, r.part_k, sems, 3, beside)
    ready("rt", "rv", "ro")
    logits = mm(r.rt[...], r.hid[...], NT)
    sig = 1.0 / (1.0 + jnp.exp(-logits))
    masks = []
    for routes in (r.rv, r.ro):
        for h in range(heads):
            for e in range(experts):
                hit = (routes[h, 0:1, :] == e) | (routes[h, 1:2, :] == e)
                masks.append(jnp.where(hit, 1.0, 0.0))
    gate = sig * jnp.concatenate(masks, axis=0)
    he = heads * experts
    r.gate[...] = gate
    out.gate_v[...] = gate[:he]
    out.gate_o[...] = gate[he:]
    out.sig_v[...] = sig[:he]
    out.sig_o[...] = sig[he:]
    ready("wv")
    for h in range(heads):
        total = None
        for e in range(experts):
            at = h * experts + e
            each = mm(r.wv[at * dh:(at + 1) * dh, :], r.hid[...], NT)
            r.each[at * dh:(at + 1) * dh, :] = each.astype(BF16)
            term = r.gate[at:at + 1, :] * each
            total = term if total is None else total + term
        r.value_own[h] = total.astype(BF16)
    mem_v_swap = Swap(given.mem_v, r.part_mem_v, sems, 1, beside)
    value_swap = Swap(r.value_own, r.part_v, sems, 4, beside)
    put("each", r.each)
    put("key_own", r.key_own)
    put("value_own", r.value_own)
    ready("wq", "cb", "pb")
    eye = (
        lax.broadcasted_iota(jnp.int32, (dh, dh), 0) == lax.broadcasted_iota(jnp.int32, (dh, dh), 1)
    ).astype(F32)

    def column(row):
        spread = jnp.broadcast_to(row, (8, dh))
        return lax.dot_general(
            eye, spread, NT, precision=lax.Precision.HIGHEST, preferred_element_type=F32
        )[:, 0:1]

    for h in range(heads):
        queries = mm(r.wq[h * dh:(h + 1) * dh, :], r.hid[...], NT)
        r.qu[h] = (queries + column(r.cb[h:h + 1, :])).astype(BF16)
        r.qv[h] = (queries + column(r.pb[h:h + 1, :])).astype(BF16)
    put("qu", r.qu)
    put("qv", r.qv)
    ready("wr", "table")
    for h in range(heads):
        r.rel[h] = mm(r.wr[h * dh:(h + 1) * dh, :], r.table[...]).astype(BF16)
    put("rel", r.rel)
    r.hid_t[...] = r.hid[...].T.reshape(r.hid_t.shape)
    put("hid", r.hid_t)
    total_keys, size = 4 * rows, sizes.query_rows
    for h in range(heads):
        for base in range(0, rows, size):
            here = slice(base, base + size)
            positional = mm(r.qv[h, :, here], r.rel[h], TN)
            r.scores[h, here, :] = pltpu.roll(
                positional, total_keys - rows + 1 + base, 1, stride=1, stride_axis=0
            )
    odd = near == 1
    ready("mem_k", "mem_v")
    mem_k_swap.wait()
    key_swap.wait()
    put("part_k", r.part_k)
    put("part_mem_k", r.part_mem_k)
    first = jnp.where(odd, 0, rows)
    for h in range(heads):
        k_one = jnp.where(odd, r.part_k[h], r.part_mem_k[h])
        keys = (r.part_mem_k[h], r.mem_k[h], k_one, r.key_own[h])
        for base in range(0, rows, size):
            here = slice(base, base + size)
            content = jnp.concatenate([mm(r.qu[h, :, here], k, TN) for k in keys], axis=1)
            row = lax.broadcasted_iota(jnp.int32, (size, total_keys), 0) + base
            col = lax.broadcasted_iota(jnp.int32, (size, total_keys), 1)
            visible = (col <= row + (total_keys - rows)) & (col >= first)
            scores = jnp.where(visible, (content + r.scores[h, here, :]) * sizes.scale, NEG_LARGE)
            peak = jnp.max(scores, axis=1, keepdims=True)
            exponents = jnp.exp(scores - peak)
            total = jnp.sum(exponents, axis=1, keepdims=True)
            probs = (exponents * (1.0 / total)).astype(BF16)
            r.probs[h, here, :] = probs
            put("probs", r.probs, h, pl.ds(base, size))
    mem_v_swap.wait()
    value_swap.wait()
    put("part_v", r.part_v)
    put("part_mem_v", r.part_mem_v)
    for h in range(heads):
        v_one = jnp.where(odd, r.part_v[h], r.part_mem_v[h])
        values = (r.part_mem_v[h], r.mem_v[h], v_one, r.value_own[h])
        att = None
        for i, v in enumerate(values):
            term = mm(v, r.probs[h, :, i * rows:(i + 1) * rows], NT)
            att = term if att is None else att + term
        out.att[h] = att.astype(BF16)
    cot_swap.wait()
    for write in writes:
        write.wait()


def early_call(inputs, sizes):
    heads, experts, dh, rows, width = sizes.heads, sizes.experts, sizes.dh, sizes.rows, sizes.width
    he, hed, hd = heads * experts, heads * experts * dh, heads * dh
    tokens = (heads, dh, rows)
    blocks = sizes.wide * sizes.deep
    hid_shape = (blocks // 2, 2, width // blocks, rows)
    anywhere = dict(
        each=((hed, rows), BF16), key_own=(tokens, BF16), value_own=(tokens, BF16), qu=(tokens, BF16),
        qv=(tokens, BF16), rel=((heads, dh, 4 * rows), BF16), hid=(hid_shape, BF16), part_k=(tokens, BF16),
        part_v=(tokens, BF16), part_mem_k=(tokens, BF16), part_mem_v=(tokens, BF16),
        probs=((heads, rows, 4 * rows), BF16), cot_in=((rows, width), BF16),
    )
    near = dict(
        att=(tokens, BF16), gate_v=((he, rows), F32), gate_o=((he, rows), F32), sig_v=((he, rows), F32),
        sig_o=((he, rows), F32),
    )
    outs = {**anywhere, **near}
    sem = pltpu.SemaphoreType.DMA
    sizes.loaded = [name for name in inputs if name != "cot"]
    held = {name: pltpu.VMEM(inputs[name].shape, inputs[name].dtype) for name in sizes.loaded}
    held.update({name: pltpu.VMEM(shape, dtype) for name, (shape, dtype) in anywhere.items() if name != "cot_in"})
    held.update(
        hid=pltpu.VMEM((rows, width), BF16), hid_t=pltpu.VMEM(hid_shape, BF16),
        scores=pltpu.VMEM((heads, rows, 4 * rows), F32), gate=pltpu.VMEM((2 * he, rows), F32),
        load_sem=sem((len(inputs),)), write_sem=sem((24,)), send_sem=sem((5,)), recv_sem=sem((5,)),
    )
    vmem, hbm = pl.BlockSpec(memory_space=pltpu.VMEM), pl.BlockSpec(memory_space=pl.ANY)
    results = pl.pallas_call(
        functools.partial(
            early_kernel, given_names=list(inputs), out_names=list(outs), held_names=list(held), sizes=sizes
        ),
        in_specs=[hbm] * len(inputs),
        out_specs=[hbm] * len(anywhere) + [vmem] * len(near),
        out_shape=[jax.ShapeDtypeStruct(shape, dtype) for shape, dtype in outs.values()],
        scratch_shapes=list(held.values()),
        compiler_params=pltpu.CompilerParams(collective_id=2, has_side_effects=True, vmem_limit_bytes=58 << 20),
        cost_estimate=pl.CostEstimate(flops=2 * 10**10, bytes_accessed=3 * 10**7, transcendentals=2 * 10**6),
    )(*inputs.values())
    return types.SimpleNamespace(**dict(zip(outs, results)))


def finish_kernel(*refs):
    load_sem, write_sem = refs[-2:]
    count = (len(refs) - 2) // 3
    given, outs, held = refs[:count], refs[count:2 * count], refs[2 * count:3 * count]
    loads = [pltpu.make_async_copy(given[i], held[i], load_sem.at[i]) for i in range(count)]
    writes = [pltpu.make_async_copy(held[i], outs[i], write_sem.at[i]) for i in range(count)]
    for copy in loads:
        copy.start()
    for load, write in zip(loads, writes):
        load.wait()
        write.start()
    for write in writes:
        write.wait()


def finished(*arrays):
    hbm = pl.BlockSpec(memory_space=pl.ANY)
    return pl.pallas_call(
        finish_kernel,
        in_specs=[hbm] * len(arrays),
        out_specs=[hbm] * len(arrays),
        out_shape=[jax.ShapeDtypeStruct(a.shape, a.dtype) for a in arrays],
        scratch_shapes=[pltpu.VMEM(a.shape, a.dtype) for a in arrays] + [pltpu.SemaphoreType.DMA((len(arrays),))] * 2,
        compiler_params=pltpu.CompilerParams(vmem_limit_bytes=60 << 20),
        cost_estimate=pl.CostEstimate(flops=0, bytes_accessed=10**7, transcendentals=0),
    )(*arrays)


def bit_names(wide_count, depth):
    wide_bits = [(WIDE, b) for b in range(int(math.log2(wide_count)))]
    deep_bits = [(DEEP, b) for b in range(int(math.log2(depth)))]
    return wide_bits, deep_bits


def bit_order(axes, wide_bits, deep_bits):
    half = len(wide_bits) // 2
    groups = dict(x=wide_bits[:half], y=wide_bits[half:], n=deep_bits[:1], f=deep_bits[1:])
    return [bit for axis in axes for bit in groups[axis]]


def natural(bits):
    return [b for b in sorted(bits, key=lambda b: (b[0] == WIDE, b[1]), reverse=True)]


def picks(left, fixed):
    free = [b for b in left if b not in fixed]
    found = []
    for number in range(1 << len(free)):
        index = 0
        for place, b in enumerate(left):
            if b in fixed:
                digit = fixed[b]
            else:
                digit = (number >> (len(free) - 1 - free.index(b))) & 1
            index = index + digit * (1 << (len(left) - 1 - place))
        found.append(index)
    return found


class Tree:
    def __init__(self, order, left, acc, send, got, slots, me):
        self.order, self.left, self.acc, self.send, self.got, self.slots, self.me = order, left, acc, send, got, slots, me
        self.level = 0
        self.copies = {}

    def fixed(self, own):
        bit = self.order[self.level]
        return {bit: self.me[bit] if own else 1 - self.me[bit]}

    def launch(self, sems, partner, src=None):
        got = self.got[self.level]
        src = self.send.at[pl.ds(0, got.shape[0])] if src is None else src
        bit = self.order[self.level]
        self.copies[self.level] = remote(src, got, sems, self.slots[self.level], lambda: partner(bit))

    def step(self):
        self.left = [b for b in self.left if b != self.order[self.level]]
        self.level += 1

    def arrive(self):
        self.copies[self.level - 1].wait()
        return self.got[self.level - 1]

    def advance(self, sems, partner):
        got = self.arrive() if self.level else None

        def piece(index):
            mine = self.acc[index].astype(F32)
            return mine if got is None else mine + got[index].astype(F32)

        for place, index in enumerate(picks(self.left, self.fixed(False))):
            self.send[place] = piece(index).astype(BF16)
        self.launch(sems, partner)
        for place, index in enumerate(picks(self.left, self.fixed(True))):
            self.acc[place] = piece(index).astype(self.acc.dtype)
        self.step()

    def finish(self, index=0):
        return self.acc[index].astype(F32) + self.got[self.level - 1][index].astype(F32)


def late_kernel(*refs, names, loaded, sizes, plan):
    r = types.SimpleNamespace(**dict(zip(names, refs)))
    given = types.SimpleNamespace(**dict(zip(loaded, refs)))
    heads, experts, dh, rows, width = sizes.heads, sizes.experts, sizes.dh, sizes.rows, sizes.width
    wide_count, depth, block = sizes.wide, sizes.deep, sizes.block
    hd, he, hed = heads * dh, heads * experts, heads * experts * dh
    blocks = wide_count * depth
    wide_bits, deep_bits = bit_names(wide_count, depth)
    bits = wide_bits + deep_bits
    place = {WIDE: lax.axis_index(WIDE), DEEP: lax.axis_index(DEEP)}
    head = lax.axis_index("head")
    me = {b: (place[b[0]] // (1 << b[1])) % 2 for b in bits}
    x_bit, near = wide_bits[0], deep_bits[0]

    def partner(bit):
        axis, number = bit
        other = place[axis] + (1 - 2 * me[bit]) * (1 << number)
        return (head, other, place[DEEP]) if axis == WIDE else (head, place[WIDE], other)

    across = other_core()
    sems = (r.send_sem, r.recv_sem)
    loads = {}

    def fetch(target, name, slot):
        loads[name] = pltpu.make_async_copy(getattr(given, name), target, r.load_sem.at[slot])
        loads[name].start()

    order = {name: number for number, name in enumerate(loaded)}

    def fetch_all(**targets):
        for name, target in targets.items():
            fetch(target, name, order[name])

    def ready(*wanted):
        for name in wanted:
            if loads.get(name) is not None:
                loads[name].wait()
                loads[name] = None

    def tree_of(axes, left, acc, send, got, slots):
        return Tree(bit_order(axes, wide_bits, deep_bits), natural(left), acc, send, got, slots, me)

    up_a = tree_of("yxfn", bits, None, None, r.got_up_a, plan.up_a)
    up_b = tree_of("nxyf", bits, None, None, r.got_up_b, plan.up_b)
    share = width // wide_count
    per_share = share // block

    def runs(fixed):
        return picks(natural(wide_bits), {b: v for b, v in fixed.items() if b[0] == WIDE})

    def rows_of(run):
        return pl.ds(pl.multiple_of(run * share, share), share)

    half = sizes.hidden_units // 2
    keep, leave = me[x_bit], 1 - me[x_bit]
    meet(across, *[partner(b) for b in bits])
    beside = partner(near)
    early = [
        remote(given.att, r.att_in, sems, plan.att, partner(x_bit)),
        remote(given.gate_o, r.gate_o_in, sems, plan.gate_o, partner(x_bit)),
        remote(given.gates, r.gates_in, sems, plan.gates, beside),
    ]
    fetch_all(hid=r.hid)

    def run_rows(ref, run):
        count = per_share // 2
        return ref[pl.ds(pl.multiple_of(run * count, count), count)].reshape(share, rows)

    near_rows = blocks // 2 * block
    small = r.small
    near_other = 1 - me[near]
    crossing, gm_swap, ffn_swap, two_swap, act_swap, hid_swap = [], [], [], [], [], []

    def middle(att_ref, gate_ref, sig_ref, wo, cot, mixed_ref, gain, low_ref, ffn_own):
        fetch_all(att=att_ref, gate_o=gate_ref, wo=wo, cot=cot, gain_two=gain, sig_o=sig_ref)

        def feed(x, cot_first, bias, up, down, two_ref):
            fetch_all(x=x, cot_in=cot_first, bias_two=bias, w_up=up, w_down=down)
            ready("att", "gate_o", "wo")
            for h in range(heads):
                for e in range(experts):
                    at = h * experts + e
                    r.gated[at * dh:(at + 1) * dh, :] = (
                        gate_ref[at:at + 1, :] * att_ref[h].astype(F32)
                    ).astype(BF16)
            r.two_own[...] = mm(r.gated[...], wo[...], TN).astype(BF16)
            part_swap = remote(r.two_own, r.head_in, sems, plan.part, across)
            ready("cot", "cot_in", "x", "gain_two", "bias_two")
            r.cot_t[:, 0:rows] = cot[...].T
            r.cot_t[:, rows:] = cot_first[...].T
            part_swap.wait()
            mixed = x[...].astype(F32) + (r.two_own[...].astype(F32) + r.head_in[...].astype(F32))
            mixed_ref[...] = mixed
            normed, _ = normalize(mixed)
            two = (normed * gain[...] + bias[...]).astype(BF16)
            two_ref[...] = two
            r.two_t[...] = two.T.reshape(r.two_t.shape)
            hid_swap.append(
                remote(given.hid.at[:, near_other], r.hid_in, sems, plan.hid, lambda: partner(near))
            )
            ready("w_up", "w_down")
            chunk = half // 2
            for which, target in ((leave, r.act_out), (keep, r.act)):
                for part in range(2):
                    units = pl.ds(pl.multiple_of(which * half + part * chunk, chunk), chunk)
                    inner = slice(part * chunk, (part + 1) * chunk)
                    value, slope = gelu_both(mm(two_ref[...], up[:, units]))
                    if target is r.act:
                        target[:, inner] = value.astype(BF16)
                    else:
                        target[:, :, inner] = value.astype(BF16).reshape(target.shape[0], target.shape[1], chunk)
                    r.pre[which, :, inner] = (mm(cot[...], down[units, :], NT) * slope).astype(BF16)
                if target is r.act_out:
                    act_swap.append(remote(r.act_out, r.act_in, sems, plan.act, lambda: partner(x_bit)))
            for number, run in enumerate(runs(up_a.fixed(False))):
                piece = mm(run_rows(r.two_t, run), r.pre[0]).astype(BF16)
                for k in range(per_share):
                    r.up_a_out[number * per_share + k] = piece[k * block:(k + 1) * block]
            up_a.launch(sems, partner, r.up_a_out)
            piece = mm(r.two_t[:, 1 - me[near]].reshape(near_rows, rows), r.pre[1]).astype(BF16)
            for at in range(blocks // 2):
                r.up_b_out[at] = piece[at * block:(at + 1) * block]
            up_b.launch(sems, partner, r.up_b_out)
            total = None
            for k in range(2):
                term = mm(r.pre[k], up[:, k * half:(k + 1) * half], NT)
                total = term if total is None else total + term
            r.two_own[...] = total.astype(BF16)
            two_swap.append(remote(r.two_own, r.two_in, sems, plan.two, across))
            mine = mm(r.act[...], down[pl.ds(pl.multiple_of(keep * half, half), half), :])
            theirs = mm(
                r.act_out[...].reshape(rows, half), down[pl.ds(pl.multiple_of(leave * half, half), half), :]
            )
            ffn_own[...] = (mine + theirs).astype(BF16)
            ffn_swap.append(remote(ffn_own, r.ffn_in, sems, plan.ffn, across))

        pl.run_scoped(
            feed, pltpu.VMEM((rows, width), BF16), pltpu.VMEM((rows, width), BF16), pltpu.VMEM((1, width), F32),
            pltpu.VMEM((width, 2 * half), BF16), pltpu.VMEM((2 * half, width), BF16), pltpu.VMEM((rows, width), BF16),
        )

        def out_back():
            normed, inverse = normalize(mixed_ref[...])
            two_swap[0].wait()
            grad_two = r.two_own[...].astype(F32) + r.two_in[...].astype(F32)
            small[2:3, :] = jnp.sum(grad_two * normed, axis=0, keepdims=True)
            small[3:4, :] = jnp.sum(grad_two, axis=0, keepdims=True)
            grad_mixed = cot[...].astype(F32) + norm_back(grad_two * gain[...], normed, inverse)
            r.grad_mixed[...] = grad_mixed
            low_ref[...] = grad_mixed.astype(BF16)
            low_t = low_ref[...].T.reshape(wide_count // 2, 2, share, rows)
            first, second = low_t[:, 0], low_t[:, 1]
            r.gm_out[...] = jnp.where(me[x_bit] == 1, first, second)
            r.gm[...] = jnp.where(me[x_bit] == 1, second, first)
            gm_swap.append(remote(r.gm_out, r.gm_in, sems, plan.gm, lambda: partner(x_bit)))
            ready("sig_o")
            for h in range(heads):
                att = att_ref[h].astype(F32)
                total = None
                for e in range(experts):
                    at = h * experts + e
                    back = mm(wo[at * dh:(at + 1) * dh, :], low_ref[...], NT)
                    gate = gate_ref[at:at + 1, :]
                    grad_gate = jnp.sum(att * back, axis=0, keepdims=True)
                    r.logits[he + at:he + at + 1, :] = grad_gate * gate * (1.0 - sig_ref[at:at + 1, :])
                    total = gate * back if total is None else total + gate * back
                r.ga[h] = total.astype(BF16)
            ffn_swap[0].wait()
            ffn_own[...] = (mixed_ref[...] + (ffn_own[...].astype(F32) + r.ffn_in[...].astype(F32))).astype(BF16)
            pltpu.make_async_copy(ffn_own, r.output, r.load_sem.at[len(loaded)]).start()

        total_keys = 4 * rows
        chunk_shape = pltpu.VMEM((heads, dh, rows), BF16)
        pl.run_scoped(
            functools.partial(attention, out_back), pltpu.VMEM((heads, rows, total_keys), BF16), chunk_shape,
            chunk_shape, pltpu.VMEM((heads, dh, total_keys), BF16), *([chunk_shape] * 8),
            pltpu.VMEM((sizes.query_rows, sizes.query_rows), BF16), pltpu.VMEM((dh, total_keys), F32),
        )
        pltpu.make_async_copy(ffn_own, r.output, r.load_sem.at[len(loaded)]).wait()

    def attention(out_back, probs, qu, qv, rel, key_own, part_k, mem_k, part_mem_k, value_own, part_v, mem_v, part_mem_v, flip,
                  acc):
        fetch_all(
            probs=probs, qu=qu, qv=qv, rel=rel, key_own=key_own, part_k=part_k, mem_k=mem_k, part_mem_k=part_mem_k,
            value_own=value_own, part_v=part_v, mem_v=mem_v, part_mem_v=part_mem_v, flip=flip,
        )

        out_back()
        ready("probs", "qu", "qv", "rel", "key_own", "part_k", "mem_k", "part_mem_k")
        ready("value_own", "part_v", "mem_v", "part_mem_v", "flip")
        odd = place[DEEP] % 2 == 1
        size = sizes.query_rows
        for h in range(heads):
            k_one = jnp.where(odd, part_k[h], part_mem_k[h])
            v_one = jnp.where(odd, part_v[h], part_mem_v[h])
            keys = (part_mem_k[h], mem_k[h], k_one, key_own[h])
            values = (part_mem_v[h], mem_v[h], v_one, value_own[h])
            bias_u = bias_v = None
            for base in range(0, rows, size):
                here = slice(base, base + size)
                turned = mm(flip[...], probs[h, here, :])
                ga = mm(r.ga[h, :, here], flip[...]).astype(BF16)
                queries_u = mm(qu[h, :, here], flip[...]).astype(BF16)
                queries_v = mm(qv[h, :, here], flip[...]).astype(BF16)
                gp = jnp.concatenate([mm(ga, v, TN) for v in values], axis=1)
                weighted = turned * gp
                delta = jnp.sum(weighted, axis=1, keepdims=True)
                gs = ((weighted - turned * delta) * sizes.scale).astype(BF16)
                gk = mm(queries_u, gs[:, 2 * rows:])
                gv = mm(ga, turned[:, 2 * rows:].astype(BF16))
                gqu = None
                for i, k in enumerate(keys):
                    part = mm(k, gs[:, i * rows:(i + 1) * rows], NT)
                    gqu = part if gqu is None else gqu + part
                gpos = pltpu.roll(gs, rows - size - base, 1, stride=1, stride_axis=0)
                gqv = mm(rel[h], gpos, NT)
                grel = mm(queries_v, gpos)
                r.gq[h * dh:(h + 1) * dh, here] = mm((gqu + gqv).astype(BF16), flip[...]).astype(BF16)
                ones = jnp.ones((8, size), F32)
                sum_u, sum_v = [
                    lax.dot_general(ones, g, NT, precision=lax.Precision.HIGHEST, preferred_element_type=F32)
                    for g in (gqu, gqv)
                ]
                if base == 0:
                    r.gk[h] = gk
                    r.gv[h] = gv
                    acc[...] = grel
                    bias_u, bias_v = sum_u, sum_v
                else:
                    r.gk[h] += gk
                    r.gv[h] += gv
                    acc[...] += grel
                    bias_u, bias_v = bias_u + sum_u, bias_v + sum_v
            r.grel[h * dh:(h + 1) * dh, :] = acc[...].astype(BF16)
            r.small[4 + h:5 + h, 0:dh] = bias_u[0:1]
            r.small[4 + heads + h:5 + heads + h, 0:dh] = bias_v[0:1]
        r.cross_out[0] = r.gk[:, :, :rows].astype(BF16)
        r.cross_out[1] = r.gv[:, :, :rows].astype(BF16)
        crossing.append(remote(r.cross_out, r.cross_in, sems, plan.cross, lambda: partner(near)))

    hd_up = sizes.hd_up
    small[4:8, :] = jnp.zeros((4, width), F32)
    tokens_of = pltpu.VMEM((heads, dh, rows), BF16)
    pl.run_scoped(
        middle, tokens_of, pltpu.VMEM((he, rows), F32), pltpu.VMEM((he, rows), F32), pltpu.VMEM((hed, width), BF16),
        pltpu.VMEM((rows, width), BF16), pltpu.VMEM((rows, width), F32), pltpu.VMEM((1, width), F32),
        pltpu.VMEM((rows, width), BF16), pltpu.VMEM((rows, width), BF16),
    )

    def rest(*held):
        b = types.SimpleNamespace(**dict(zip(sizes.late_names, held)))
        fetch_all(each=b.each, sigs=b.sigs, gates=b.gates, wv=b.wv, wq=b.wq, wk=b.wk, rt=b.rt, x=b.x, gain=b.gain)
        up_a.acc, up_a.send, up_b.acc, up_b.send = r.act_out, b.send_up_a, b.acc_up_b, b.send_up_b
        far = [v for v in bits if v != near]
        out = tree_of("ynf", [v for v in bits if v != x_bit], b.acc_out, b.send_out, r.got_out, plan.out)
        value = tree_of("xyf", far, b.acc_value, b.send_value, r.got_value, plan.value)
        query = tree_of("xynf", bits, b.acc_query, b.send_query, r.got_query, plan.query)
        down = tree_of("yfn", bits, r.up_b_out, r.up_a_out, r.got_down, plan.down)
        half_count = len(wide_bits) // 2
        for tree in (out, down):
            tree.order = tree.order[:half_count] + wide_bits[1:half_count] + tree.order[half_count:]
        state = []

        def down_part(own):
            for number, run in enumerate(runs(down.fixed(own))):
                at_rows = rows_of(run)
                part = mm(r.cot_t[at_rows, 0:rows], r.act[...]) + mm(
                    r.cot_t[at_rows, rows:], r.act_in[...].reshape(rows, half)
                )
                for k in range(per_share):
                    at = number * per_share + k
                    piece = part[k * block:(k + 1) * block]
                    if own:
                        down.acc[at] = piece.astype(BF16)
                    else:
                        down.send[at] = piece.astype(BF16)
            if own:
                down.step()
            else:
                down.launch(sems, partner)

        def up_a_keep():
            for number, run in enumerate(runs(up_a.fixed(True))):
                part = mm(run_rows(r.two_t, run), r.pre[0])
                for k in range(per_share):
                    up_a.acc[number * per_share + k] = part[k * block:(k + 1) * block].astype(BF16)
            up_a.step()

        def up_b_keep():
            part = mm(r.two_t[:, me[near]].reshape(near_rows, rows), r.pre[1])
            for at in range(blocks // 2):
                up_b.acc[at] = part[at * block:(at + 1) * block].astype(BF16)
            up_b.step()

        def out_part():
            mine = mm(r.gm[...].reshape(near_rows, rows), r.gated[...], NT)
            for at in range(blocks // 2):
                out.acc[at] = mine[at * block:(at + 1) * block].astype(BF16)
            early[0].wait()
            early[1].wait()
            for h in range(heads):
                for e in range(experts):
                    at = h * experts + e
                    r.gated[at * dh:(at + 1) * dh, :] = (
                        r.gate_o_in[at:at + 1, :] * r.att_in[h].astype(F32)
                    ).astype(BF16)
            gm_swap[0].wait()
            theirs = mm(r.gm_in[...].reshape(near_rows, rows), r.gated[...], NT)
            for at in range(blocks // 2):
                out.acc[at] = (out.acc[at].astype(F32) + theirs[at * block:(at + 1) * block]).astype(BF16)
            out.advance(sems, partner)

        def own_part():
            ready("each", "sigs", "gates")
            crossing[0].wait()
            even = jnp.where(place[DEEP] % 2 == 0, 1.0, 0.0)
            for h in range(heads):
                gk = r.gk[h, :, rows:] + even * r.cross_in[0, h].astype(F32)
                gv = r.gv[h, :, rows:] + even * r.cross_in[1, h].astype(F32)
                b.own_out[h * dh:(h + 1) * dh, :] = gv.astype(BF16)
                b.own_out[hd + h * dh:hd + (h + 1) * dh, :] = gk.astype(BF16)
                for e in range(experts):
                    at = h * experts + e
                    gate = b.gates[at:at + 1, :]
                    grad_gate = jnp.sum(gv * b.each[at * dh:(at + 1) * dh, :].astype(F32), axis=0, keepdims=True)
                    r.logits[at:at + 1, :] = grad_gate * gate * (1.0 - b.sigs[at:at + 1, :])
                    b.grads[at * dh:(at + 1) * dh, :] = (gate * gv).astype(BF16)
            tail = b.own_out.shape[0] - 2 * hd
            logits = jnp.concatenate([r.logits[0:2 * he, :], jnp.zeros((tail - 2 * he, rows), F32)], axis=0)
            b.own_out[2 * hd:, :] = logits.astype(BF16)
            state_own.append(remote(b.own_out, r.own_in, sems, plan.own, partner(near)))
            b.grads[hed:, :] = b.own_out[hd:, :]

        def hidden_part():
            ready("wv", "wq", "wk", "rt")
            grad_hidden = mm(b.grads[0:hed, :], b.wv[...], TN)
            grad_hidden += mm(r.gq[...], b.wq[...], TN)
            grad_hidden += mm(b.grads[hed:hed + hd, :], b.wk[...], TN)
            grad_hidden += mm(b.grads[hed + hd:hed + hd + 2 * he, :], b.rt[...], TN)
            r.two_own[...] = grad_hidden.astype(BF16)
            state_head.append(remote(r.two_own, r.head_in, sems, plan.head, across))

        def norm_part():
            ready("x", "gain")
            state_head[0].wait()
            grad_hidden = r.two_own[...].astype(F32) + r.head_in[...].astype(F32)
            normed, inverse = normalize(b.x[...].astype(F32))
            small[0:1, :] = jnp.sum(grad_hidden * normed, axis=0, keepdims=True)
            small[1:2, :] = jnp.sum(grad_hidden, axis=0, keepdims=True)
            state.append(remote(small, r.small_in.at[0], sems, plan.small[0], partner(bits[0])))
            r.grad_mixed[...] += norm_back(grad_hidden * b.gain[...], normed, inverse)
            input_copy = pltpu.make_async_copy(r.grad_mixed, r.grad_input, r.load_sem.at[len(loaded) + 1])
            input_copy.start()
            state_input.append(input_copy)

        def small_step():
            at = len(state) - 1
            if at == len(bits):
                return
            state[at].wait()
            small[...] = small[...] + r.small_in[at]
            state.append(
                None if at + 1 == len(bits)
                else remote(small, r.small_in.at[at + 1], sems, plan.small[at + 1], partner(bits[at + 1]))
            )

        def value_own():
            ready("hid")
            mine = mm(r.hid[:, me[near]].reshape(near_rows, rows), b.grads[...], NT)
            for at in range(blocks // 2):
                value.acc[at] = mine[at * block:(at + 1) * block]

        def value_part():
            early[2].wait()
            hid_swap[0].wait()
            state_own[0].wait()
            for at in range(he):
                h = at // experts
                b.grads[at * dh:(at + 1) * dh, :] = (
                    r.gates_in[at:at + 1, :] * r.own_in[h * dh:(h + 1) * dh, :].astype(F32)
                ).astype(BF16)
            b.grads[hed:, :] = r.own_in[hd:, :]
            theirs = mm(r.hid_in[...].reshape(near_rows, rows), b.grads[...], NT)
            for at in range(blocks // 2):
                value.acc[at] += theirs[at * block:(at + 1) * block]
            value.advance(sems, partner)

        def table_copy(number, run):
            return pltpu.make_async_copy(
                given.table.at[rows_of(run)], b.table.at[pl.ds(number * share, share)], r.table_sem.at[number]
            )

        for number, run in enumerate(runs(query.fixed(False))):
            table_copy(number, run).start()

        def query_part(own):
            if not own and hd_up > hd:
                for at in range(blocks // 2):
                    query.send[at, :, hd:hd_up] = jnp.zeros((block, hd_up - hd), BF16)
                    query.acc[at, :, hd:hd_up] = jnp.zeros((block, hd_up - hd), BF16)
            ready("hid")
            for number, run in enumerate(runs(query.fixed(own))):
                table_copy(number, run).wait()
                part = mm(run_rows(r.hid, run), r.gq[...], NT)
                part_rel = mm(b.table[number * share:(number + 1) * share, :], r.grel[...], NT)
                for k in range(per_share):
                    at = number * per_share + k
                    piece, piece_rel = part[k * block:(k + 1) * block], part_rel[k * block:(k + 1) * block]
                    if own:
                        query.acc[at, :, 0:hd] = piece.astype(BF16)
                        query.acc[at, :, hd_up:] = piece_rel.astype(BF16)
                    else:
                        query.send[at, :, 0:hd] = piece.astype(BF16)
                        query.send[at, :, hd_up:] = piece_rel.astype(BF16)
            if own:
                query.step()
            else:
                query.launch(sems, partner)
                for number, run in enumerate(runs(query.fixed(True))):
                    table_copy(number, run).start()

        state_own, state_head, state_input = [], [], []
        def half_part():
            down.arrive()
            r.half_out[...] = down.finish(leave).astype(BF16)
            state_own.append(remote(r.half_out, r.half_in, sems, plan.half, partner(x_bit)))
            r.g_down[:, pl.ds(pl.multiple_of(keep * half, half), half)] = down.finish(keep)

        def next_level(tree):
            if tree.level < len(tree.order):
                tree.advance(sems, partner)

        act_swap[0].wait()
        up_a_keep()
        next_level(up_a)
        down_part(False)
        own_part()
        up_b_keep()
        next_level(up_b)
        next_level(up_a)
        down_part(True)
        query_part(False)
        value_own()
        query_part(True)
        out_part()
        next_level(down)
        hidden_part()
        next_level(up_a)
        value_part()
        next_level(up_b)
        next_level(out)
        norm_part()
        next_level(query)
        next_level(query)
        next_level(up_b)
        next_level(down)
        next_level(value)
        small_step()
        next_level(out)
        next_level(query)
        small_step()
        next_level(value)
        half_part()
        small_step()
        while len(state) <= len(bits):
            small_step()
        r.small_out[...] = small[...]
        for number, tree in enumerate((up_a, up_b)):
            tree.arrive()
            r.g_up[:, number * half:(number + 1) * half] = tree.finish()
        out.arrive()
        total = out.finish()
        for at in range(he):
            r.g_out[at] = total[:, at * dh:(at + 1) * dh]
        value.arrive()
        total = value.finish()
        for at in range(he):
            r.g_value[at] = total[:, at * dh:(at + 1) * dh]
        for h in range(heads):
            r.g_key[:, h, :] = total[:, hed + h * dh:hed + (h + 1) * dh]
        r.g_router[...] = total[:, hed + hd:hed + hd + 2 * he]
        query.arrive()
        total = query.finish()
        for h in range(heads):
            r.g_query[:, h, :] = total[:, h * dh:(h + 1) * dh]
            r.g_rel[:, h, :] = total[:, hd_up + h * dh:hd_up + (h + 1) * dh]
        state_own[1].wait()
        r.g_down[:, pl.ds(pl.multiple_of(leave * half, half), half)] = r.half_in[...].astype(F32)
        state_input[0].wait()

    pl.run_scoped(rest, *sizes.late_scratch)


def late_call(inputs, sizes):
    wide_bits, deep_bits = bit_names(sizes.wide, sizes.deep)
    bits = len(wide_bits) + len(deep_bits)
    blocks = sizes.wide * sizes.deep
    block, rows, width, heads, dh = sizes.block, sizes.rows, sizes.width, sizes.heads, sizes.dh
    he, hd = heads * sizes.experts, heads * dh
    hed, half = he * dh, sizes.hidden_units // 2
    tail = 32
    sizes.hd_up = -(-hd // 128) * 128
    sizes.value_n = hed + hd + tail
    query_n = sizes.hd_up + hd
    count = 15 + 7 * bits
    slots = iter(range(count))

    def levels():
        return [next(slots) for _ in range(bits)]

    plan = types.SimpleNamespace(
        two=next(slots), ffn=next(slots), act=next(slots), gm=next(slots), cross=next(slots), part=next(slots),
        att=next(slots), gate_o=next(slots), gates=next(slots), hid=next(slots),
        own=next(slots), head=next(slots), half=next(slots), small=levels(), up_a=levels(), up_b=levels(),
        out=levels(), query=levels(), down=levels(), value=levels(),
    )

    def got(n, start, stop):
        return [pltpu.VMEM((blocks >> (level + 1), block, n), BF16) for level in range(start, stop)]

    def taken(name):
        return pltpu.VMEM(inputs[name].shape, inputs[name].dtype)

    sem = pltpu.SemaphoreType.DMA
    token_rows = pltpu.VMEM((rows, width), BF16)
    near_half = pltpu.VMEM((blocks // 2, block, rows), BF16)
    x_half = pltpu.VMEM((sizes.wide // 2, width // sizes.wide, rows), BF16)
    first_half = pltpu.VMEM((blocks // 2, block, half), BF16)
    scratch = dict(
        act=pltpu.VMEM((rows, half), BF16), hid=taken("hid"), two_t=taken("hid"),
        pre=pltpu.VMEM((2, rows, half), BF16), cot_t=pltpu.VMEM((width, 2 * rows), BF16),
        gated=pltpu.VMEM((hed, rows), BF16), att_in=taken("att"), gate_o_in=taken("gate_o"), gates_in=taken("gates"),
        two_own=token_rows, two_in=token_rows, ffn_in=token_rows, head_in=token_rows,
        act_in=first_half, act_out=first_half, up_a_out=first_half, up_b_out=first_half,
        hid_in=near_half, gm=x_half, gm_in=x_half, gm_out=x_half,
        grad_mixed=pltpu.VMEM((rows, width), F32), table_sem=sem((sizes.wide // 2,)),
        small=pltpu.VMEM((8, width), F32), small_in=pltpu.VMEM((bits, 8, width), F32),
        logits=pltpu.VMEM((2 * he, rows), F32), ga=pltpu.VMEM((heads, dh, rows), BF16),
        gq=pltpu.VMEM((hd, rows), BF16), gk=pltpu.VMEM((heads, dh, 2 * rows), F32),
        gv=pltpu.VMEM((heads, dh, 2 * rows), F32), grel=pltpu.VMEM((hd, 4 * rows), BF16),
        cross_out=pltpu.VMEM((2, heads, dh, rows), BF16), cross_in=pltpu.VMEM((2, heads, dh, rows), BF16),
        own_in=pltpu.VMEM((2 * hd + tail, rows), BF16), half_in=pltpu.VMEM((block, half), BF16),
        half_out=pltpu.VMEM((block, half), BF16),
        got_up_a=got(half, 0, bits), got_up_b=got(half, 0, bits), got_out=got(hed, 1, bits),
        got_query=got(query_n, 0, bits), got_down=got(half, 0, bits - 1), got_value=got(sizes.value_n, 1, bits),
        load_sem=sem((len(inputs) + 3,)), send_sem=sem((count,)), recv_sem=sem((count,)),
    )
    late = dict(
        send_out=pltpu.VMEM((blocks >> 2, block, hed), BF16), acc_out=pltpu.VMEM((blocks >> 1, block, hed), BF16),
        table=pltpu.VMEM((width // 2, 4 * rows), BF16), each=taken("each"), sigs=taken("sigs"), gates=taken("gates"), wv=taken("wv"),
        wq=taken("wq"), wk=taken("wk"), rt=taken("rt"), x=taken("x"), gain=taken("gain"),
        own_out=pltpu.VMEM((2 * hd + tail, rows), BF16), grads=pltpu.VMEM((sizes.value_n, rows), BF16),
        send_up_a=pltpu.VMEM((blocks >> 2, block, half), BF16), send_up_b=pltpu.VMEM((blocks >> 2, block, half), BF16),
        acc_up_b=pltpu.VMEM((blocks >> 1, block, half), BF16),
        send_query=pltpu.VMEM((blocks >> 1, block, query_n), BF16),
        acc_query=pltpu.VMEM((blocks >> 1, block, query_n), BF16),
        send_value=pltpu.VMEM((blocks >> 2, block, sizes.value_n), BF16),
        acc_value=pltpu.VMEM((blocks >> 1, block, sizes.value_n), F32),
    )
    sizes.late_names, sizes.late_scratch = list(late), list(late.values())
    outs = dict(
        g_down=((block, 2 * half), F32), g_up=((block, 2 * half), F32), g_out=((he, block, dh), F32),
        g_value=((he, block, dh), F32), g_query=((block, heads, dh), F32), g_key=((block, heads, dh), F32),
        g_rel=((block, heads, dh), F32), g_router=((block, 2 * he), F32), small_out=((8, width), F32),
        grad_input=((rows, width), F32), output=((rows, width), BF16),
    )
    flat, tree = jax.tree.flatten(list(scratch.values()))

    def kernel(*refs):
        held = jax.tree.unflatten(tree, refs[len(inputs) + len(outs):])
        late_kernel(
            *refs[:len(inputs) + len(outs)], *held, names=[None] * 0 + [n + "_" for n in inputs] + list(outs) + list(scratch),
            loaded=list(inputs), sizes=sizes, plan=plan,
        )

    vmem, anywhere = pl.BlockSpec(memory_space=pltpu.VMEM), pl.BlockSpec(memory_space=pl.ANY)
    results = pl.pallas_call(
        kernel,
        in_specs=[anywhere] * len(inputs),
        out_specs=[vmem] * (len(outs) - 2) + [anywhere] * 2,
        out_shape=[jax.ShapeDtypeStruct(shape, dtype) for shape, dtype in outs.values()],
        scratch_shapes=flat,
        compiler_params=pltpu.CompilerParams(collective_id=0, has_side_effects=True, vmem_limit_bytes=60 << 20),
        cost_estimate=pl.CostEstimate(flops=4 * 10**10, bytes_accessed=10**8, transcendentals=0),
    )(*inputs.values())
    return types.SimpleNamespace(**dict(zip(outs, results)))


def body(
    layer_input, mem_keys, mem_values, route_value, route_output, ln1_gain, ln1_bias, w_query, w_key, w_rel,
    content_bias, position_bias, w_value, w_out, router_value, router_output, ln2_gain, ln2_bias, w_up, w_down,
    cotangent,
):
    rows, width = layer_input.shape
    heads, dh = content_bias.shape
    experts = w_value.shape[1]
    odd = (lax.axis_index("dp") % 2).astype(jnp.int32)
    scale = 1.0 / math.sqrt(dh)
    total_keys = 4 * rows
    block = rows // 2
    hd = heads * dh
    hed = heads * experts * dh

    wq = jnp.transpose(w_query, (1, 2, 0)).reshape(hd, width)
    wk = jnp.transpose(w_key, (1, 2, 0)).reshape(hd, width)
    wr = jnp.transpose(w_rel, (1, 2, 0)).reshape(hd, width)
    wv = jnp.transpose(w_value, (0, 1, 3, 2)).reshape(hed, width)
    wo = w_out.reshape(hed, width)
    rt = jnp.concatenate(
        [jnp.transpose(r, (1, 2, 0)).reshape(heads * experts, width) for r in (router_value, router_output)], axis=0
    )
    mem_k = jnp.transpose(mem_keys, (1, 2, 0))
    mem_v = jnp.transpose(mem_values, (1, 2, 0))
    rv = jnp.transpose(route_value, (0, 2, 1))
    ro = jnp.transpose(route_output, (0, 2, 1))
    rt = jnp.concatenate(
        [jnp.transpose(r, (1, 2, 0)).reshape(heads * experts, width) for r in (router_value, router_output)], axis=0
    )
    table = jnp.asarray(position_table(total_keys, width))
    first = early_call(dict(
        x=layer_input, gain=ln1_gain.reshape(1, width), bias=ln1_bias.reshape(1, width), wk=wk, rt=rt, rv=rv, ro=ro,
        wv=wv, wq=wq, cb=content_bias, pb=position_bias, wr=wr, table=table, mem_k=mem_k, mem_v=mem_v, cot=cotangent,
    ), types.SimpleNamespace(
        heads=heads, experts=experts, dh=dh, rows=rows, width=width, wide=lax.axis_size(WIDE),
        deep=lax.axis_size(DEEP), scale=scale, query_rows=block,
    ))
    att, gate_v, gate_o, sig_v, sig_o, hid = first.att, first.gate_v, first.gate_o, first.sig_v, first.sig_o, first.hid
    wide_count, depth = lax.axis_size(WIDE), lax.axis_size(DEEP)
    blocks = wide_count * depth
    block_rows, he = width // blocks, heads * experts
    hidden_units = w_up.shape[1]
    wide_bits, deep_bits = bit_names(wide_count, depth)
    gain_two, bias_two = ln2_gain.reshape(1, width), ln2_bias.reshape(1, width)
    sem = pltpu.SemaphoreType.DMA

    def shapes(*pairs):
        return [jax.ShapeDtypeStruct(shape, dtype) for shape, dtype in pairs]

    flip = jnp.asarray(np.eye(block, dtype=np.float32)[::-1].astype(BF16))
    inputs = dict(
        hid=hid, gates=gate_v, cot=cotangent, cot_in=first.cot_in, gain_two=gain_two, bias_two=bias_two, w_up=w_up,
        w_down=w_down, att=att, gate_o=gate_o, sig_o=sig_o, wo=wo,
        flip=flip, probs=first.probs, qu=first.qu, qv=first.qv, rel=first.rel,
        key_own=first.key_own, part_k=first.part_k, mem_k=mem_k, part_mem_k=first.part_mem_k,
        value_own=first.value_own, part_v=first.part_v, mem_v=mem_v, part_mem_v=first.part_mem_v,
        table=table, sigs=sig_v, each=first.each, wv=wv, wq=wq, wk=wk, rt=rt,
        x=layer_input, gain=ln1_gain.reshape(1, width),
    )
    done = late_call(inputs, types.SimpleNamespace(
        heads=heads, experts=experts, dh=dh, rows=rows, width=width, wide=wide_count, deep=depth, block=block_rows,
        hidden_units=hidden_units, scale=scale, query_rows=block,
    ))
    start = (lax.axis_index(WIDE) * depth + lax.axis_index(DEEP)) * block_rows
    ln = lax.dynamic_slice_in_dim(done.small_out, start, block_rows, axis=1)
    biases = done.small_out[4:, :dh].reshape(2, heads, dh)
    routers = done.g_router.reshape(block_rows, 2, heads, experts)

    output, grad_input, g_query, g_key, g_rel, g_value, g_out, g_up, g_down = finished(
        done.output, done.grad_input, done.g_query, done.g_key, done.g_rel, done.g_value, done.g_out, done.g_up,
        done.g_down,
    )

    def by_expert(values):
        return values.reshape(heads, experts, block_rows, dh)

    return (
        output, grad_input, ln[0], ln[1], g_query, g_key, g_rel, biases[0], biases[1],
        by_expert(g_value), jnp.transpose(by_expert(g_out), (0, 1, 3, 2)), routers[:, 0], routers[:, 1],
        ln[2], ln[3], g_up, jnp.transpose(g_down),
    )


def solution(mesh):
    tokens = ("wide", "dp")
    return jax.shard_map(
        body,
        mesh=mesh,
        in_specs=(
            P(tokens, None), P(tokens, "head", None), P(tokens, "head", None), P("head", tokens, None),
            P("head", tokens, None), P(), P(), P(None, "head", None), P(None, "head", None), P(None, "head", None),
            P("head", None), P("head", None), P("head", None, None, None), P("head", None, None, None),
            P(None, "head", None), P(None, "head", None), P(), P(), P(None, "head"), P("head", None), P(tokens, None),
        ),
        out_specs=(
            P(tokens, None), P(tokens, None), P(tokens), P(tokens), P(tokens, "head", None), P(tokens, "head", None),
            P(tokens, "head", None), P("head", None), P("head", None), P("head", None, tokens, None),
            P("head", None, None, tokens), P(tokens, "head", None), P(tokens, "head", None), P(tokens), P(tokens),
            P(tokens, "head"), P("head", tokens),
        ),
        check_vma=False,
    )
```

```python
import functools
import math
import types

import jax
import jax.numpy as jnp
import numpy as np
from jax import lax
from jax.experimental import pallas as pl
from jax.experimental.pallas import tpu as pltpu
from jax.sharding import PartitionSpec as P

EPSILON = 1e-05
NEG_LARGE = -1e30
F32 = jnp.float32
BF16 = jnp.bfloat16
WIDE, DEEP = "wide", "dp"

NN = (((1,), (0,)), ((), ()))
NT = (((1,), (1,)), ((), ()))
TN = (((0,), (0,)), ((), ()))


def mm(a, b, dims=NN):
    return lax.dot_general(a, b, dims, preferred_element_type=F32)


def normalize(values):
    row_mean = jnp.mean(values, axis=-1, keepdims=True)
    centered = values - row_mean
    variance = jnp.mean(centered * centered, axis=-1, keepdims=True)
    inverse = lax.rsqrt(variance + EPSILON)
    return (centered * inverse, inverse)


def norm_back(grad_normed, normed, inverse):
    first_mean = jnp.mean(grad_normed, axis=-1, keepdims=True)
    second_mean = jnp.mean(grad_normed * normed, axis=-1, keepdims=True)
    return inverse * (grad_normed - first_mean - normed * second_mean)


def position_table(extent, model_width):
    half_width = model_width // 2
    frequencies = np.exp(
        np.arange(half_width, dtype=np.float32) * np.float32(-2.0 * math.log(10000.0) / model_width)
    ).astype(np.float32)
    distance = np.arange(extent - 1, -1, -1).astype(np.float32)
    angles = (frequencies[:, None] * distance[None, :]).astype(np.float64)
    return np.concatenate([np.sin(angles), np.cos(angles)], axis=0).astype(np.float32).astype(BF16)


def whole(array):
    return pl.BlockSpec(array.shape, lambda *_: (0,) * len(array.shape))


def gelu_both(x):
    c = math.sqrt(2.0 / math.pi)
    square = x * x
    t = jnp.tanh(c * x * (1.0 + 0.044715 * square))
    half = 0.5 * (1.0 + t)
    return x * half, half + 0.5 * x * (1.0 - t * t) * (c * (1.0 + 3.0 * 0.044715 * square))


def meet(*devices):
    barrier = pltpu.get_barrier_semaphore()
    for device in devices:
        pl.semaphore_signal(barrier, inc=1, device_id=device, device_id_type=pl.DeviceIdType.MESH)
    pl.semaphore_wait(barrier, len(devices))


def other_core():
    return (1 - lax.axis_index("head"), lax.axis_index("wide"), lax.axis_index("dp"))


class Swap:
    def __init__(self, src, dst, sems, slot, device):
        self.parts = (src, dst, sems, slot, device)
        self.copy().start()

    def copy(self):
        src, dst, sems, slot, device = self.parts
        return pltpu.make_async_remote_copy(
            src_ref=src, dst_ref=dst, send_sem=sems[0].at[slot], recv_sem=sems[1].at[slot],
            device_id=device() if callable(device) else device, device_id_type=pl.DeviceIdType.MESH,
        )

    def wait(self):
        self.copy().wait()


remote = Swap


def early_kernel(*refs, given_names, out_names, held_names, sizes):
    count = len(given_names)
    given = types.SimpleNamespace(**dict(zip(given_names, refs)))
    out = types.SimpleNamespace(**dict(zip(out_names, refs[count:])))
    r = types.SimpleNamespace(**dict(zip(held_names, refs[count + len(out_names):])))
    heads, experts, dh, rows, width = sizes.heads, sizes.experts, sizes.dh, sizes.rows, sizes.width
    deep, wide = lax.axis_index(DEEP), lax.axis_index(WIDE)
    near = deep % 2
    beside = (lax.axis_index("head"), wide, deep + 1 - 2 * near)
    across = (lax.axis_index("head"), wide + 1 - 2 * (wide % 2), deep)
    sems = (r.send_sem, r.recv_sem)
    loads, writes = {}, []

    def fetch(*names):
        for name in names:
            slot = given_names.index(name)
            loads[name] = pltpu.make_async_copy(getattr(given, name), getattr(r, name), r.load_sem.at[slot])
            loads[name].start()

    def ready(*names):
        for name in names:
            loads[name].wait()

    def put(name, source, *at):
        target = getattr(out, name)
        if at:
            source, target = source.at[at], target.at[at]
        writes.append(pltpu.make_async_copy(source, target, r.write_sem.at[len(writes)]))
        writes[-1].start()

    fetch(*sizes.loaded)
    meet(beside, across)
    mem_k_swap = Swap(given.mem_k, r.part_mem_k, sems, 0, beside)
    cot_swap = Swap(given.cot, out.cot_in, sems, 2, across)
    ready("x", "gain", "bias")
    normed, _ = normalize(r.x[...].astype(F32))
    hid = (normed * r.gain[...] + r.bias[...]).astype(BF16)
    r.hid[...] = hid
    ready("wk")
    for h in range(heads):
        r.key_own[h] = mm(r.wk[h * dh:(h + 1) * dh, :], r.hid[...], NT).astype(BF16)
    key_swap = Swap(r.key_own, r.part_k, sems, 3, beside)
    ready("router_v", "router_o", "rv", "ro")
    lines = []
    for router in (r.router_v, r.router_o):
        given_lines = [router[e].astype(F32) for e in range(experts)]
        lines += [given_lines[e][h:h + 1] for h in range(heads) for e in range(experts)]
    r.rt[...] = jnp.concatenate(lines, axis=0).astype(BF16)
    put("rt", r.rt)
    logits = mm(r.rt[...], r.hid[...], NT)
    sig = 1.0 / (1.0 + jnp.exp(-logits))
    masks = []
    for routes in (r.rv, r.ro):
        for h in range(heads):
            for e in range(experts):
                hit = (routes[h, 0:1, :] == e) | (routes[h, 1:2, :] == e)
                masks.append(jnp.where(hit, 1.0, 0.0))
    gate = sig * jnp.concatenate(masks, axis=0)
    he = heads * experts
    r.gate[...] = gate
    out.gate_v[...] = gate[:he]
    out.gate_o[...] = gate[he:]
    out.sig_v[...] = sig[:he]
    out.sig_o[...] = sig[he:]
    ready("wv")
    for h in range(heads):
        total = None
        for e in range(experts):
            at = h * experts + e
            each = mm(r.wv[at * dh:(at + 1) * dh, :], r.hid[...], NT)
            r.each[at * dh:(at + 1) * dh, :] = each.astype(BF16)
            term = r.gate[at:at + 1, :] * each
            total = term if total is None else total + term
        r.value_own[h] = total.astype(BF16)
    mem_v_swap = Swap(given.mem_v, r.part_mem_v, sems, 1, beside)
    value_swap = Swap(r.value_own, r.part_v, sems, 4, beside)
    put("each", r.each)
    put("key_own", r.key_own)
    put("value_own", r.value_own)
    ready("wq", "cb", "pb")
    eye = (
        lax.broadcasted_iota(jnp.int32, (dh, dh), 0) == lax.broadcasted_iota(jnp.int32, (dh, dh), 1)
    ).astype(F32)

    def column(row):
        spread = jnp.broadcast_to(row, (8, dh))
        return lax.dot_general(
            eye, spread, NT, precision=lax.Precision.HIGHEST, preferred_element_type=F32
        )[:, 0:1]

    for h in range(heads):
        queries = mm(r.wq[h * dh:(h + 1) * dh, :], r.hid[...], NT)
        r.qu[h] = (queries + column(r.cb[h:h + 1, :])).astype(BF16)
        r.qv[h] = (queries + column(r.pb[h:h + 1, :])).astype(BF16)
    put("qu", r.qu)
    put("qv", r.qv)
    ready("wr", "table")
    for h in range(heads):
        r.rel[h] = mm(r.wr[h * dh:(h + 1) * dh, :], r.table[...]).astype(BF16)
    put("rel", r.rel)
    r.hid_t[...] = r.hid[...].T.reshape(r.hid_t.shape)
    put("hid", r.hid_t)
    total_keys, size = 4 * rows, sizes.query_rows
    for h in range(heads):
        for base in range(0, rows, size):
            here = slice(base, base + size)
            positional = mm(r.qv[h, :, here], r.rel[h], TN)
            r.scores[h, here, :] = pltpu.roll(
                positional, total_keys - rows + 1 + base, 1, stride=1, stride_axis=0
            )
    odd = near == 1
    ready("mem_k", "mem_v")
    mem_k_swap.wait()
    key_swap.wait()
    put("part_k", r.part_k)
    put("part_mem_k", r.part_mem_k)
    first = jnp.where(odd, 0, rows)
    for h in range(heads):
        k_one = jnp.where(odd, r.part_k[h], r.part_mem_k[h])
        keys = (r.part_mem_k[h], r.mem_k[h], k_one, r.key_own[h])
        for base in range(0, rows, size):
            here = slice(base, base + size)
            content = jnp.concatenate([mm(r.qu[h, :, here], k, TN) for k in keys], axis=1)
            row = lax.broadcasted_iota(jnp.int32, (size, total_keys), 0) + base
            col = lax.broadcasted_iota(jnp.int32, (size, total_keys), 1)
            visible = (col <= row + (total_keys - rows)) & (col >= first)
            scores = jnp.where(visible, (content + r.scores[h, here, :]) * sizes.scale, NEG_LARGE)
            peak = jnp.max(scores, axis=1, keepdims=True)
            exponents = jnp.exp(scores - peak)
            total = jnp.sum(exponents, axis=1, keepdims=True)
            probs = (exponents * (1.0 / total)).astype(BF16)
            r.probs[h, here, :] = probs
            put("probs", r.probs, h, pl.ds(base, size))
    mem_v_swap.wait()
    value_swap.wait()
    put("part_v", r.part_v)
    put("part_mem_v", r.part_mem_v)
    for h in range(heads):
        v_one = jnp.where(odd, r.part_v[h], r.part_mem_v[h])
        values = (r.part_mem_v[h], r.mem_v[h], v_one, r.value_own[h])
        att = None
        for i, v in enumerate(values):
            term = mm(v, r.probs[h, :, i * rows:(i + 1) * rows], NT)
            att = term if att is None else att + term
        out.att[h] = att.astype(BF16)
    cot_swap.wait()
    for write in writes:
        write.wait()


def early_call(inputs, sizes):
    heads, experts, dh, rows, width = sizes.heads, sizes.experts, sizes.dh, sizes.rows, sizes.width
    he, hed, hd = heads * experts, heads * experts * dh, heads * dh
    tokens = (heads, dh, rows)
    blocks = sizes.wide * sizes.deep
    hid_shape = (blocks // 2, 2, width // blocks, rows)
    anywhere = dict(
        each=((hed, rows), BF16), key_own=(tokens, BF16), value_own=(tokens, BF16), qu=(tokens, BF16),
        qv=(tokens, BF16), rel=((heads, dh, 4 * rows), BF16), hid=(hid_shape, BF16), part_k=(tokens, BF16),
        part_v=(tokens, BF16), part_mem_k=(tokens, BF16), part_mem_v=(tokens, BF16),
        probs=((heads, rows, 4 * rows), BF16), rt=((2 * he, width), BF16), cot_in=((rows, width), BF16),
    )
    near = dict(
        att=(tokens, BF16), gate_v=((he, rows), F32), gate_o=((he, rows), F32), sig_v=((he, rows), F32),
        sig_o=((he, rows), F32),
    )
    outs = {**anywhere, **near}
    sem = pltpu.SemaphoreType.DMA
    sizes.loaded = [name for name in inputs if name != "cot"]
    held = {name: pltpu.VMEM(inputs[name].shape, inputs[name].dtype) for name in sizes.loaded}
    held.update({name: pltpu.VMEM(shape, dtype) for name, (shape, dtype) in anywhere.items() if name != "cot_in"})
    held.update(
        hid=pltpu.VMEM((rows, width), BF16), hid_t=pltpu.VMEM(hid_shape, BF16),
        scores=pltpu.VMEM((heads, rows, 4 * rows), F32), gate=pltpu.VMEM((2 * he, rows), F32),
        load_sem=sem((len(inputs),)), write_sem=sem((24,)), send_sem=sem((5,)), recv_sem=sem((5,)),
    )
    vmem, hbm = pl.BlockSpec(memory_space=pltpu.VMEM), pl.BlockSpec(memory_space=pl.ANY)
    results = pl.pallas_call(
        functools.partial(
            early_kernel, given_names=list(inputs), out_names=list(outs), held_names=list(held), sizes=sizes
        ),
        in_specs=[hbm] * len(inputs),
        out_specs=[hbm] * len(anywhere) + [vmem] * len(near),
        out_shape=[jax.ShapeDtypeStruct(shape, dtype) for shape, dtype in outs.values()],
        scratch_shapes=list(held.values()),
        compiler_params=pltpu.CompilerParams(collective_id=2, has_side_effects=True, vmem_limit_bytes=58 << 20),
        cost_estimate=pl.CostEstimate(flops=2 * 10**10, bytes_accessed=3 * 10**7, transcendentals=2 * 10**6),
    )(*inputs.values())
    return types.SimpleNamespace(**dict(zip(outs, results)))


def finish_kernel(*refs):
    load_sem, write_sem = refs[-2:]
    count = (len(refs) - 2) // 3
    given, outs, held = refs[:count], refs[count:2 * count], refs[2 * count:3 * count]
    loads = [pltpu.make_async_copy(given[i], held[i], load_sem.at[i]) for i in range(count)]
    writes = [pltpu.make_async_copy(held[i], outs[i], write_sem.at[i]) for i in range(count)]
    for copy in loads:
        copy.start()
    for load, write in zip(loads, writes):
        load.wait()
        write.start()
    for write in writes:
        write.wait()


def finished(*arrays):
    hbm = pl.BlockSpec(memory_space=pl.ANY)
    return pl.pallas_call(
        finish_kernel,
        in_specs=[hbm] * len(arrays),
        out_specs=[hbm] * len(arrays),
        out_shape=[jax.ShapeDtypeStruct(a.shape, a.dtype) for a in arrays],
        scratch_shapes=[pltpu.VMEM(a.shape, a.dtype) for a in arrays] + [pltpu.SemaphoreType.DMA((len(arrays),))] * 2,
        compiler_params=pltpu.CompilerParams(vmem_limit_bytes=60 << 20),
        cost_estimate=pl.CostEstimate(flops=0, bytes_accessed=10**7, transcendentals=0),
    )(*arrays)


def bit_names(wide_count, depth):
    wide_bits = [(WIDE, b) for b in range(int(math.log2(wide_count)))]
    deep_bits = [(DEEP, b) for b in range(int(math.log2(depth)))]
    return wide_bits, deep_bits


def bit_order(axes, wide_bits, deep_bits):
    half = len(wide_bits) // 2
    groups = dict(x=wide_bits[:half], y=wide_bits[half:], n=deep_bits[:1], f=deep_bits[1:])
    return [bit for axis in axes for bit in groups[axis]]


def natural(bits):
    return [b for b in sorted(bits, key=lambda b: (b[0] == WIDE, b[1]), reverse=True)]


def picks(left, fixed):
    free = [b for b in left if b not in fixed]
    found = []
    for number in range(1 << len(free)):
        index = 0
        for place, b in enumerate(left):
            if b in fixed:
                digit = fixed[b]
            else:
                digit = (number >> (len(free) - 1 - free.index(b))) & 1
            index = index + digit * (1 << (len(left) - 1 - place))
        found.append(index)
    return found


class Tree:
    def __init__(self, order, left, acc, send, got, slots, me):
        self.order, self.left, self.acc, self.send, self.got, self.slots, self.me = order, left, acc, send, got, slots, me
        self.level = 0
        self.copies = {}

    def fixed(self, own):
        bit = self.order[self.level]
        return {bit: self.me[bit] if own else 1 - self.me[bit]}

    def launch(self, sems, partner, src=None):
        got = self.got[self.level]
        src = self.send.at[pl.ds(0, got.shape[0])] if src is None else src
        bit = self.order[self.level]
        self.copies[self.level] = remote(src, got, sems, self.slots[self.level], lambda: partner(bit))

    def step(self):
        self.left = [b for b in self.left if b != self.order[self.level]]
        self.level += 1

    def arrive(self):
        self.copies[self.level - 1].wait()
        return self.got[self.level - 1]

    def advance(self, sems, partner):
        got = self.arrive() if self.level else None

        def piece(index):
            mine = self.acc[index].astype(F32)
            return mine if got is None else mine + got[index].astype(F32)

        for place, index in enumerate(picks(self.left, self.fixed(False))):
            self.send[place] = piece(index).astype(BF16)
        self.launch(sems, partner)
        for place, index in enumerate(picks(self.left, self.fixed(True))):
            self.acc[place] = piece(index).astype(self.acc.dtype)
        self.step()

    def finish(self, index=0):
        return self.acc[index].astype(F32) + self.got[self.level - 1][index].astype(F32)


def late_kernel(*refs, names, loaded, sizes, plan):
    r = types.SimpleNamespace(**dict(zip(names, refs)))
    given = types.SimpleNamespace(**dict(zip(loaded, refs)))
    heads, experts, dh, rows, width = sizes.heads, sizes.experts, sizes.dh, sizes.rows, sizes.width
    wide_count, depth, block = sizes.wide, sizes.deep, sizes.block
    hd, he, hed = heads * dh, heads * experts, heads * experts * dh
    blocks = wide_count * depth
    wide_bits, deep_bits = bit_names(wide_count, depth)
    bits = wide_bits + deep_bits
    place = {WIDE: lax.axis_index(WIDE), DEEP: lax.axis_index(DEEP)}
    head = lax.axis_index("head")
    me = {b: (place[b[0]] // (1 << b[1])) % 2 for b in bits}
    x_bit, near = wide_bits[0], deep_bits[0]

    def partner(bit):
        axis, number = bit
        other = place[axis] + (1 - 2 * me[bit]) * (1 << number)
        return (head, other, place[DEEP]) if axis == WIDE else (head, place[WIDE], other)

    across = other_core()
    sems = (r.send_sem, r.recv_sem)
    loads = {}

    def fetch(target, name, slot):
        loads[name] = pltpu.make_async_copy(getattr(given, name), target, r.load_sem.at[slot])
        loads[name].start()

    order = {name: number for number, name in enumerate(loaded)}

    def fetch_all(**targets):
        for name, target in targets.items():
            fetch(target, name, order[name])

    def ready(*wanted):
        for name in wanted:
            if loads.get(name) is not None:
                loads[name].wait()
                loads[name] = None

    def tree_of(axes, left, acc, send, got, slots):
        return Tree(bit_order(axes, wide_bits, deep_bits), natural(left), acc, send, got, slots, me)

    up_a = tree_of("yxfn", bits, None, None, r.got_up_a, plan.up_a)
    up_b = tree_of("nxyf", bits, None, None, r.got_up_b, plan.up_b)
    share = width // wide_count
    per_share = share // block

    def runs(fixed):
        return picks(natural(wide_bits), {b: v for b, v in fixed.items() if b[0] == WIDE})

    def rows_of(run):
        return pl.ds(pl.multiple_of(run * share, share), share)

    half = sizes.hidden_units // 2
    keep, leave = me[x_bit], 1 - me[x_bit]
    meet(across, *[partner(b) for b in bits])
    beside = partner(near)
    early = [
        remote(given.att, r.att_in, sems, plan.att, partner(x_bit)),
        remote(given.gate_o, r.gate_o_in, sems, plan.gate_o, partner(x_bit)),
        remote(given.gates, r.gates_in, sems, plan.gates, beside),
    ]
    fetch_all(hid=r.hid)

    def run_rows(ref, run):
        count = per_share // 2
        return ref[pl.ds(pl.multiple_of(run * count, count), count)].reshape(share, rows)

    near_rows = blocks // 2 * block
    small = r.small
    near_other = 1 - me[near]
    crossing, gm_swap, ffn_swap, two_swap, act_swap, hid_swap = [], [], [], [], [], []

    def middle(att_ref, gate_ref, sig_ref, wo, cot, mixed_ref, gain, low_ref, ffn_own):
        fetch_all(att=att_ref, gate_o=gate_ref, wo=wo, cot=cot, gain_two=gain, sig_o=sig_ref)

        def feed(x, cot_first, bias, up, down, two_ref):
            fetch_all(x=x, cot_in=cot_first, bias_two=bias, w_up=up, w_down=down)
            ready("att", "gate_o", "wo")
            for h in range(heads):
                for e in range(experts):
                    at = h * experts + e
                    r.gated[at * dh:(at + 1) * dh, :] = (
                        gate_ref[at:at + 1, :] * att_ref[h].astype(F32)
                    ).astype(BF16)
            r.two_own[...] = mm(r.gated[...], wo[...], TN).astype(BF16)
            part_swap = remote(r.two_own, r.head_in, sems, plan.part, across)
            ready("cot", "cot_in", "x", "gain_two", "bias_two")
            r.cot_t[:, 0:rows] = cot[...].T
            r.cot_t[:, rows:] = cot_first[...].T
            part_swap.wait()
            mixed = x[...].astype(F32) + (r.two_own[...].astype(F32) + r.head_in[...].astype(F32))
            mixed_ref[...] = mixed
            normed, _ = normalize(mixed)
            two = (normed * gain[...] + bias[...]).astype(BF16)
            two_ref[...] = two
            r.two_t[...] = two.T.reshape(r.two_t.shape)
            hid_swap.append(
                remote(given.hid.at[:, near_other], r.hid_in, sems, plan.hid, lambda: partner(near))
            )
            ready("w_up", "w_down")
            chunk = half // 2
            for which, target in ((leave, r.act_out), (keep, r.act)):
                for part in range(2):
                    units = pl.ds(pl.multiple_of(which * half + part * chunk, chunk), chunk)
                    inner = slice(part * chunk, (part + 1) * chunk)
                    value, slope = gelu_both(mm(two_ref[...], up[:, units]))
                    if target is r.act:
                        target[:, inner] = value.astype(BF16)
                    else:
                        target[:, :, inner] = value.astype(BF16).reshape(target.shape[0], target.shape[1], chunk)
                    r.pre[which, :, inner] = (mm(cot[...], down[units, :], NT) * slope).astype(BF16)
                if target is r.act_out:
                    act_swap.append(remote(r.act_out, r.act_in, sems, plan.act, lambda: partner(x_bit)))
            for number, run in enumerate(runs(up_a.fixed(False))):
                piece = mm(run_rows(r.two_t, run), r.pre[0]).astype(BF16)
                for k in range(per_share):
                    r.up_a_out[number * per_share + k] = piece[k * block:(k + 1) * block]
            up_a.launch(sems, partner, r.up_a_out)
            piece = mm(r.two_t[:, 1 - me[near]].reshape(near_rows, rows), r.pre[1]).astype(BF16)
            for at in range(blocks // 2):
                r.up_b_out[at] = piece[at * block:(at + 1) * block]
            up_b.launch(sems, partner, r.up_b_out)
            total = None
            for k in range(2):
                term = mm(r.pre[k], up[:, k * half:(k + 1) * half], NT)
                total = term if total is None else total + term
            r.two_own[...] = total.astype(BF16)
            two_swap.append(remote(r.two_own, r.two_in, sems, plan.two, across))
            mine = mm(r.act[...], down[pl.ds(pl.multiple_of(keep * half, half), half), :])
            theirs = mm(
                r.act_out[...].reshape(rows, half), down[pl.ds(pl.multiple_of(leave * half, half), half), :]
            )
            ffn_own[...] = (mine + theirs).astype(BF16)
            ffn_swap.append(remote(ffn_own, r.ffn_in, sems, plan.ffn, across))

        pl.run_scoped(
            feed, pltpu.VMEM((rows, width), BF16), pltpu.VMEM((rows, width), BF16), pltpu.VMEM((1, width), F32),
            pltpu.VMEM((width, 2 * half), BF16), pltpu.VMEM((2 * half, width), BF16), pltpu.VMEM((rows, width), BF16),
        )

        def out_back():
            normed, inverse = normalize(mixed_ref[...])
            two_swap[0].wait()
            grad_two = r.two_own[...].astype(F32) + r.two_in[...].astype(F32)
            small[2:3, :] = jnp.sum(grad_two * normed, axis=0, keepdims=True)
            small[3:4, :] = jnp.sum(grad_two, axis=0, keepdims=True)
            grad_mixed = cot[...].astype(F32) + norm_back(grad_two * gain[...], normed, inverse)
            r.grad_mixed[...] = grad_mixed
            low_ref[...] = grad_mixed.astype(BF16)
            low_t = low_ref[...].T.reshape(wide_count // 2, 2, share, rows)
            first, second = low_t[:, 0], low_t[:, 1]
            r.gm_out[...] = jnp.where(me[x_bit] == 1, first, second)
            r.gm[...] = jnp.where(me[x_bit] == 1, second, first)
            gm_swap.append(remote(r.gm_out, r.gm_in, sems, plan.gm, lambda: partner(x_bit)))
            ready("sig_o")
            for h in range(heads):
                att = att_ref[h].astype(F32)
                total = None
                for e in range(experts):
                    at = h * experts + e
                    back = mm(wo[at * dh:(at + 1) * dh, :], low_ref[...], NT)
                    gate = gate_ref[at:at + 1, :]
                    grad_gate = jnp.sum(att * back, axis=0, keepdims=True)
                    r.logits[he + at:he + at + 1, :] = grad_gate * gate * (1.0 - sig_ref[at:at + 1, :])
                    total = gate * back if total is None else total + gate * back
                r.ga[h] = total.astype(BF16)
            ffn_swap[0].wait()
            ffn_own[...] = (mixed_ref[...] + (ffn_own[...].astype(F32) + r.ffn_in[...].astype(F32))).astype(BF16)
            pltpu.make_async_copy(ffn_own, r.output, r.load_sem.at[len(loaded)]).start()

        total_keys = 4 * rows
        chunk_shape = pltpu.VMEM((heads, dh, rows), BF16)
        pl.run_scoped(
            functools.partial(attention, out_back), pltpu.VMEM((heads, rows, total_keys), BF16), chunk_shape,
            chunk_shape, pltpu.VMEM((heads, dh, total_keys), BF16), *([chunk_shape] * 8),
            pltpu.VMEM((sizes.query_rows, sizes.query_rows), BF16), pltpu.VMEM((dh, total_keys), F32),
        )
        pltpu.make_async_copy(ffn_own, r.output, r.load_sem.at[len(loaded)]).wait()

    def attention(out_back, probs, qu, qv, rel, key_own, part_k, mem_k, part_mem_k, value_own, part_v, mem_v, part_mem_v, flip,
                  acc):
        fetch_all(
            probs=probs, qu=qu, qv=qv, rel=rel, key_own=key_own, part_k=part_k, mem_k=mem_k, part_mem_k=part_mem_k,
            value_own=value_own, part_v=part_v, mem_v=mem_v, part_mem_v=part_mem_v, flip=flip,
        )

        out_back()
        ready("probs", "qu", "qv", "rel", "key_own", "part_k", "mem_k", "part_mem_k")
        ready("value_own", "part_v", "mem_v", "part_mem_v", "flip")
        odd = place[DEEP] % 2 == 1
        size = sizes.query_rows
        for h in range(heads):
            k_one = jnp.where(odd, part_k[h], part_mem_k[h])
            v_one = jnp.where(odd, part_v[h], part_mem_v[h])
            keys = (part_mem_k[h], mem_k[h], k_one, key_own[h])
            values = (part_mem_v[h], mem_v[h], v_one, value_own[h])
            bias_u = bias_v = None
            for base in range(0, rows, size):
                here = slice(base, base + size)
                turned = mm(flip[...], probs[h, here, :])
                ga = mm(r.ga[h, :, here], flip[...]).astype(BF16)
                queries_u = mm(qu[h, :, here], flip[...]).astype(BF16)
                queries_v = mm(qv[h, :, here], flip[...]).astype(BF16)
                gp = jnp.concatenate([mm(ga, v, TN) for v in values], axis=1)
                weighted = turned * gp
                delta = jnp.sum(weighted, axis=1, keepdims=True)
                gs = ((weighted - turned * delta) * sizes.scale).astype(BF16)
                gk = mm(queries_u, gs[:, 2 * rows:])
                gv = mm(ga, turned[:, 2 * rows:].astype(BF16))
                gqu = None
                for i, k in enumerate(keys):
                    part = mm(k, gs[:, i * rows:(i + 1) * rows], NT)
                    gqu = part if gqu is None else gqu + part
                gpos = pltpu.roll(gs, rows - size - base, 1, stride=1, stride_axis=0)
                gqv = mm(rel[h], gpos, NT)
                grel = mm(queries_v, gpos)
                r.gq[h * dh:(h + 1) * dh, here] = mm((gqu + gqv).astype(BF16), flip[...]).astype(BF16)
                ones = jnp.ones((8, size), F32)
                sum_u, sum_v = [
                    lax.dot_general(ones, g, NT, precision=lax.Precision.HIGHEST, preferred_element_type=F32)
                    for g in (gqu, gqv)
                ]
                if base == 0:
                    r.gk[h] = gk
                    r.gv[h] = gv
                    acc[...] = grel
                    bias_u, bias_v = sum_u, sum_v
                else:
                    r.gk[h] += gk
                    r.gv[h] += gv
                    acc[...] += grel
                    bias_u, bias_v = bias_u + sum_u, bias_v + sum_v
            r.grel[h * dh:(h + 1) * dh, :] = acc[...].astype(BF16)
            r.small[4 + h:5 + h, 0:dh] = bias_u[0:1]
            r.small[4 + heads + h:5 + heads + h, 0:dh] = bias_v[0:1]
        r.cross_out[0] = r.gk[:, :, :rows].astype(BF16)
        r.cross_out[1] = r.gv[:, :, :rows].astype(BF16)
        crossing.append(remote(r.cross_out, r.cross_in, sems, plan.cross, lambda: partner(near)))

    hd_up = sizes.hd_up
    small[4:8, :] = jnp.zeros((4, width), F32)
    tokens_of = pltpu.VMEM((heads, dh, rows), BF16)
    pl.run_scoped(
        middle, tokens_of, pltpu.VMEM((he, rows), F32), pltpu.VMEM((he, rows), F32), pltpu.VMEM((hed, width), BF16),
        pltpu.VMEM((rows, width), BF16), pltpu.VMEM((rows, width), F32), pltpu.VMEM((1, width), F32),
        pltpu.VMEM((rows, width), BF16), pltpu.VMEM((rows, width), BF16),
    )

    def rest(*held):
        b = types.SimpleNamespace(**dict(zip(sizes.late_names, held)))
        fetch_all(each=b.each, sigs=b.sigs, gates=b.gates, wv=b.wv, wq=b.wq, wk=b.wk, rt=b.rt, x=b.x, gain=b.gain)
        up_a.acc, up_a.send, up_b.acc, up_b.send = r.act_out, b.send_up_a, b.acc_up_b, b.send_up_b
        far = [v for v in bits if v != near]
        out = tree_of("ynf", [v for v in bits if v != x_bit], b.acc_out, b.send_out, r.got_out, plan.out)
        value = tree_of("xyf", far, b.acc_value, b.send_value, r.got_value, plan.value)
        query = tree_of("xynf", bits, b.acc_query, b.send_query, r.got_query, plan.query)
        down = tree_of("yfn", bits, r.up_b_out, r.up_a_out, r.got_down, plan.down)
        half_count = len(wide_bits) // 2
        for tree in (out, down):
            tree.order = tree.order[:half_count] + wide_bits[1:half_count] + tree.order[half_count:]
        state = []

        def down_part(own):
            for number, run in enumerate(runs(down.fixed(own))):
                at_rows = rows_of(run)
                part = mm(r.cot_t[at_rows, 0:rows], r.act[...]) + mm(
                    r.cot_t[at_rows, rows:], r.act_in[...].reshape(rows, half)
                )
                for k in range(per_share):
                    at = number * per_share + k
                    piece = part[k * block:(k + 1) * block]
                    if own:
                        down.acc[at] = piece.astype(BF16)
                    else:
                        down.send[at] = piece.astype(BF16)
            if own:
                down.step()
            else:
                down.launch(sems, partner)

        def up_a_keep():
            for number, run in enumerate(runs(up_a.fixed(True))):
                part = mm(run_rows(r.two_t, run), r.pre[0])
                for k in range(per_share):
                    up_a.acc[number * per_share + k] = part[k * block:(k + 1) * block].astype(BF16)
            up_a.step()

        def up_b_keep():
            part = mm(r.two_t[:, me[near]].reshape(near_rows, rows), r.pre[1])
            for at in range(blocks // 2):
                up_b.acc[at] = part[at * block:(at + 1) * block].astype(BF16)
            up_b.step()

        def out_part():
            mine = mm(r.gm[...].reshape(near_rows, rows), r.gated[...], NT)
            for at in range(blocks // 2):
                out.acc[at] = mine[at * block:(at + 1) * block].astype(BF16)
            early[0].wait()
            early[1].wait()
            for h in range(heads):
                for e in range(experts):
                    at = h * experts + e
                    r.gated[at * dh:(at + 1) * dh, :] = (
                        r.gate_o_in[at:at + 1, :] * r.att_in[h].astype(F32)
                    ).astype(BF16)
            gm_swap[0].wait()
            theirs = mm(r.gm_in[...].reshape(near_rows, rows), r.gated[...], NT)
            for at in range(blocks // 2):
                out.acc[at] = (out.acc[at].astype(F32) + theirs[at * block:(at + 1) * block]).astype(BF16)
            out.advance(sems, partner)

        def own_part():
            ready("each", "sigs", "gates")
            crossing[0].wait()
            even = jnp.where(place[DEEP] % 2 == 0, 1.0, 0.0)
            for h in range(heads):
                gk = r.gk[h, :, rows:] + even * r.cross_in[0, h].astype(F32)
                gv = r.gv[h, :, rows:] + even * r.cross_in[1, h].astype(F32)
                b.own_out[h * dh:(h + 1) * dh, :] = gv.astype(BF16)
                b.own_out[hd + h * dh:hd + (h + 1) * dh, :] = gk.astype(BF16)
                for e in range(experts):
                    at = h * experts + e
                    gate = b.gates[at:at + 1, :]
                    grad_gate = jnp.sum(gv * b.each[at * dh:(at + 1) * dh, :].astype(F32), axis=0, keepdims=True)
                    r.logits[at:at + 1, :] = grad_gate * gate * (1.0 - b.sigs[at:at + 1, :])
                    b.grads[at * dh:(at + 1) * dh, :] = (gate * gv).astype(BF16)
            tail = b.own_out.shape[0] - 2 * hd
            logits = jnp.concatenate([r.logits[0:2 * he, :], jnp.zeros((tail - 2 * he, rows), F32)], axis=0)
            b.own_out[2 * hd:, :] = logits.astype(BF16)
            state_own.append(remote(b.own_out, r.own_in, sems, plan.own, partner(near)))
            b.grads[hed:, :] = b.own_out[hd:, :]

        def hidden_part():
            ready("wv", "wq", "wk", "rt")
            grad_hidden = mm(b.grads[0:hed, :], b.wv[...], TN)
            grad_hidden += mm(r.gq[...], b.wq[...], TN)
            grad_hidden += mm(b.grads[hed:hed + hd, :], b.wk[...], TN)
            grad_hidden += mm(b.grads[hed + hd:hed + hd + 2 * he, :], b.rt[...], TN)
            r.two_own[...] = grad_hidden.astype(BF16)
            state_head.append(remote(r.two_own, r.head_in, sems, plan.head, across))

        def norm_part():
            ready("x", "gain")
            state_head[0].wait()
            grad_hidden = r.two_own[...].astype(F32) + r.head_in[...].astype(F32)
            normed, inverse = normalize(b.x[...].astype(F32))
            small[0:1, :] = jnp.sum(grad_hidden * normed, axis=0, keepdims=True)
            small[1:2, :] = jnp.sum(grad_hidden, axis=0, keepdims=True)
            state.append(remote(small, r.small_in.at[0], sems, plan.small[0], partner(bits[0])))
            r.grad_mixed[...] += norm_back(grad_hidden * b.gain[...], normed, inverse)
            input_copy = pltpu.make_async_copy(r.grad_mixed, r.grad_input, r.load_sem.at[len(loaded) + 1])
            input_copy.start()
            state_input.append(input_copy)

        def small_step():
            at = len(state) - 1
            if at == len(bits):
                return
            state[at].wait()
            small[...] = small[...] + r.small_in[at]
            state.append(
                None if at + 1 == len(bits)
                else remote(small, r.small_in.at[at + 1], sems, plan.small[at + 1], partner(bits[at + 1]))
            )

        def value_own():
            ready("hid")
            mine = mm(r.hid[:, me[near]].reshape(near_rows, rows), b.grads[...], NT)
            for at in range(blocks // 2):
                value.acc[at] = mine[at * block:(at + 1) * block]

        def value_part():
            early[2].wait()
            hid_swap[0].wait()
            state_own[0].wait()
            for at in range(he):
                h = at // experts
                b.grads[at * dh:(at + 1) * dh, :] = (
                    r.gates_in[at:at + 1, :] * r.own_in[h * dh:(h + 1) * dh, :].astype(F32)
                ).astype(BF16)
            b.grads[hed:, :] = r.own_in[hd:, :]
            theirs = mm(r.hid_in[...].reshape(near_rows, rows), b.grads[...], NT)
            for at in range(blocks // 2):
                value.acc[at] += theirs[at * block:(at + 1) * block]
            value.advance(sems, partner)

        def table_copy(number, run):
            return pltpu.make_async_copy(
                given.table.at[rows_of(run)], b.table.at[pl.ds(number * share, share)], r.table_sem.at[number]
            )

        for number, run in enumerate(runs(query.fixed(False))):
            table_copy(number, run).start()

        def query_part(own):
            if not own and hd_up > hd:
                for at in range(blocks // 2):
                    query.send[at, :, hd:hd_up] = jnp.zeros((block, hd_up - hd), BF16)
                    query.acc[at, :, hd:hd_up] = jnp.zeros((block, hd_up - hd), BF16)
            ready("hid")
            for number, run in enumerate(runs(query.fixed(own))):
                table_copy(number, run).wait()
                part = mm(run_rows(r.hid, run), r.gq[...], NT)
                part_rel = mm(b.table[number * share:(number + 1) * share, :], r.grel[...], NT)
                for k in range(per_share):
                    at = number * per_share + k
                    piece, piece_rel = part[k * block:(k + 1) * block], part_rel[k * block:(k + 1) * block]
                    if own:
                        query.acc[at, :, 0:hd] = piece.astype(BF16)
                        query.acc[at, :, hd_up:] = piece_rel.astype(BF16)
                    else:
                        query.send[at, :, 0:hd] = piece.astype(BF16)
                        query.send[at, :, hd_up:] = piece_rel.astype(BF16)
            if own:
                query.step()
            else:
                query.launch(sems, partner)
                for number, run in enumerate(runs(query.fixed(True))):
                    table_copy(number, run).start()

        state_own, state_head, state_input = [], [], []
        def half_part():
            down.arrive()
            r.half_out[...] = down.finish(leave).astype(BF16)
            state_own.append(remote(r.half_out, r.half_in, sems, plan.half, partner(x_bit)))
            r.g_down[:, pl.ds(pl.multiple_of(keep * half, half), half)] = down.finish(keep)

        def next_level(tree):
            if tree.level < len(tree.order):
                tree.advance(sems, partner)

        act_swap[0].wait()
        up_a_keep()
        next_level(up_a)
        down_part(False)
        own_part()
        up_b_keep()
        next_level(up_b)
        next_level(up_a)
        down_part(True)
        query_part(False)
        value_own()
        query_part(True)
        out_part()
        next_level(down)
        hidden_part()
        next_level(up_a)
        value_part()
        next_level(up_b)
        next_level(out)
        norm_part()
        next_level(query)
        next_level(query)
        next_level(up_b)
        next_level(down)
        next_level(value)
        small_step()
        next_level(out)
        next_level(query)
        small_step()
        next_level(value)
        half_part()
        small_step()
        while len(state) <= len(bits):
            small_step()
        r.small_out[...] = small[...]
        r.bias_u[...] = small[4:4 + heads, 0:dh]
        r.bias_v[...] = small[4 + heads:4 + 2 * heads, 0:dh]
        for number, tree in enumerate((up_a, up_b)):
            tree.arrive()
            r.g_up[:, number * half:(number + 1) * half] = tree.finish()
        out.arrive()
        total = out.finish()
        for at in range(he):
            r.g_out[at] = total[:, at * dh:(at + 1) * dh]
        value.arrive()
        total = value.finish()
        for at in range(he):
            r.g_value[at] = total[:, at * dh:(at + 1) * dh]
        for h in range(heads):
            r.g_key[:, h, :] = total[:, hed + h * dh:hed + (h + 1) * dh]
        eye = (
            lax.broadcasted_iota(jnp.int32, (block, block), 0) == lax.broadcasted_iota(jnp.int32, (block, block), 1)
        ).astype(F32)
        turned = lax.dot_general(
            total[:, hed + hd:hed + hd + 2 * he], eye, TN, precision=lax.Precision.HIGHEST, preferred_element_type=F32
        )
        for h in range(heads):
            for e in range(experts):
                at = h * experts + e
                r.g_router_v[e, h:h + 1, :] = turned[at:at + 1]
                r.g_router_o[e, h:h + 1, :] = turned[he + at:he + at + 1]
        query.arrive()
        total = query.finish()
        for h in range(heads):
            r.g_query[:, h, :] = total[:, h * dh:(h + 1) * dh]
            r.g_rel[:, h, :] = total[:, hd_up + h * dh:hd_up + (h + 1) * dh]
        state_own[1].wait()
        r.g_down[:, pl.ds(pl.multiple_of(leave * half, half), half)] = r.half_in[...].astype(F32)
        state_input[0].wait()

    pl.run_scoped(rest, *sizes.late_scratch)


def late_call(inputs, sizes):
    wide_bits, deep_bits = bit_names(sizes.wide, sizes.deep)
    bits = len(wide_bits) + len(deep_bits)
    blocks = sizes.wide * sizes.deep
    block, rows, width, heads, dh = sizes.block, sizes.rows, sizes.width, sizes.heads, sizes.dh
    he, hd = heads * sizes.experts, heads * dh
    hed, half = he * dh, sizes.hidden_units // 2
    tail = 32
    sizes.hd_up = -(-hd // 128) * 128
    sizes.value_n = hed + hd + tail
    query_n = sizes.hd_up + hd
    count = 15 + 7 * bits
    slots = iter(range(count))

    def levels():
        return [next(slots) for _ in range(bits)]

    plan = types.SimpleNamespace(
        two=next(slots), ffn=next(slots), act=next(slots), gm=next(slots), cross=next(slots), part=next(slots),
        att=next(slots), gate_o=next(slots), gates=next(slots), hid=next(slots),
        own=next(slots), head=next(slots), half=next(slots), small=levels(), up_a=levels(), up_b=levels(),
        out=levels(), query=levels(), down=levels(), value=levels(),
    )

    def got(n, start, stop):
        return [pltpu.VMEM((blocks >> (level + 1), block, n), BF16) for level in range(start, stop)]

    def taken(name):
        return pltpu.VMEM(inputs[name].shape, inputs[name].dtype)

    sem = pltpu.SemaphoreType.DMA
    token_rows = pltpu.VMEM((rows, width), BF16)
    near_half = pltpu.VMEM((blocks // 2, block, rows), BF16)
    x_half = pltpu.VMEM((sizes.wide // 2, width // sizes.wide, rows), BF16)
    first_half = pltpu.VMEM((blocks // 2, block, half), BF16)
    scratch = dict(
        act=pltpu.VMEM((rows, half), BF16), hid=taken("hid"), two_t=taken("hid"),
        pre=pltpu.VMEM((2, rows, half), BF16), cot_t=pltpu.VMEM((width, 2 * rows), BF16),
        gated=pltpu.VMEM((hed, rows), BF16), att_in=taken("att"), gate_o_in=taken("gate_o"), gates_in=taken("gates"),
        two_own=token_rows, two_in=token_rows, ffn_in=token_rows, head_in=token_rows,
        act_in=first_half, act_out=first_half, up_a_out=first_half, up_b_out=first_half,
        hid_in=near_half, gm=x_half, gm_in=x_half, gm_out=x_half,
        grad_mixed=pltpu.VMEM((rows, width), F32), table_sem=sem((sizes.wide // 2,)),
        small=pltpu.VMEM((8, width), F32), small_in=pltpu.VMEM((bits, 8, width), F32),
        logits=pltpu.VMEM((2 * he, rows), F32), ga=pltpu.VMEM((heads, dh, rows), BF16),
        gq=pltpu.VMEM((hd, rows), BF16), gk=pltpu.VMEM((heads, dh, 2 * rows), F32),
        gv=pltpu.VMEM((heads, dh, 2 * rows), F32), grel=pltpu.VMEM((hd, 4 * rows), BF16),
        cross_out=pltpu.VMEM((2, heads, dh, rows), BF16), cross_in=pltpu.VMEM((2, heads, dh, rows), BF16),
        own_in=pltpu.VMEM((2 * hd + tail, rows), BF16), half_in=pltpu.VMEM((block, half), BF16),
        half_out=pltpu.VMEM((block, half), BF16),
        got_up_a=got(half, 0, bits), got_up_b=got(half, 0, bits), got_out=got(hed, 1, bits),
        got_query=got(query_n, 0, bits), got_down=got(half, 0, bits - 1), got_value=got(sizes.value_n, 1, bits),
        load_sem=sem((len(inputs) + 3,)), send_sem=sem((count,)), recv_sem=sem((count,)),
    )
    late = dict(
        send_out=pltpu.VMEM((blocks >> 2, block, hed), BF16), acc_out=pltpu.VMEM((blocks >> 1, block, hed), BF16),
        table=pltpu.VMEM((width // 2, 4 * rows), BF16), each=taken("each"), sigs=taken("sigs"), gates=taken("gates"), wv=taken("wv"),
        wq=taken("wq"), wk=taken("wk"), rt=taken("rt"), x=taken("x"), gain=taken("gain"),
        own_out=pltpu.VMEM((2 * hd + tail, rows), BF16), grads=pltpu.VMEM((sizes.value_n, rows), BF16),
        send_up_a=pltpu.VMEM((blocks >> 2, block, half), BF16), send_up_b=pltpu.VMEM((blocks >> 2, block, half), BF16),
        acc_up_b=pltpu.VMEM((blocks >> 1, block, half), BF16),
        send_query=pltpu.VMEM((blocks >> 1, block, query_n), BF16),
        acc_query=pltpu.VMEM((blocks >> 1, block, query_n), BF16),
        send_value=pltpu.VMEM((blocks >> 2, block, sizes.value_n), BF16),
        acc_value=pltpu.VMEM((blocks >> 1, block, sizes.value_n), F32),
    )
    sizes.late_names, sizes.late_scratch = list(late), list(late.values())
    outs = dict(
        g_down=((block, 2 * half), F32), g_up=((block, 2 * half), F32), g_out=((he, block, dh), F32),
        g_value=((he, block, dh), F32), g_query=((block, heads, dh), F32), g_key=((block, heads, dh), F32),
        g_rel=((block, heads, dh), F32), g_router_v=((sizes.experts, heads, block), F32),
        g_router_o=((sizes.experts, heads, block), F32), bias_u=((heads, dh), F32), bias_v=((heads, dh), F32), small_out=((8, width), F32),
        grad_input=((rows, width), F32), output=((rows, width), BF16),
    )
    flat, tree = jax.tree.flatten(list(scratch.values()))

    def kernel(*refs):
        held = jax.tree.unflatten(tree, refs[len(inputs) + len(outs):])
        late_kernel(
            *refs[:len(inputs) + len(outs)], *held, names=[None] * 0 + [n + "_" for n in inputs] + list(outs) + list(scratch),
            loaded=list(inputs), sizes=sizes, plan=plan,
        )

    vmem, anywhere = pl.BlockSpec(memory_space=pltpu.VMEM), pl.BlockSpec(memory_space=pl.ANY)
    results = pl.pallas_call(
        kernel,
        in_specs=[anywhere] * len(inputs),
        out_specs=[vmem] * (len(outs) - 2) + [anywhere] * 2,
        out_shape=[jax.ShapeDtypeStruct(shape, dtype) for shape, dtype in outs.values()],
        scratch_shapes=flat,
        compiler_params=pltpu.CompilerParams(collective_id=0, has_side_effects=True, vmem_limit_bytes=60 << 20),
        cost_estimate=pl.CostEstimate(flops=4 * 10**10, bytes_accessed=10**8, transcendentals=0),
    )(*inputs.values())
    return types.SimpleNamespace(**dict(zip(outs, results)))


def body(
    layer_input, mem_keys, mem_values, route_value, route_output, ln1_gain, ln1_bias, w_query, w_key, w_rel,
    content_bias, position_bias, w_value, w_out, router_value, router_output, ln2_gain, ln2_bias, w_up, w_down,
    cotangent,
):
    rows, width = layer_input.shape
    heads, dh = content_bias.shape
    experts = w_value.shape[1]
    odd = (lax.axis_index("dp") % 2).astype(jnp.int32)
    scale = 1.0 / math.sqrt(dh)
    total_keys = 4 * rows
    block = rows // 2
    hd = heads * dh
    hed = heads * experts * dh

    wq = jnp.transpose(w_query, (1, 2, 0)).reshape(hd, width)
    wk = jnp.transpose(w_key, (1, 2, 0)).reshape(hd, width)
    wr = jnp.transpose(w_rel, (1, 2, 0)).reshape(hd, width)
    wv = jnp.transpose(w_value, (0, 1, 3, 2)).reshape(hed, width)
    wo = w_out.reshape(hed, width)
    mem_k = jnp.transpose(mem_keys, (1, 2, 0))
    mem_v = jnp.transpose(mem_values, (1, 2, 0))
    rv = jnp.transpose(route_value, (0, 2, 1))
    ro = jnp.transpose(route_output, (0, 2, 1))
    table = jnp.asarray(position_table(total_keys, width))
    first = early_call(dict(
        x=layer_input, gain=ln1_gain.reshape(1, width), bias=ln1_bias.reshape(1, width), wk=wk, rv=rv, ro=ro,
        router_v=jnp.transpose(router_value, (2, 1, 0)), router_o=jnp.transpose(router_output, (2, 1, 0)),
        wv=wv, wq=wq, cb=content_bias, pb=position_bias, wr=wr, table=table, mem_k=mem_k, mem_v=mem_v, cot=cotangent,
    ), types.SimpleNamespace(
        heads=heads, experts=experts, dh=dh, rows=rows, width=width, wide=lax.axis_size(WIDE),
        deep=lax.axis_size(DEEP), scale=scale, query_rows=block,
    ))
    att, gate_v, gate_o, sig_v, sig_o, hid = first.att, first.gate_v, first.gate_o, first.sig_v, first.sig_o, first.hid
    wide_count, depth = lax.axis_size(WIDE), lax.axis_size(DEEP)
    blocks = wide_count * depth
    block_rows, he = width // blocks, heads * experts
    hidden_units = w_up.shape[1]
    wide_bits, deep_bits = bit_names(wide_count, depth)
    gain_two, bias_two = ln2_gain.reshape(1, width), ln2_bias.reshape(1, width)
    sem = pltpu.SemaphoreType.DMA

    def shapes(*pairs):
        return [jax.ShapeDtypeStruct(shape, dtype) for shape, dtype in pairs]

    flip = jnp.asarray(np.eye(block, dtype=np.float32)[::-1].astype(BF16))
    inputs = dict(
        hid=hid, gates=gate_v, cot=cotangent, cot_in=first.cot_in, gain_two=gain_two, bias_two=bias_two, w_up=w_up,
        w_down=w_down, att=att, gate_o=gate_o, sig_o=sig_o, wo=wo,
        flip=flip, probs=first.probs, qu=first.qu, qv=first.qv, rel=first.rel,
        key_own=first.key_own, part_k=first.part_k, mem_k=mem_k, part_mem_k=first.part_mem_k,
        value_own=first.value_own, part_v=first.part_v, mem_v=mem_v, part_mem_v=first.part_mem_v,
        table=table, sigs=sig_v, each=first.each, wv=wv, wq=wq, wk=wk, rt=first.rt,
        x=layer_input, gain=ln1_gain.reshape(1, width),
    )
    done = late_call(inputs, types.SimpleNamespace(
        heads=heads, experts=experts, dh=dh, rows=rows, width=width, wide=wide_count, deep=depth, block=block_rows,
        hidden_units=hidden_units, scale=scale, query_rows=block,
    ))
    start = (lax.axis_index(WIDE) * depth + lax.axis_index(DEEP)) * block_rows
    ln = lax.dynamic_slice_in_dim(done.small_out, start, block_rows, axis=1)
    (output, grad_input, g_query, g_key, g_rel, g_value, g_out, g_up, g_down, g_router_v, g_router_o, bias_u,
     bias_v) = finished(
        done.output, done.grad_input, done.g_query, done.g_key, done.g_rel, done.g_value, done.g_out, done.g_up,
        done.g_down, done.g_router_v, done.g_router_o, done.bias_u, done.bias_v,
    )

    def by_expert(values):
        return values.reshape(heads, experts, block_rows, dh)

    return (
        output, grad_input, ln[0], ln[1], g_query, g_key, g_rel, bias_u, bias_v,
        by_expert(g_value), jnp.transpose(by_expert(g_out), (0, 1, 3, 2)), jnp.transpose(g_router_v, (2, 1, 0)),
        jnp.transpose(g_router_o, (2, 1, 0)),
        ln[2], ln[3], g_up, jnp.transpose(g_down),
    )


def solution(mesh):
    tokens = ("wide", "dp")
    return jax.shard_map(
        body,
        mesh=mesh,
        in_specs=(
            P(tokens, None), P(tokens, "head", None), P(tokens, "head", None), P("head", tokens, None),
            P("head", tokens, None), P(), P(), P(None, "head", None), P(None, "head", None), P(None, "head", None),
            P("head", None), P("head", None), P("head", None, None, None), P("head", None, None, None),
            P(None, "head", None), P(None, "head", None), P(), P(), P(None, "head"), P("head", None), P(tokens, None),
        ),
        out_specs=(
            P(tokens, None), P(tokens, None), P(tokens), P(tokens), P(tokens, "head", None), P(tokens, "head", None),
            P(tokens, "head", None), P("head", None), P("head", None), P("head", None, tokens, None),
            P("head", None, None, tokens), P(tokens, "head", None), P(tokens, "head", None), P(tokens), P(tokens),
            P(tokens, "head"), P("head", tokens),
        ),
        check_vma=False,
    )
```

```python
import functools
import math
import types

import jax
import jax.numpy as jnp
import numpy as np
from jax import lax
from jax.experimental import pallas as pl
from jax.experimental.pallas import tpu as pltpu
from jax.sharding import PartitionSpec as P

EPSILON = 1e-05
NEG_LARGE = -1e30
F32 = jnp.float32
BF16 = jnp.bfloat16
WIDE, DEEP = "wide", "dp"

NN = (((1,), (0,)), ((), ()))
NT = (((1,), (1,)), ((), ()))
TN = (((0,), (0,)), ((), ()))


def mm(a, b, dims=NN):
    return lax.dot_general(a, b, dims, preferred_element_type=F32)


def normalize(values):
    row_mean = jnp.mean(values, axis=-1, keepdims=True)
    centered = values - row_mean
    variance = jnp.mean(centered * centered, axis=-1, keepdims=True)
    inverse = lax.rsqrt(variance + EPSILON)
    return (centered * inverse, inverse)


def norm_back(grad_normed, normed, inverse):
    first_mean = jnp.mean(grad_normed, axis=-1, keepdims=True)
    second_mean = jnp.mean(grad_normed * normed, axis=-1, keepdims=True)
    return inverse * (grad_normed - first_mean - normed * second_mean)


def position_table(extent, model_width):
    half_width = model_width // 2
    frequencies = np.exp(
        np.arange(half_width, dtype=np.float32) * np.float32(-2.0 * math.log(10000.0) / model_width)
    ).astype(np.float32)
    distance = np.arange(extent - 1, -1, -1).astype(np.float32)
    angles = (frequencies[:, None] * distance[None, :]).astype(np.float64)
    return np.concatenate([np.sin(angles), np.cos(angles)], axis=0).astype(np.float32).astype(BF16)


def whole(array):
    return pl.BlockSpec(array.shape, lambda *_: (0,) * len(array.shape))


def gelu_both(x):
    c = math.sqrt(2.0 / math.pi)
    square = x * x
    t = jnp.tanh(c * x * (1.0 + 0.044715 * square))
    half = 0.5 * (1.0 + t)
    return x * half, half + 0.5 * x * (1.0 - t * t) * (c * (1.0 + 3.0 * 0.044715 * square))


def meet(*devices):
    barrier = pltpu.get_barrier_semaphore()
    for device in devices:
        pl.semaphore_signal(barrier, inc=1, device_id=device, device_id_type=pl.DeviceIdType.MESH)
    pl.semaphore_wait(barrier, len(devices))


def other_core():
    return (1 - lax.axis_index("head"), lax.axis_index("wide"), lax.axis_index("dp"))


class Swap:
    def __init__(self, src, dst, sems, slot, device):
        self.parts = (src, dst, sems, slot, device)
        self.copy().start()

    def copy(self):
        src, dst, sems, slot, device = self.parts
        return pltpu.make_async_remote_copy(
            src_ref=src, dst_ref=dst, send_sem=sems[0].at[slot], recv_sem=sems[1].at[slot],
            device_id=device() if callable(device) else device, device_id_type=pl.DeviceIdType.MESH,
        )

    def wait(self):
        self.copy().wait()


remote = Swap


def early_kernel(*refs, given_names, out_names, held_names, sizes):
    count = len(given_names)
    given = types.SimpleNamespace(**dict(zip(given_names, refs)))
    out = types.SimpleNamespace(**dict(zip(out_names, refs[count:])))
    r = types.SimpleNamespace(**dict(zip(held_names, refs[count + len(out_names):])))
    heads, experts, dh, rows, width = sizes.heads, sizes.experts, sizes.dh, sizes.rows, sizes.width
    deep, wide = lax.axis_index(DEEP), lax.axis_index(WIDE)
    near = deep % 2
    beside = (lax.axis_index("head"), wide, deep + 1 - 2 * near)
    across = (lax.axis_index("head"), wide + 1 - 2 * (wide % 2), deep)
    sems = (r.send_sem, r.recv_sem)
    loads, writes = {}, []

    def fetch(*names):
        for name in names:
            slot = given_names.index(name)
            loads[name] = pltpu.make_async_copy(getattr(given, name), getattr(r, name), r.load_sem.at[slot])
            loads[name].start()

    def ready(*names):
        for name in names:
            loads[name].wait()

    def put(name, source, *at):
        target = getattr(out, name)
        if at:
            source, target = source.at[at], target.at[at]
        writes.append(pltpu.make_async_copy(source, target, r.write_sem.at[len(writes)]))
        writes[-1].start()

    fetch(*sizes.loaded)
    meet(beside, across)
    mem_k_swap = Swap(given.mem_k, r.part_mem_k, sems, 0, beside)
    cot_swap = Swap(given.cot, out.cot_in, sems, 2, across)
    ready("x", "gain", "bias")
    normed, _ = normalize(r.x[...].astype(F32))
    hid = (normed * r.gain[...] + r.bias[...]).astype(BF16)
    r.hid[...] = hid
    ready("wk")
    for h in range(heads):
        r.key_own[h] = mm(r.wk[h * dh:(h + 1) * dh, :], r.hid[...], NT).astype(BF16)
    key_swap = Swap(r.key_own, r.part_k, sems, 3, beside)
    ready("router_v", "router_o", "rv", "ro")
    lines = []
    for router in (r.router_v, r.router_o):
        given_lines = [router[e].astype(F32) for e in range(experts)]
        lines += [given_lines[e][h:h + 1] for h in range(heads) for e in range(experts)]
    r.rt[...] = jnp.concatenate(lines, axis=0).astype(BF16)
    put("rt", r.rt)
    logits = mm(r.rt[...], r.hid[...], NT)
    sig = 1.0 / (1.0 + jnp.exp(-logits))
    masks = []
    for routes in (r.rv, r.ro):
        for h in range(heads):
            for e in range(experts):
                hit = (routes[h, 0:1, :] == e) | (routes[h, 1:2, :] == e)
                masks.append(jnp.where(hit, 1.0, 0.0))
    gate = sig * jnp.concatenate(masks, axis=0)
    he = heads * experts
    r.gate[...] = gate
    out.gate_v[...] = gate[:he]
    out.gate_o[...] = gate[he:]
    out.sig_v[...] = sig[:he]
    out.sig_o[...] = sig[he:]
    ready("wv")
    for h in range(heads):
        total = None
        for e in range(experts):
            at = h * experts + e
            each = mm(r.wv[at * dh:(at + 1) * dh, :], r.hid[...], NT)
            r.each[at * dh:(at + 1) * dh, :] = each.astype(BF16)
            term = r.gate[at:at + 1, :] * each
            total = term if total is None else total + term
        r.value_own[h] = total.astype(BF16)
    mem_v_swap = Swap(given.mem_v, r.part_mem_v, sems, 1, beside)
    value_swap = Swap(r.value_own, r.part_v, sems, 4, beside)
    put("each", r.each)
    put("key_own", r.key_own)
    put("value_own", r.value_own)
    ready("wq", "cb", "pb")
    eye = (
        lax.broadcasted_iota(jnp.int32, (dh, dh), 0) == lax.broadcasted_iota(jnp.int32, (dh, dh), 1)
    ).astype(F32)

    def column(row):
        spread = jnp.broadcast_to(row, (8, dh))
        return lax.dot_general(
            eye, spread, NT, precision=lax.Precision.HIGHEST, preferred_element_type=F32
        )[:, 0:1]

    for h in range(heads):
        queries = mm(r.wq[h * dh:(h + 1) * dh, :], r.hid[...], NT)
        r.qu[h] = (queries + column(r.cb[h:h + 1, :])).astype(BF16)
        r.qv[h] = (queries + column(r.pb[h:h + 1, :])).astype(BF16)
    put("qu", r.qu)
    put("qv", r.qv)
    ready("wr", "table")
    for h in range(heads):
        r.rel[h] = mm(r.wr[h * dh:(h + 1) * dh, :], r.table[...]).astype(BF16)
    put("rel", r.rel)
    r.hid_t[...] = r.hid[...].T.reshape(r.hid_t.shape)
    put("hid", r.hid_t)
    total_keys, size = 4 * rows, sizes.query_rows
    for h in range(heads):
        for base in range(0, rows, size):
            here = slice(base, base + size)
            positional = mm(r.qv[h, :, here], r.rel[h], TN)
            r.scores[h, here, :] = pltpu.roll(
                positional, total_keys - rows + 1 + base, 1, stride=1, stride_axis=0
            )
    odd = near == 1
    ready("mem_k", "mem_v")
    mem_k_swap.wait()
    key_swap.wait()
    put("part_k", r.part_k)
    put("part_mem_k", r.part_mem_k)
    first = jnp.where(odd, 0, rows)
    for h in range(heads):
        k_one = jnp.where(odd, r.part_k[h], r.part_mem_k[h])
        keys = (r.part_mem_k[h], r.mem_k[h], k_one, r.key_own[h])
        for base in range(0, rows, size):
            here = slice(base, base + size)
            content = jnp.concatenate([mm(r.qu[h, :, here], k, TN) for k in keys], axis=1)
            row = lax.broadcasted_iota(jnp.int32, (size, total_keys), 0) + base
            col = lax.broadcasted_iota(jnp.int32, (size, total_keys), 1)
            visible = (col <= row + (total_keys - rows)) & (col >= first)
            scores = jnp.where(visible, (content + r.scores[h, here, :]) * sizes.scale, NEG_LARGE)
            peak = jnp.max(scores, axis=1, keepdims=True)
            exponents = jnp.exp(scores - peak)
            total = jnp.sum(exponents, axis=1, keepdims=True)
            probs = (exponents * (1.0 / total)).astype(BF16)
            r.probs[h, here, :] = probs
            put("probs", r.probs, h, pl.ds(base, size))
    here_terms = [
        mm(r.mem_v[h], r.probs[h, :, rows:2 * rows], NT) + mm(r.value_own[h], r.probs[h, :, 3 * rows:], NT)
        for h in range(heads)
    ]
    mem_v_swap.wait()
    value_swap.wait()
    put("part_v", r.part_v)
    put("part_mem_v", r.part_mem_v)
    for h in range(heads):
        v_one = jnp.where(odd, r.part_v[h], r.part_mem_v[h])
        att = here_terms[h] + mm(r.part_mem_v[h], r.probs[h, :, 0:rows], NT)
        att = att + mm(v_one, r.probs[h, :, 2 * rows:3 * rows], NT)
        out.att[h] = att.astype(BF16)
    cot_swap.wait()
    for write in writes:
        write.wait()


def early_call(inputs, sizes):
    heads, experts, dh, rows, width = sizes.heads, sizes.experts, sizes.dh, sizes.rows, sizes.width
    he, hed, hd = heads * experts, heads * experts * dh, heads * dh
    tokens = (heads, dh, rows)
    blocks = sizes.wide * sizes.deep
    hid_shape = (blocks // 2, 2, width // blocks, rows)
    anywhere = dict(
        each=((hed, rows), BF16), key_own=(tokens, BF16), value_own=(tokens, BF16), qu=(tokens, BF16),
        qv=(tokens, BF16), rel=((heads, dh, 4 * rows), BF16), hid=(hid_shape, BF16), part_k=(tokens, BF16),
        part_v=(tokens, BF16), part_mem_k=(tokens, BF16), part_mem_v=(tokens, BF16),
        probs=((heads, rows, 4 * rows), BF16), rt=((2 * he, width), BF16), cot_in=((rows, width), BF16),
    )
    near = dict(
        att=(tokens, BF16), gate_v=((he, rows), F32), gate_o=((he, rows), F32), sig_v=((he, rows), F32),
        sig_o=((he, rows), F32),
    )
    outs = {**anywhere, **near}
    sem = pltpu.SemaphoreType.DMA
    sizes.loaded = [name for name in inputs if name != "cot"]
    held = {name: pltpu.VMEM(inputs[name].shape, inputs[name].dtype) for name in sizes.loaded}
    held.update({name: pltpu.VMEM(shape, dtype) for name, (shape, dtype) in anywhere.items() if name != "cot_in"})
    held.update(
        hid=pltpu.VMEM((rows, width), BF16), hid_t=pltpu.VMEM(hid_shape, BF16),
        scores=pltpu.VMEM((heads, rows, 4 * rows), F32), gate=pltpu.VMEM((2 * he, rows), F32),
        load_sem=sem((len(inputs),)), write_sem=sem((24,)), send_sem=sem((5,)), recv_sem=sem((5,)),
    )
    vmem, hbm = pl.BlockSpec(memory_space=pltpu.VMEM), pl.BlockSpec(memory_space=pl.ANY)
    results = pl.pallas_call(
        functools.partial(
            early_kernel, given_names=list(inputs), out_names=list(outs), held_names=list(held), sizes=sizes
        ),
        in_specs=[hbm] * len(inputs),
        out_specs=[hbm] * len(anywhere) + [vmem] * len(near),
        out_shape=[jax.ShapeDtypeStruct(shape, dtype) for shape, dtype in outs.values()],
        scratch_shapes=list(held.values()),
        compiler_params=pltpu.CompilerParams(collective_id=2, has_side_effects=True, vmem_limit_bytes=58 << 20),
        cost_estimate=pl.CostEstimate(flops=2 * 10**10, bytes_accessed=3 * 10**7, transcendentals=2 * 10**6),
    )(*inputs.values())
    return types.SimpleNamespace(**dict(zip(outs, results)))


def finish_kernel(*refs):
    load_sem, write_sem = refs[-2:]
    count = (len(refs) - 2) // 3
    given, outs, held = refs[:count], refs[count:2 * count], refs[2 * count:3 * count]
    loads = [pltpu.make_async_copy(given[i], held[i], load_sem.at[i]) for i in range(count)]
    writes = [pltpu.make_async_copy(held[i], outs[i], write_sem.at[i]) for i in range(count)]
    for copy in loads:
        copy.start()
    for load, write in zip(loads, writes):
        load.wait()
        write.start()
    for write in writes:
        write.wait()


def finished(*arrays):
    hbm = pl.BlockSpec(memory_space=pl.ANY)
    return pl.pallas_call(
        finish_kernel,
        in_specs=[hbm] * len(arrays),
        out_specs=[hbm] * len(arrays),
        out_shape=[jax.ShapeDtypeStruct(a.shape, a.dtype) for a in arrays],
        scratch_shapes=[pltpu.VMEM(a.shape, a.dtype) for a in arrays] + [pltpu.SemaphoreType.DMA((len(arrays),))] * 2,
        compiler_params=pltpu.CompilerParams(vmem_limit_bytes=60 << 20),
        cost_estimate=pl.CostEstimate(flops=0, bytes_accessed=10**7, transcendentals=0),
    )(*arrays)


def bit_names(wide_count, depth):
    wide_bits = [(WIDE, b) for b in range(int(math.log2(wide_count)))]
    deep_bits = [(DEEP, b) for b in range(int(math.log2(depth)))]
    return wide_bits, deep_bits


def bit_order(axes, wide_bits, deep_bits):
    half = len(wide_bits) // 2
    groups = dict(x=wide_bits[:half], y=wide_bits[half:], n=deep_bits[:1], f=deep_bits[1:])
    return [bit for axis in axes for bit in groups[axis]]


def natural(bits):
    return [b for b in sorted(bits, key=lambda b: (b[0] == WIDE, b[1]), reverse=True)]


def picks(left, fixed):
    free = [b for b in left if b not in fixed]
    found = []
    for number in range(1 << len(free)):
        index = 0
        for place, b in enumerate(left):
            if b in fixed:
                digit = fixed[b]
            else:
                digit = (number >> (len(free) - 1 - free.index(b))) & 1
            index = index + digit * (1 << (len(left) - 1 - place))
        found.append(index)
    return found


class Tree:
    def __init__(self, order, left, acc, send, got, slots, me):
        self.order, self.left, self.acc, self.send, self.got, self.slots, self.me = order, left, acc, send, got, slots, me
        self.level = 0
        self.copies = {}

    def fixed(self, own):
        bit = self.order[self.level]
        return {bit: self.me[bit] if own else 1 - self.me[bit]}

    def launch(self, sems, partner, src=None):
        got = self.got[self.level]
        src = self.send.at[pl.ds(0, got.shape[0])] if src is None else src
        bit = self.order[self.level]
        self.copies[self.level] = remote(src, got, sems, self.slots[self.level], lambda: partner(bit))

    def step(self):
        self.left = [b for b in self.left if b != self.order[self.level]]
        self.level += 1

    def arrive(self):
        self.copies[self.level - 1].wait()
        return self.got[self.level - 1]

    def advance(self, sems, partner):
        got = self.arrive() if self.level else None

        def piece(index):
            mine = self.acc[index].astype(F32)
            return mine if got is None else mine + got[index].astype(F32)

        for place, index in enumerate(picks(self.left, self.fixed(False))):
            self.send[place] = piece(index).astype(BF16)
        self.launch(sems, partner)
        for place, index in enumerate(picks(self.left, self.fixed(True))):
            self.acc[place] = piece(index).astype(self.acc.dtype)
        self.step()

    def finish(self, index=0):
        return self.acc[index].astype(F32) + self.got[self.level - 1][index].astype(F32)


def late_kernel(*refs, names, loaded, sizes, plan):
    r = types.SimpleNamespace(**dict(zip(names, refs)))
    given = types.SimpleNamespace(**dict(zip(loaded, refs)))
    heads, experts, dh, rows, width = sizes.heads, sizes.experts, sizes.dh, sizes.rows, sizes.width
    wide_count, depth, block = sizes.wide, sizes.deep, sizes.block
    hd, he, hed = heads * dh, heads * experts, heads * experts * dh
    blocks = wide_count * depth
    wide_bits, deep_bits = bit_names(wide_count, depth)
    bits = wide_bits + deep_bits
    place = {WIDE: lax.axis_index(WIDE), DEEP: lax.axis_index(DEEP)}
    head = lax.axis_index("head")
    me = {b: (place[b[0]] // (1 << b[1])) % 2 for b in bits}
    x_bit, near = wide_bits[0], deep_bits[0]

    def partner(bit):
        axis, number = bit
        other = place[axis] + (1 - 2 * me[bit]) * (1 << number)
        return (head, other, place[DEEP]) if axis == WIDE else (head, place[WIDE], other)

    across = other_core()
    sems = (r.send_sem, r.recv_sem)
    loads = {}

    def fetch(target, name, slot):
        loads[name] = pltpu.make_async_copy(getattr(given, name), target, r.load_sem.at[slot])
        loads[name].start()

    order = {name: number for number, name in enumerate(loaded)}

    def fetch_all(**targets):
        for name, target in targets.items():
            fetch(target, name, order[name])

    def ready(*wanted):
        for name in wanted:
            if loads.get(name) is not None:
                loads[name].wait()
                loads[name] = None

    def tree_of(axes, left, acc, send, got, slots):
        return Tree(bit_order(axes, wide_bits, deep_bits), natural(left), acc, send, got, slots, me)

    up_a = tree_of("yxfn", bits, None, None, r.got_up_a, plan.up_a)
    up_b = tree_of("nxyf", bits, None, None, r.got_up_b, plan.up_b)
    share = width // wide_count
    per_share = share // block

    def runs(fixed):
        return picks(natural(wide_bits), {b: v for b, v in fixed.items() if b[0] == WIDE})

    def rows_of(run):
        return pl.ds(pl.multiple_of(run * share, share), share)

    half = sizes.hidden_units // 2
    keep, leave = me[x_bit], 1 - me[x_bit]
    meet(across, *[partner(b) for b in bits])
    beside = partner(near)
    early = [
        remote(given.att, r.att_in, sems, plan.att, partner(x_bit)),
        remote(given.gate_o, r.gate_o_in, sems, plan.gate_o, partner(x_bit)),
        remote(given.gates, r.gates_in, sems, plan.gates, beside),
    ]
    fetch_all(hid=r.hid)

    def run_rows(ref, run):
        count = per_share // 2
        return ref[pl.ds(pl.multiple_of(run * count, count), count)].reshape(share, rows)

    near_rows = blocks // 2 * block
    small = r.small
    near_other = 1 - me[near]
    crossing, gm_swap, ffn_swap, two_swap, act_swap, hid_swap = [], [], [], [], [], []

    def middle(att_ref, gate_ref, sig_ref, wo, cot, mixed_ref, gain, low_ref, ffn_own):
        fetch_all(att=att_ref, gate_o=gate_ref, wo=wo, cot=cot, gain_two=gain, sig_o=sig_ref)

        def feed(x, cot_first, bias, up, down, two_ref):
            fetch_all(x=x, cot_in=cot_first, bias_two=bias, w_up=up, w_down=down)
            ready("att", "gate_o", "wo")
            for h in range(heads):
                for e in range(experts):
                    at = h * experts + e
                    r.gated[at * dh:(at + 1) * dh, :] = (
                        gate_ref[at:at + 1, :] * att_ref[h].astype(F32)
                    ).astype(BF16)
            r.two_own[...] = mm(r.gated[...], wo[...], TN).astype(BF16)
            part_swap = remote(r.two_own, r.head_in, sems, plan.part, across)
            ready("cot", "cot_in", "x", "gain_two", "bias_two")
            r.cot_t[:, 0:rows] = cot[...].T
            r.cot_t[:, rows:] = cot_first[...].T
            part_swap.wait()
            mixed = x[...].astype(F32) + (r.two_own[...].astype(F32) + r.head_in[...].astype(F32))
            mixed_ref[...] = mixed
            normed, _ = normalize(mixed)
            two = (normed * gain[...] + bias[...]).astype(BF16)
            two_ref[...] = two
            r.two_t[...] = two.T.reshape(r.two_t.shape)
            hid_swap.append(
                remote(given.hid.at[:, near_other], r.hid_in, sems, plan.hid, lambda: partner(near))
            )
            ready("w_up", "w_down")
            chunk = half // 2
            for which, target in ((leave, r.act_out), (keep, r.act)):
                for part in range(2):
                    units = pl.ds(pl.multiple_of(which * half + part * chunk, chunk), chunk)
                    inner = slice(part * chunk, (part + 1) * chunk)
                    value, slope = gelu_both(mm(two_ref[...], up[:, units]))
                    if target is r.act:
                        target[:, inner] = value.astype(BF16)
                    else:
                        target[:, :, inner] = value.astype(BF16).reshape(target.shape[0], target.shape[1], chunk)
                    r.pre[which, :, inner] = (mm(cot[...], down[units, :], NT) * slope).astype(BF16)
                if target is r.act_out:
                    act_swap.append(remote(r.act_out, r.act_in, sems, plan.act, lambda: partner(x_bit)))
            for number, run in enumerate(runs(up_a.fixed(False))):
                piece = mm(run_rows(r.two_t, run), r.pre[0]).astype(BF16)
                for k in range(per_share):
                    r.up_a_out[number * per_share + k] = piece[k * block:(k + 1) * block]
            up_a.launch(sems, partner, r.up_a_out)
            piece = mm(r.two_t[:, 1 - me[near]].reshape(near_rows, rows), r.pre[1]).astype(BF16)
            for at in range(blocks // 2):
                r.up_b_out[at] = piece[at * block:(at + 1) * block]
            up_b.launch(sems, partner, r.up_b_out)
            total = None
            for k in range(2):
                term = mm(r.pre[k], up[:, k * half:(k + 1) * half], NT)
                total = term if total is None else total + term
            r.two_own[...] = total.astype(BF16)
            two_swap.append(remote(r.two_own, r.two_in, sems, plan.two, across))
            mine = mm(r.act[...], down[pl.ds(pl.multiple_of(keep * half, half), half), :])
            theirs = mm(
                r.act_out[...].reshape(rows, half), down[pl.ds(pl.multiple_of(leave * half, half), half), :]
            )
            ffn_own[...] = (mine + theirs).astype(BF16)
            ffn_swap.append(remote(ffn_own, r.ffn_in, sems, plan.ffn, across))

        pl.run_scoped(
            feed, pltpu.VMEM((rows, width), BF16), pltpu.VMEM((rows, width), BF16), pltpu.VMEM((1, width), F32),
            pltpu.VMEM((width, 2 * half), BF16), pltpu.VMEM((2 * half, width), BF16), pltpu.VMEM((rows, width), BF16),
        )

        def out_back():
            normed, inverse = normalize(mixed_ref[...])
            two_swap[0].wait()
            grad_two = r.two_own[...].astype(F32) + r.two_in[...].astype(F32)
            small[2:3, :] = jnp.sum(grad_two * normed, axis=0, keepdims=True)
            small[3:4, :] = jnp.sum(grad_two, axis=0, keepdims=True)
            grad_mixed = cot[...].astype(F32) + norm_back(grad_two * gain[...], normed, inverse)
            r.grad_mixed[...] = grad_mixed
            low_ref[...] = grad_mixed.astype(BF16)
            low_t = low_ref[...].T.reshape(wide_count // 2, 2, share, rows)
            first, second = low_t[:, 0], low_t[:, 1]
            r.gm_out[...] = jnp.where(me[x_bit] == 1, first, second)
            r.gm[...] = jnp.where(me[x_bit] == 1, second, first)
            gm_swap.append(remote(r.gm_out, r.gm_in, sems, plan.gm, lambda: partner(x_bit)))
            ready("sig_o")
            for h in range(heads):
                att = att_ref[h].astype(F32)
                total = None
                for e in range(experts):
                    at = h * experts + e
                    back = mm(wo[at * dh:(at + 1) * dh, :], low_ref[...], NT)
                    gate = gate_ref[at:at + 1, :]
                    grad_gate = jnp.sum(att * back, axis=0, keepdims=True)
                    r.logits[he + at:he + at + 1, :] = grad_gate * gate * (1.0 - sig_ref[at:at + 1, :])
                    total = gate * back if total is None else total + gate * back
                r.ga[h] = total.astype(BF16)
            ffn_swap[0].wait()
            ffn_own[...] = (mixed_ref[...] + (ffn_own[...].astype(F32) + r.ffn_in[...].astype(F32))).astype(BF16)
            pltpu.make_async_copy(ffn_own, r.output, r.load_sem.at[len(loaded)]).start()

        total_keys = 4 * rows
        chunk_shape = pltpu.VMEM((heads, dh, rows), BF16)
        pl.run_scoped(
            functools.partial(attention, out_back), pltpu.VMEM((heads, rows, total_keys), BF16), chunk_shape,
            chunk_shape, pltpu.VMEM((heads, dh, total_keys), BF16), *([chunk_shape] * 8),
            pltpu.VMEM((sizes.query_rows, sizes.query_rows), BF16), pltpu.VMEM((dh, total_keys), F32),
        )
        pltpu.make_async_copy(ffn_own, r.output, r.load_sem.at[len(loaded)]).wait()

    def attention(out_back, probs, qu, qv, rel, key_own, part_k, mem_k, part_mem_k, value_own, part_v, mem_v, part_mem_v, flip,
                  acc):
        fetch_all(
            probs=probs, qu=qu, qv=qv, rel=rel, key_own=key_own, part_k=part_k, mem_k=mem_k, part_mem_k=part_mem_k,
            value_own=value_own, part_v=part_v, mem_v=mem_v, part_mem_v=part_mem_v, flip=flip,
        )

        out_back()
        ready("probs", "qu", "qv", "rel", "key_own", "part_k", "mem_k", "part_mem_k")
        ready("value_own", "part_v", "mem_v", "part_mem_v", "flip")
        odd = place[DEEP] % 2 == 1
        size = sizes.query_rows
        for h in range(heads):
            k_one = jnp.where(odd, part_k[h], part_mem_k[h])
            v_one = jnp.where(odd, part_v[h], part_mem_v[h])
            keys = (part_mem_k[h], mem_k[h], k_one, key_own[h])
            values = (part_mem_v[h], mem_v[h], v_one, value_own[h])
            bias_u = bias_v = None
            for base in range(0, rows, size):
                here = slice(base, base + size)
                turned = mm(flip[...], probs[h, here, :])
                ga = mm(r.ga[h, :, here], flip[...]).astype(BF16)
                queries_u = mm(qu[h, :, here], flip[...]).astype(BF16)
                queries_v = mm(qv[h, :, here], flip[...]).astype(BF16)
                gp = jnp.concatenate([mm(ga, v, TN) for v in values], axis=1)
                weighted = turned * gp
                delta = jnp.sum(weighted, axis=1, keepdims=True)
                gs = ((weighted - turned * delta) * sizes.scale).astype(BF16)
                gk = mm(queries_u, gs[:, 2 * rows:])
                gv = mm(ga, turned[:, 2 * rows:].astype(BF16))
                gqu = None
                for i, k in enumerate(keys):
                    part = mm(k, gs[:, i * rows:(i + 1) * rows], NT)
                    gqu = part if gqu is None else gqu + part
                gpos = pltpu.roll(gs, rows - size - base, 1, stride=1, stride_axis=0)
                gqv = mm(rel[h], gpos, NT)
                grel = mm(queries_v, gpos)
                r.gq[h * dh:(h + 1) * dh, here] = mm((gqu + gqv).astype(BF16), flip[...]).astype(BF16)
                ones = jnp.ones((8, size), F32)
                sum_u, sum_v = [
                    lax.dot_general(ones, g, NT, precision=lax.Precision.HIGHEST, preferred_element_type=F32)
                    for g in (gqu, gqv)
                ]
                if base == 0:
                    r.gk[h] = gk
                    r.gv[h] = gv
                    acc[...] = grel
                    bias_u, bias_v = sum_u, sum_v
                else:
                    r.gk[h] += gk
                    r.gv[h] += gv
                    acc[...] += grel
                    bias_u, bias_v = bias_u + sum_u, bias_v + sum_v
            r.grel[h * dh:(h + 1) * dh, :] = acc[...].astype(BF16)
            r.small[4 + h:5 + h, 0:dh] = bias_u[0:1]
            r.small[4 + heads + h:5 + heads + h, 0:dh] = bias_v[0:1]
        r.cross_out[0] = r.gk[:, :, :rows].astype(BF16)
        r.cross_out[1] = r.gv[:, :, :rows].astype(BF16)
        crossing.append(remote(r.cross_out, r.cross_in, sems, plan.cross, lambda: partner(near)))

    hd_up = sizes.hd_up
    small[4:8, :] = jnp.zeros((4, width), F32)
    tokens_of = pltpu.VMEM((heads, dh, rows), BF16)
    pl.run_scoped(
        middle, tokens_of, pltpu.VMEM((he, rows), F32), pltpu.VMEM((he, rows), F32), pltpu.VMEM((hed, width), BF16),
        pltpu.VMEM((rows, width), BF16), pltpu.VMEM((rows, width), F32), pltpu.VMEM((1, width), F32),
        pltpu.VMEM((rows, width), BF16), pltpu.VMEM((rows, width), BF16),
    )

    def rest(*held):
        b = types.SimpleNamespace(**dict(zip(sizes.late_names, held)))
        fetch_all(each=b.each, sigs=b.sigs, gates=b.gates, wv=b.wv, wq=b.wq, wk=b.wk, rt=b.rt, x=b.x, gain=b.gain)
        up_a.acc, up_a.send, up_b.acc, up_b.send = r.act_out, b.send_up_a, b.acc_up_b, b.send_up_b
        far = [v for v in bits if v != near]
        out = tree_of("ynf", [v for v in bits if v != x_bit], b.acc_out, b.send_out, r.got_out, plan.out)
        value = tree_of("xyf", far, b.acc_value, b.send_value, r.got_value, plan.value)
        query = tree_of("xynf", bits, b.acc_query, b.send_query, r.got_query, plan.query)
        down = tree_of("yfn", bits, r.up_b_out, r.up_a_out, r.got_down, plan.down)
        half_count = len(wide_bits) // 2
        for tree in (out, down):
            tree.order = tree.order[:half_count] + wide_bits[1:half_count] + tree.order[half_count:]
        state = []

        def down_part(own):
            for number, run in enumerate(runs(down.fixed(own))):
                at_rows = rows_of(run)
                part = mm(r.cot_t[at_rows, 0:rows], r.act[...]) + mm(
                    r.cot_t[at_rows, rows:], r.act_in[...].reshape(rows, half)
                )
                for k in range(per_share):
                    at = number * per_share + k
                    piece = part[k * block:(k + 1) * block]
                    if own:
                        down.acc[at] = piece.astype(BF16)
                    else:
                        down.send[at] = piece.astype(BF16)
            if own:
                down.step()
            else:
                down.launch(sems, partner)

        def up_a_keep():
            for number, run in enumerate(runs(up_a.fixed(True))):
                part = mm(run_rows(r.two_t, run), r.pre[0])
                for k in range(per_share):
                    up_a.acc[number * per_share + k] = part[k * block:(k + 1) * block].astype(BF16)
            up_a.step()

        def up_b_keep():
            part = mm(r.two_t[:, me[near]].reshape(near_rows, rows), r.pre[1])
            for at in range(blocks // 2):
                up_b.acc[at] = part[at * block:(at + 1) * block].astype(BF16)
            up_b.step()

        def out_part():
            mine = mm(r.gm[...].reshape(near_rows, rows), r.gated[...], NT)
            for at in range(blocks // 2):
                out.acc[at] = mine[at * block:(at + 1) * block].astype(BF16)
            early[0].wait()
            early[1].wait()
            for h in range(heads):
                for e in range(experts):
                    at = h * experts + e
                    r.gated[at * dh:(at + 1) * dh, :] = (
                        r.gate_o_in[at:at + 1, :] * r.att_in[h].astype(F32)
                    ).astype(BF16)
            gm_swap[0].wait()
            theirs = mm(r.gm_in[...].reshape(near_rows, rows), r.gated[...], NT)
            for at in range(blocks // 2):
                out.acc[at] = (out.acc[at].astype(F32) + theirs[at * block:(at + 1) * block]).astype(BF16)
            out.advance(sems, partner)

        def own_part():
            ready("each", "sigs", "gates")
            crossing[0].wait()
            even = jnp.where(place[DEEP] % 2 == 0, 1.0, 0.0)
            for h in range(heads):
                gk = r.gk[h, :, rows:] + even * r.cross_in[0, h].astype(F32)
                gv = r.gv[h, :, rows:] + even * r.cross_in[1, h].astype(F32)
                b.own_out[h * dh:(h + 1) * dh, :] = gv.astype(BF16)
                b.own_out[hd + h * dh:hd + (h + 1) * dh, :] = gk.astype(BF16)
                for e in range(experts):
                    at = h * experts + e
                    gate = b.gates[at:at + 1, :]
                    grad_gate = jnp.sum(gv * b.each[at * dh:(at + 1) * dh, :].astype(F32), axis=0, keepdims=True)
                    r.logits[at:at + 1, :] = grad_gate * gate * (1.0 - b.sigs[at:at + 1, :])
                    b.grads[at * dh:(at + 1) * dh, :] = (gate * gv).astype(BF16)
            tail = b.own_out.shape[0] - 2 * hd
            logits = jnp.concatenate([r.logits[0:2 * he, :], jnp.zeros((tail - 2 * he, rows), F32)], axis=0)
            b.own_out[2 * hd:, :] = logits.astype(BF16)
            state_own.append(remote(b.own_out, r.own_in, sems, plan.own, partner(near)))
            b.grads[hed:, :] = b.own_out[hd:, :]

        def hidden_part():
            ready("wv", "wq", "wk", "rt")
            grad_hidden = mm(b.grads[0:hed, :], b.wv[...], TN)
            grad_hidden += mm(r.gq[...], b.wq[...], TN)
            grad_hidden += mm(b.grads[hed:hed + hd, :], b.wk[...], TN)
            grad_hidden += mm(b.grads[hed + hd:hed + hd + 2 * he, :], b.rt[...], TN)
            r.two_own[...] = grad_hidden.astype(BF16)
            state_head.append(remote(r.two_own, r.head_in, sems, plan.head, across))

        def norm_part():
            ready("x", "gain")
            state_head[0].wait()
            grad_hidden = r.two_own[...].astype(F32) + r.head_in[...].astype(F32)
            normed, inverse = normalize(b.x[...].astype(F32))
            small[0:1, :] = jnp.sum(grad_hidden * normed, axis=0, keepdims=True)
            small[1:2, :] = jnp.sum(grad_hidden, axis=0, keepdims=True)
            state.append(remote(small, r.small_in.at[0], sems, plan.small[0], partner(bits[0])))
            r.grad_mixed[...] += norm_back(grad_hidden * b.gain[...], normed, inverse)
            input_copy = pltpu.make_async_copy(r.grad_mixed, r.grad_input, r.load_sem.at[len(loaded) + 1])
            input_copy.start()
            state_input.append(input_copy)

        def small_step():
            at = len(state) - 1
            if at == len(bits):
                return
            state[at].wait()
            small[...] = small[...] + r.small_in[at]
            state.append(
                None if at + 1 == len(bits)
                else remote(small, r.small_in.at[at + 1], sems, plan.small[at + 1], partner(bits[at + 1]))
            )

        def value_own():
            ready("hid")
            mine = mm(r.hid[:, me[near]].reshape(near_rows, rows), b.grads[...], NT)
            for at in range(blocks // 2):
                value.acc[at] = mine[at * block:(at + 1) * block]

        def value_part():
            early[2].wait()
            hid_swap[0].wait()
            state_own[0].wait()
            for at in range(he):
                h = at // experts
                b.grads[at * dh:(at + 1) * dh, :] = (
                    r.gates_in[at:at + 1, :] * r.own_in[h * dh:(h + 1) * dh, :].astype(F32)
                ).astype(BF16)
            b.grads[hed:, :] = r.own_in[hd:, :]
            theirs = mm(r.hid_in[...].reshape(near_rows, rows), b.grads[...], NT)
            for at in range(blocks // 2):
                value.acc[at] += theirs[at * block:(at + 1) * block]
            value.advance(sems, partner)

        def table_copy(number, run):
            return pltpu.make_async_copy(
                given.table.at[rows_of(run)], b.table.at[pl.ds(number * share, share)], r.table_sem.at[number]
            )

        for number, run in enumerate(runs(query.fixed(False))):
            table_copy(number, run).start()

        def query_part(own):
            if not own and hd_up > hd:
                for at in range(blocks // 2):
                    query.send[at, :, hd:hd_up] = jnp.zeros((block, hd_up - hd), BF16)
                    query.acc[at, :, hd:hd_up] = jnp.zeros((block, hd_up - hd), BF16)
            ready("hid")
            for number, run in enumerate(runs(query.fixed(own))):
                table_copy(number, run).wait()
                part = mm(run_rows(r.hid, run), r.gq[...], NT)
                part_rel = mm(b.table[number * share:(number + 1) * share, :], r.grel[...], NT)
                for k in range(per_share):
                    at = number * per_share + k
                    piece, piece_rel = part[k * block:(k + 1) * block], part_rel[k * block:(k + 1) * block]
                    if own:
                        query.acc[at, :, 0:hd] = piece.astype(BF16)
                        query.acc[at, :, hd_up:] = piece_rel.astype(BF16)
                    else:
                        query.send[at, :, 0:hd] = piece.astype(BF16)
                        query.send[at, :, hd_up:] = piece_rel.astype(BF16)
            if own:
                query.step()
            else:
                query.launch(sems, partner)
                for number, run in enumerate(runs(query.fixed(True))):
                    table_copy(number, run).start()

        state_own, state_head, state_input = [], [], []
        def half_part():
            down.arrive()
            r.half_out[...] = down.finish(leave).astype(BF16)
            state_own.append(remote(r.half_out, r.half_in, sems, plan.half, partner(x_bit)))
            r.g_down[:, pl.ds(pl.multiple_of(keep * half, half), half)] = down.finish(keep)

        def next_level(tree):
            if tree.level < len(tree.order):
                tree.advance(sems, partner)

        act_swap[0].wait()
        up_a_keep()
        next_level(up_a)
        down_part(False)
        own_part()
        up_b_keep()
        next_level(up_b)
        next_level(up_a)
        down_part(True)
        query_part(False)
        value_own()
        query_part(True)
        out_part()
        next_level(down)
        hidden_part()
        next_level(up_a)
        value_part()
        next_level(up_b)
        next_level(out)
        norm_part()
        next_level(query)
        next_level(query)
        next_level(up_b)
        next_level(down)
        next_level(value)
        small_step()
        next_level(out)
        next_level(query)
        small_step()
        next_level(value)
        half_part()
        small_step()
        while len(state) <= len(bits):
            small_step()
        r.small_out[...] = small[...]
        r.bias_u[...] = small[4:4 + heads, 0:dh]
        r.bias_v[...] = small[4 + heads:4 + 2 * heads, 0:dh]
        for number, tree in enumerate((up_a, up_b)):
            tree.arrive()
            r.g_up[:, number * half:(number + 1) * half] = tree.finish()
        out.arrive()
        total = out.finish()
        for at in range(he):
            r.g_out[at] = total[:, at * dh:(at + 1) * dh]
        value.arrive()
        total = value.finish()
        for at in range(he):
            r.g_value[at] = total[:, at * dh:(at + 1) * dh]
        for h in range(heads):
            r.g_key[:, h, :] = total[:, hed + h * dh:hed + (h + 1) * dh]
        eye = (
            lax.broadcasted_iota(jnp.int32, (block, block), 0) == lax.broadcasted_iota(jnp.int32, (block, block), 1)
        ).astype(F32)
        turned = lax.dot_general(
            total[:, hed + hd:hed + hd + 2 * he], eye, TN, precision=lax.Precision.HIGHEST, preferred_element_type=F32
        )
        for h in range(heads):
            for e in range(experts):
                at = h * experts + e
                r.g_router_v[e, h:h + 1, :] = turned[at:at + 1]
                r.g_router_o[e, h:h + 1, :] = turned[he + at:he + at + 1]
        query.arrive()
        total = query.finish()
        for h in range(heads):
            r.g_query[:, h, :] = total[:, h * dh:(h + 1) * dh]
            r.g_rel[:, h, :] = total[:, hd_up + h * dh:hd_up + (h + 1) * dh]
        state_own[1].wait()
        r.g_down[:, pl.ds(pl.multiple_of(leave * half, half), half)] = r.half_in[...].astype(F32)
        state_input[0].wait()

    pl.run_scoped(rest, *sizes.late_scratch)


def late_call(inputs, sizes):
    wide_bits, deep_bits = bit_names(sizes.wide, sizes.deep)
    bits = len(wide_bits) + len(deep_bits)
    blocks = sizes.wide * sizes.deep
    block, rows, width, heads, dh = sizes.block, sizes.rows, sizes.width, sizes.heads, sizes.dh
    he, hd = heads * sizes.experts, heads * dh
    hed, half = he * dh, sizes.hidden_units // 2
    tail = 32
    sizes.hd_up = -(-hd // 128) * 128
    sizes.value_n = hed + hd + tail
    query_n = sizes.hd_up + hd
    count = 15 + 7 * bits
    slots = iter(range(count))

    def levels():
        return [next(slots) for _ in range(bits)]

    plan = types.SimpleNamespace(
        two=next(slots), ffn=next(slots), act=next(slots), gm=next(slots), cross=next(slots), part=next(slots),
        att=next(slots), gate_o=next(slots), gates=next(slots), hid=next(slots),
        own=next(slots), head=next(slots), half=next(slots), small=levels(), up_a=levels(), up_b=levels(),
        out=levels(), query=levels(), down=levels(), value=levels(),
    )

    def got(n, start, stop):
        return [pltpu.VMEM((blocks >> (level + 1), block, n), BF16) for level in range(start, stop)]

    def taken(name):
        return pltpu.VMEM(inputs[name].shape, inputs[name].dtype)

    sem = pltpu.SemaphoreType.DMA
    token_rows = pltpu.VMEM((rows, width), BF16)
    near_half = pltpu.VMEM((blocks // 2, block, rows), BF16)
    x_half = pltpu.VMEM((sizes.wide // 2, width // sizes.wide, rows), BF16)
    first_half = pltpu.VMEM((blocks // 2, block, half), BF16)
    scratch = dict(
        act=pltpu.VMEM((rows, half), BF16), hid=taken("hid"), two_t=taken("hid"),
        pre=pltpu.VMEM((2, rows, half), BF16), cot_t=pltpu.VMEM((width, 2 * rows), BF16),
        gated=pltpu.VMEM((hed, rows), BF16), att_in=taken("att"), gate_o_in=taken("gate_o"), gates_in=taken("gates"),
        two_own=token_rows, two_in=token_rows, ffn_in=token_rows, head_in=token_rows,
        act_in=first_half, act_out=first_half, up_a_out=first_half, up_b_out=first_half,
        hid_in=near_half, gm=x_half, gm_in=x_half, gm_out=x_half,
        grad_mixed=pltpu.VMEM((rows, width), F32), table_sem=sem((sizes.wide // 2,)),
        small=pltpu.VMEM((8, width), F32), small_in=pltpu.VMEM((bits, 8, width), F32),
        logits=pltpu.VMEM((2 * he, rows), F32), ga=pltpu.VMEM((heads, dh, rows), BF16),
        gq=pltpu.VMEM((hd, rows), BF16), gk=pltpu.VMEM((heads, dh, 2 * rows), F32),
        gv=pltpu.VMEM((heads, dh, 2 * rows), F32), grel=pltpu.VMEM((hd, 4 * rows), BF16),
        cross_out=pltpu.VMEM((2, heads, dh, rows), BF16), cross_in=pltpu.VMEM((2, heads, dh, rows), BF16),
        own_in=pltpu.VMEM((2 * hd + tail, rows), BF16), half_in=pltpu.VMEM((block, half), BF16),
        half_out=pltpu.VMEM((block, half), BF16),
        got_up_a=got(half, 0, bits), got_up_b=got(half, 0, bits), got_out=got(hed, 1, bits),
        got_query=got(query_n, 0, bits), got_down=got(half, 0, bits - 1), got_value=got(sizes.value_n, 1, bits),
        load_sem=sem((len(inputs) + 3,)), send_sem=sem((count,)), recv_sem=sem((count,)),
    )
    late = dict(
        send_out=pltpu.VMEM((blocks >> 2, block, hed), BF16), acc_out=pltpu.VMEM((blocks >> 1, block, hed), BF16),
        table=pltpu.VMEM((width // 2, 4 * rows), BF16), each=taken("each"), sigs=taken("sigs"), gates=taken("gates"), wv=taken("wv"),
        wq=taken("wq"), wk=taken("wk"), rt=taken("rt"), x=taken("x"), gain=taken("gain"),
        own_out=pltpu.VMEM((2 * hd + tail, rows), BF16), grads=pltpu.VMEM((sizes.value_n, rows), BF16),
        send_up_a=pltpu.VMEM((blocks >> 2, block, half), BF16), send_up_b=pltpu.VMEM((blocks >> 2, block, half), BF16),
        acc_up_b=pltpu.VMEM((blocks >> 1, block, half), BF16),
        send_query=pltpu.VMEM((blocks >> 1, block, query_n), BF16),
        acc_query=pltpu.VMEM((blocks >> 1, block, query_n), BF16),
        send_value=pltpu.VMEM((blocks >> 2, block, sizes.value_n), BF16),
        acc_value=pltpu.VMEM((blocks >> 1, block, sizes.value_n), F32),
    )
    sizes.late_names, sizes.late_scratch = list(late), list(late.values())
    outs = dict(
        g_down=((block, 2 * half), F32), g_up=((block, 2 * half), F32), g_out=((he, block, dh), F32),
        g_value=((he, block, dh), F32), g_query=((block, heads, dh), F32), g_key=((block, heads, dh), F32),
        g_rel=((block, heads, dh), F32), g_router_v=((sizes.experts, heads, block), F32),
        g_router_o=((sizes.experts, heads, block), F32), bias_u=((heads, dh), F32), bias_v=((heads, dh), F32), small_out=((8, width), F32),
        grad_input=((rows, width), F32), output=((rows, width), BF16),
    )
    flat, tree = jax.tree.flatten(list(scratch.values()))

    def kernel(*refs):
        held = jax.tree.unflatten(tree, refs[len(inputs) + len(outs):])
        late_kernel(
            *refs[:len(inputs) + len(outs)], *held, names=[None] * 0 + [n + "_" for n in inputs] + list(outs) + list(scratch),
            loaded=list(inputs), sizes=sizes, plan=plan,
        )

    vmem, anywhere = pl.BlockSpec(memory_space=pltpu.VMEM), pl.BlockSpec(memory_space=pl.ANY)
    results = pl.pallas_call(
        kernel,
        in_specs=[anywhere] * len(inputs),
        out_specs=[vmem] * (len(outs) - 2) + [anywhere] * 2,
        out_shape=[jax.ShapeDtypeStruct(shape, dtype) for shape, dtype in outs.values()],
        scratch_shapes=flat,
        compiler_params=pltpu.CompilerParams(collective_id=0, has_side_effects=True, vmem_limit_bytes=60 << 20),
        cost_estimate=pl.CostEstimate(flops=4 * 10**10, bytes_accessed=10**8, transcendentals=0),
    )(*inputs.values())
    return types.SimpleNamespace(**dict(zip(outs, results)))


def body(
    layer_input, mem_keys, mem_values, route_value, route_output, ln1_gain, ln1_bias, w_query, w_key, w_rel,
    content_bias, position_bias, w_value, w_out, router_value, router_output, ln2_gain, ln2_bias, w_up, w_down,
    cotangent,
):
    rows, width = layer_input.shape
    heads, dh = content_bias.shape
    experts = w_value.shape[1]
    odd = (lax.axis_index("dp") % 2).astype(jnp.int32)
    scale = 1.0 / math.sqrt(dh)
    total_keys = 4 * rows
    block = rows // 2
    hd = heads * dh
    hed = heads * experts * dh

    wq = jnp.transpose(w_query, (1, 2, 0)).reshape(hd, width)
    wk = jnp.transpose(w_key, (1, 2, 0)).reshape(hd, width)
    wr = jnp.transpose(w_rel, (1, 2, 0)).reshape(hd, width)
    wv = jnp.transpose(w_value, (0, 1, 3, 2)).reshape(hed, width)
    wo = w_out.reshape(hed, width)
    mem_k = jnp.transpose(mem_keys, (1, 2, 0))
    mem_v = jnp.transpose(mem_values, (1, 2, 0))
    rv = jnp.transpose(route_value, (0, 2, 1))
    ro = jnp.transpose(route_output, (0, 2, 1))
    table = jnp.asarray(position_table(total_keys, width))
    first = early_call(dict(
        x=layer_input, gain=ln1_gain.reshape(1, width), bias=ln1_bias.reshape(1, width), wk=wk, rv=rv, ro=ro,
        router_v=jnp.transpose(router_value, (2, 1, 0)), router_o=jnp.transpose(router_output, (2, 1, 0)),
        wv=wv, wq=wq, cb=content_bias, pb=position_bias, wr=wr, table=table, mem_k=mem_k, mem_v=mem_v, cot=cotangent,
    ), types.SimpleNamespace(
        heads=heads, experts=experts, dh=dh, rows=rows, width=width, wide=lax.axis_size(WIDE),
        deep=lax.axis_size(DEEP), scale=scale, query_rows=block,
    ))
    att, gate_v, gate_o, sig_v, sig_o, hid = first.att, first.gate_v, first.gate_o, first.sig_v, first.sig_o, first.hid
    wide_count, depth = lax.axis_size(WIDE), lax.axis_size(DEEP)
    blocks = wide_count * depth
    block_rows, he = width // blocks, heads * experts
    hidden_units = w_up.shape[1]
    wide_bits, deep_bits = bit_names(wide_count, depth)
    gain_two, bias_two = ln2_gain.reshape(1, width), ln2_bias.reshape(1, width)
    sem = pltpu.SemaphoreType.DMA

    def shapes(*pairs):
        return [jax.ShapeDtypeStruct(shape, dtype) for shape, dtype in pairs]

    flip = jnp.asarray(np.eye(block, dtype=np.float32)[::-1].astype(BF16))
    inputs = dict(
        hid=hid, gates=gate_v, cot=cotangent, cot_in=first.cot_in, gain_two=gain_two, bias_two=bias_two, w_up=w_up,
        w_down=w_down, att=att, gate_o=gate_o, sig_o=sig_o, wo=wo,
        flip=flip, probs=first.probs, qu=first.qu, qv=first.qv, rel=first.rel,
        key_own=first.key_own, part_k=first.part_k, mem_k=mem_k, part_mem_k=first.part_mem_k,
        value_own=first.value_own, part_v=first.part_v, mem_v=mem_v, part_mem_v=first.part_mem_v,
        table=table, sigs=sig_v, each=first.each, wv=wv, wq=wq, wk=wk, rt=first.rt,
        x=layer_input, gain=ln1_gain.reshape(1, width),
    )
    done = late_call(inputs, types.SimpleNamespace(
        heads=heads, experts=experts, dh=dh, rows=rows, width=width, wide=wide_count, deep=depth, block=block_rows,
        hidden_units=hidden_units, scale=scale, query_rows=block,
    ))
    start = (lax.axis_index(WIDE) * depth + lax.axis_index(DEEP)) * block_rows
    ln = lax.dynamic_slice_in_dim(done.small_out, start, block_rows, axis=1)
    (output, grad_input, g_query, g_key, g_rel, g_value, g_out, g_up, g_down, g_router_v, g_router_o, bias_u,
     bias_v) = finished(
        done.output, done.grad_input, done.g_query, done.g_key, done.g_rel, done.g_value, done.g_out, done.g_up,
        done.g_down, done.g_router_v, done.g_router_o, done.bias_u, done.bias_v,
    )

    def by_expert(values):
        return values.reshape(heads, experts, block_rows, dh)

    return (
        output, grad_input, ln[0], ln[1], g_query, g_key, g_rel, bias_u, bias_v,
        by_expert(g_value), jnp.transpose(by_expert(g_out), (0, 1, 3, 2)), jnp.transpose(g_router_v, (2, 1, 0)),
        jnp.transpose(g_router_o, (2, 1, 0)),
        ln[2], ln[3], g_up, jnp.transpose(g_down),
    )


def solution(mesh):
    tokens = ("wide", "dp")
    return jax.shard_map(
        body,
        mesh=mesh,
        in_specs=(
            P(tokens, None), P(tokens, "head", None), P(tokens, "head", None), P("head", tokens, None),
            P("head", tokens, None), P(), P(), P(None, "head", None), P(None, "head", None), P(None, "head", None),
            P("head", None), P("head", None), P("head", None, None, None), P("head", None, None, None),
            P(None, "head", None), P(None, "head", None), P(), P(), P(None, "head"), P("head", None), P(tokens, None),
        ),
        out_specs=(
            P(tokens, None), P(tokens, None), P(tokens), P(tokens), P(tokens, "head", None), P(tokens, "head", None),
            P(tokens, "head", None), P("head", None), P("head", None), P("head", None, tokens, None),
            P("head", None, None, tokens), P(tokens, "head", None), P(tokens, "head", None), P(tokens), P(tokens),
            P(tokens, "head"), P("head", tokens),
        ),
        check_vma=False,
    )
```
